256 devices in a mesh: fsdp: 32 (over y_hi, z, core), vocab: 8 (over y_lo, x).
Axes of the slice: x: 4, y: 4 (y_hi: 2, y_lo: 2; y = y_hi * 2 + y_lo), z: 8, core: 2. Of those that a mesh axis runs over, the one named last changes fastest.
Arguments:
- resid: bfloat16 [3072, 2304], P('fsdp'), may hold values from -6 to 6
- queries: bfloat16 [3072, 2048], P('fsdp', 'vocab'), may hold values from -8 to 8
- new_keys: bfloat16 [3072, 2048], P('fsdp', 'vocab'), may hold values from -6 to 6
- new_values: bfloat16 [3072, 2048], P('fsdp', 'vocab'), may hold values from -12 to 12
- pool_keys: bfloat16 [2048, 128, 2048], P('fsdp', None, 'vocab'), may hold values from -6 to 6
- pool_values: bfloat16 [2048, 128, 2048], P('fsdp', None, 'vocab'), may hold values from -12 to 12
- page_table: int32 [64, 32], P('fsdp'), may hold values from 0 to 95, as said below
- serve_pages: int32 [32, 32, 1], P('fsdp'), may hold values from 32 to 63, as said below
- cache_lengths: int32 [64], P('fsdp'), may hold values from 512 to 4096
- parents: int32 [64, 48], P('fsdp'), may hold values from 0 to 46, as said below
- out_weight: bfloat16 [2048, 2304], P('vocab'), may hold values from -0.125 to 0.125
- norm_gain: float32 [2304], replicated, may hold values from 0.5 to 1.5
- router: bfloat16 [2304, 8], replicated, may hold values from -0.25 to 0.25
- routes: int32 [3072, 2], P('fsdp'), may hold values from 0 to 7, all different within a row; in each aligned block of 96 rows (0 to 95, 96 to 191, ...) at most 36 rows name the same one
- gate_weight: bfloat16 [8, 2304, 5760], P('vocab', None, 'fsdp'), may hold values from -0.125 to 0.125
- up_weight: bfloat16 [8, 2304, 5760], P('vocab', None, 'fsdp'), may hold values from -0.125 to 0.125
- down_weight: bfloat16 [8, 5760, 2304], P('vocab', 'fsdp'), may hold values from -0.078125 to 0.078125
Outputs:
- hidden_out: bfloat16 [3072, 2304], P('fsdp', 'vocab')
The draws below stay inside these ranges and needn't reach their ends.
Inputs may be any that keep to these rules, and one draw needn't show every extreme that they name: `page_table`: within the rows of one device every entry appears once; entries below 32 name pages of the device's own pool, entries from 64 on name pages held for it by some device (possibly itself), each of those once; entry 64 + h names the one page that device h holds for it. `serve_pages`: each holding device lists each of its pages from 32 on exactly once. `parents`: node 0 is the root and its own parent; every other node's parent comes before it. `routes`: each row names two different experts; within the rows of one device no expert is named more than 36 times.
All inputs are finite; a program needn't handle non-finite values.
Results may differ from the reference program's by a relative error of at most 0.01.
Values may be sent and summed in bfloat16 or wider, within the bound.
A program may use at most 128 MiB of HBM per device.

```python
import math
import jax
import jax.numpy as jnp
import numpy as np
from jax import lax

D = 2304
FF = 5760
EXPERTS = 8
TOPK = 2
HEAD_DIM = 64
HEADS = 32
TREE = 48
PAGE = 128
PAGES_REQ = 32
REQ_DEV = 2
FEATS = 2048
TOK_DEV = 96
REQUESTS = 64
TOKENS = 3072
CAPACITY = 36
LOCAL_PAGES = 32
POOL_PAGES = 64
SLOTS = 1
MAXLEN = 4096
N_FSDP = 32


def attention_pair(key):
    query_seed = jax.random.fold_in(key, 101)
    keys_seed = jax.random.fold_in(key, 102)
    drawn_queries = jnp.clip(2.0 * jax.random.normal(query_seed, (TOKENS, FEATS), jnp.float32), -8.0, 8.0)
    drawn_keys = jnp.clip(jax.random.normal(keys_seed, (TOKENS, FEATS), jnp.float32), -6.0, 6.0)
    return (drawn_queries, drawn_keys)


def draw_queries(key, part):
    return attention_pair(key)[0].astype(jnp.bfloat16)


def draw_new_keys(key, part):
    return attention_pair(key)[1].astype(jnp.bfloat16)


def draw_page_table(key, part):
    devices = REQUESTS // REQ_DEV

    def one_device(device_index):
        shuffled = jax.random.permutation(jax.random.fold_in(key, device_index), 2 * LOCAL_PAGES).astype(jnp.int32)
        return jnp.where(shuffled < LOCAL_PAGES, shuffled, shuffled + LOCAL_PAGES)
    tables = jax.vmap(one_device)(jnp.arange(devices, dtype=jnp.int32))
    return tables.reshape(REQUESTS, PAGES_REQ).astype(jnp.int32)


def draw_serve_pages(key, part):
    devices = REQUESTS // REQ_DEV

    def one_holder(device_index):
        shuffled = jax.random.permutation(jax.random.fold_in(key, device_index), LOCAL_PAGES).astype(jnp.int32)
        return (shuffled + LOCAL_PAGES).reshape(devices, SLOTS)
    return jax.vmap(one_holder)(jnp.arange(devices, dtype=jnp.int32)).astype(jnp.int32)


def draw_cache_lengths(key, part):
    drawn = jax.random.randint(key, (REQUESTS,), MAXLEN // 8, MAXLEN + 1, dtype=jnp.int32)
    drawn = drawn.at[0].set(MAXLEN)
    drawn = drawn.at[1].set(MAXLEN // 8)
    return drawn.astype(jnp.int32)


def draw_parents(key, part):
    bounds = jnp.maximum(jnp.arange(TREE, dtype=jnp.int32), 1)
    drawn = jax.random.randint(key, (REQUESTS, TREE), 0, bounds[None, :], dtype=jnp.int32)
    drawn = drawn.at[:, TREE - 1].set(TREE - 2)
    return drawn.astype(jnp.int32)


def shard_levels(own_key, extent, split, smallest, largest):
    def one(axis_at, shards_of):
        steps = jax.random.uniform(jax.random.fold_in(jax.random.fold_in(own_key, 6), axis_at), (shards_of,), jnp.float32, smallest / len(split), largest / len(split))
        return jnp.repeat(jnp.exp(steps), extent[axis_at] // shards_of).reshape((-1,) + (1,) * (len(extent) - axis_at - 1))

    factor_of = one(*split[0])
    for cut in split[1:]:
        factor_of = factor_of * one(*cut)
    return factor_of


def assign_block(rng, own, number, rows, number_of, top, bound, skew):
    ranking = jax.random.permutation(rng, number_of)
    crowded, common = shares(number_of, rows * top, bound, skew, True), shares(number_of, rows * top, bound, skew, False)
    places = jnp.arange(number_of)

    def named(tallies, turn):
        used = int((tallies > 0).sum())
        fixed = max(1, used // 4)
        passed = fixed + (places - fixed + turn * (used - fixed)) % max(1, number_of - fixed)
        return jnp.zeros((number_of,), jnp.int32).at[ranking[jnp.where(places < fixed, places, passed)]].set(jnp.asarray(tallies, jnp.int32))

    tallies = jnp.where(number % 4 == 0, named(crowded, number // 4), named(common, number - number // 4 - 1))
    mixed = jax.random.permutation(jax.random.fold_in(own, 3), number_of)
    giver, sink = mixed[0:number_of // 2 * 2:2], mixed[1:number_of // 2 * 2:2]
    room = jnp.minimum(tallies[giver] - 1, bound - tallies[sink]) // 2
    room = jnp.where((giver == ranking[0]) | (sink == ranking[0]) | (tallies[sink] == 0), 0, jnp.maximum(room, 0))
    passed = jax.random.randint(jax.random.fold_in(own, 4), (number_of // 2,), 0, 1 << 20) % (room + 1)
    tallies = tallies.at[giver].add(-passed).at[sink].add(passed)
    items = jnp.searchsorted(jnp.cumsum(tallies), jnp.arange(rows * top), side="right").astype(jnp.int32)
    table = items.reshape(top, rows).T
    table = table[jax.random.permutation(jax.random.fold_in(own, 1), rows)]
    turn = jax.random.randint(jax.random.fold_in(own, 2), (rows, 1), 0, top)
    return jnp.take_along_axis(table, (jnp.arange(top)[None, :] + turn) % top, axis=1)


def shares(amount, total, most, skew, full):
    loads = [(1 << 20) // math.isqrt(rank ** skew) + 1 for rank in range(1, amount + 1)]
    largest = most if full else min(most, max(-(-total // amount), total * loads[0] // sum(loads)))
    least = 1 if total - largest >= amount - 1 else 0
    counts, surplus = [largest] + [least] * (amount - 1), total - largest - least * (amount - 1)
    while surplus > 0:
        candidates = [i for i in range(1, amount) if counts[i] < largest] or [i for i in range(1, amount) if counts[i] < most]
        mass, left = sum([loads[i] for i in candidates]), surplus
        for i in candidates:
            more = min(most - counts[i], max(1, left * loads[i] // mass), surplus)
            counts[i] = counts[i] + more
            surplus = surplus - more
    return np.array(counts)


def centred(rng, extent, spread, reach, pieces=(), kind=jnp.bfloat16):
    values = spread * jax.random.normal(rng, extent, jnp.float32)
    if pieces:
        values = values * shard_levels(rng, extent, pieces, -0.22, 0.18)
    return jnp.clip(values, -reach, reach).astype(kind)


def setup_inputs(seed: int = 0) -> dict:
    streams_of = jax.random.split(jax.random.key(seed), 18)
    resid = centred(streams_of[0], (TOKENS, D), 1.0, 6.0, ((0, 32),))
    queries = draw_queries(jax.random.fold_in(streams_of[17], 71), 0)
    new_keys = draw_new_keys(jax.random.fold_in(streams_of[17], 71), 0)
    new_values = centred(streams_of[3], (TOKENS, FEATS), 2.0, 12.0, ((0, 32), (1, 8)))
    pool_keys = centred(streams_of[4], (N_FSDP * POOL_PAGES, PAGE, FEATS), 1.0, 6.0, ((0, 32), (2, 8)))
    pool_values = centred(streams_of[5], (N_FSDP * POOL_PAGES, PAGE, FEATS), 2.0, 12.0, ((0, 32), (2, 8)))
    page_table = draw_page_table(jax.random.fold_in(streams_of[17], 71), 0)
    serve_pages = draw_serve_pages(jax.random.fold_in(streams_of[17], 71), 0)
    cache_lengths = draw_cache_lengths(jax.random.fold_in(streams_of[17], 71), 0)
    parents = draw_parents(jax.random.fold_in(streams_of[17], 71), 0)
    out_weight = centred(streams_of[10], (FEATS, D), FEATS ** -0.5, 0.125, ((0, 8),))
    norm_gain = jnp.clip(1.0 + 0.1 * jax.random.normal(streams_of[11], (D,), jnp.float32), 0.5, 1.5)
    router = centred(streams_of[12], (D, EXPERTS), (D // 4) ** -0.5, 0.25)
    routes_keys = jax.random.split(jax.random.fold_in(streams_of[13], 1), TOKENS // TOK_DEV)
    routes_turns = jax.random.permutation(jax.random.fold_in(streams_of[13], 3), TOKENS // TOK_DEV)
    routes = jax.vmap(lambda own, number: assign_block(jax.random.fold_in(streams_of[13], 2), own, number, TOK_DEV, EXPERTS, TOPK, CAPACITY, 1))(routes_keys, routes_turns).reshape((TOKENS, TOPK))
    gate_weight = centred(streams_of[14], (EXPERTS, D, FF), D ** -0.5, 0.125, ((0, 8), (2, 32)))
    up_weight = centred(streams_of[15], (EXPERTS, D, FF), D ** -0.5, 0.125, ((0, 8), (2, 32)))
    down_weight = centred(streams_of[16], (EXPERTS, FF, D), FF ** -0.5, 0.078125, ((0, 8), (1, 32)))
    return {"resid": resid, "queries": queries, "new_keys": new_keys, "new_values": new_values, "pool_keys": pool_keys, "pool_values": pool_values, "page_table": page_table, "serve_pages": serve_pages, "cache_lengths": cache_lengths, "parents": parents, "out_weight": out_weight, "norm_gain": norm_gain, "router": router, "routes": routes, "gate_weight": gate_weight, "up_weight": up_weight, "down_weight": down_weight}


NEGATIVE = -1e+30
EPSILON = 1e-05

def ancestors(parent_row):
    positions = jnp.arange(TREE, dtype=jnp.int32)
    linked = (parent_row[:, None] == positions[None, :]).astype(jnp.float32)
    reached = jnp.minimum(linked + jnp.eye(TREE, dtype=jnp.float32), 1.0)
    for rounds in range(max(1, TREE.bit_length())):
        reached = jnp.minimum(jnp.dot(reached, reached, precision=lax.Precision.HIGHEST), 1.0)
    return reached > 0.5

def reference(resid, queries, new_keys, new_values, pool_keys, pool_values, page_table, serve_pages, cache_lengths, parents, out_weight, norm_gain, router, routes, gate_weight, up_weight, down_weight):
    device_of = (jnp.arange(REQUESTS, dtype=jnp.int32) // REQ_DEV)[:, None]
    is_local = page_table < POOL_PAGES
    slot_index = jnp.maximum(page_table - POOL_PAGES, 0)
    holder = (slot_index // SLOTS).astype(jnp.int32)
    within = (slot_index % SLOTS).astype(jnp.int32)
    owner_grid = jnp.broadcast_to(device_of, holder.shape).astype(jnp.int32)
    served = serve_pages[holder, owner_grid, within]
    global_page = jnp.where(is_local, device_of * POOL_PAGES + page_table, holder * POOL_PAGES + served).astype(jnp.int32)
    score_scale = HEAD_DIM ** (-0.5)

    def attend(request):
        pages = global_page[request]
        cache_keys = pool_keys[pages].reshape(MAXLEN, HEADS, HEAD_DIM).astype(jnp.float32)
        cache_values = pool_values[pages].reshape(MAXLEN, HEADS, HEAD_DIM).astype(jnp.float32)
        start_row = (request * TREE).astype(jnp.int32)
        query_rows = lax.dynamic_slice_in_dim(queries, start_row, TREE, 0).reshape(TREE, HEADS, HEAD_DIM).astype(jnp.float32)
        tree_keys = lax.dynamic_slice_in_dim(new_keys, start_row, TREE, 0).reshape(TREE, HEADS, HEAD_DIM).astype(jnp.float32)
        tree_values = lax.dynamic_slice_in_dim(new_values, start_row, TREE, 0).reshape(TREE, HEADS, HEAD_DIM).astype(jnp.float32)
        cache_scores = jnp.einsum('qhd,khd->hqk', query_rows, cache_keys, precision=lax.Precision.HIGHEST) * score_scale
        tree_scores = jnp.einsum('qhd,khd->hqk', query_rows, tree_keys, precision=lax.Precision.HIGHEST) * score_scale
        visible = jnp.arange(MAXLEN, dtype=jnp.int32) < cache_lengths[request]
        ancestry = ancestors(parents[request])
        cache_scores = jnp.where(visible[None, None, :], cache_scores, NEGATIVE)
        tree_scores = jnp.where(ancestry[None, :, :], tree_scores, NEGATIVE)
        scores = jnp.concatenate([cache_scores, tree_scores], axis=-1)
        highest = lax.optimization_barrier(jnp.max(scores, axis=-1, keepdims=True))
        weights = lax.optimization_barrier(jnp.exp(scores - highest).astype(jnp.bfloat16)).astype(jnp.float32)
        denominator = lax.optimization_barrier(jnp.sum(weights, axis=-1))
        values_all = jnp.concatenate([cache_values, tree_values], axis=0)
        mixture = jnp.einsum('hqk,khd->qhd', weights, values_all, precision=lax.Precision.HIGHEST)
        mixture = mixture / jnp.transpose(denominator)[:, :, None]
        return mixture.astype(jnp.bfloat16).reshape(TREE, FEATS)
    attended = lax.map(attend, jnp.arange(REQUESTS, dtype=jnp.int32)).reshape(TOKENS, FEATS)
    projected = jnp.dot(attended, out_weight, preferred_element_type=jnp.float32)
    hidden_mid = resid.astype(jnp.float32) + projected
    normed = (hidden_mid * lax.rsqrt(lax.optimization_barrier(jnp.mean(hidden_mid * hidden_mid, axis=-1, keepdims=True)) + EPSILON) * norm_gain).astype(jnp.bfloat16)
    logits = jnp.dot(normed, router, preferred_element_type=jnp.float32)
    labels = jnp.arange(EXPERTS, dtype=jnp.int32)
    picked = routes[:, :, None] == labels[None, None, :]
    chosen = lax.optimization_barrier(jnp.sum(jnp.where(picked, logits[:, None, :], 0.0), axis=-1))
    first_gate = 1.0 / (1.0 + jnp.exp(chosen[:, 1] - chosen[:, 0]))
    second_gate = 1.0 / (1.0 + jnp.exp(chosen[:, 0] - chosen[:, 1]))
    gate_table = jnp.where(picked[:, 0], first_gate[:, None], 0.0) + jnp.where(picked[:, 1], second_gate[:, None], 0.0)
    expert_hits = jnp.any(picked, axis=1).astype(jnp.int32).reshape(N_FSDP, TOK_DEV, EXPERTS)
    expert_ranks = jnp.cumsum(expert_hits, axis=1, dtype=jnp.int32) - expert_hits
    slot_ids = jnp.arange(CAPACITY, dtype=jnp.int32)
    dispatch = (jnp.transpose(expert_hits, (0, 2, 1))[:, :, None, :] > 0) & (jnp.transpose(expert_ranks, (0, 2, 1))[:, :, None, :] == slot_ids[None, None, :, None])
    row_ids = jnp.arange(TOK_DEV, dtype=jnp.int32)
    token_of = lax.optimization_barrier(jnp.sum(jnp.where(dispatch, row_ids[None, None, None, :], 0), axis=-1)).astype(jnp.int32)
    token_of = (token_of + (jnp.arange(N_FSDP, dtype=jnp.int32) * TOK_DEV)[:, None, None]).astype(jnp.int32)
    filled = jnp.any(dispatch, axis=-1)

    def expert_step(carry, expert):
        token_flat = token_of[:, expert, :].reshape(-1)
        rows = normed[token_flat]
        gate_proj = jnp.dot(rows, gate_weight[expert], preferred_element_type=jnp.float32)
        lifted = jnp.dot(rows, up_weight[expert], preferred_element_type=jnp.float32)
        active = (jax.nn.silu(gate_proj) * lifted).astype(jnp.bfloat16)
        result = jnp.dot(active, down_weight[expert], preferred_element_type=jnp.float32)
        scaling = jnp.where(filled[:, expert, :].reshape(-1), gate_table[token_flat, expert], 0.0)
        return (carry.at[token_flat].add(scaling[:, None] * result), None)
    expert_total, unused = lax.scan(expert_step, jnp.zeros((TOKENS, D), jnp.float32), jnp.arange(EXPERTS, dtype=jnp.int32))
    return (hidden_mid + expert_total).astype(jnp.bfloat16)
```

```python
import functools

import jax
import jax.numpy as jnp
from jax import lax
from jax.experimental import pallas as pl
from jax.experimental.pallas import tpu as pltpu
from jax.sharding import PartitionSpec as P

HEAD_DIM = 64
CAPACITY = 36
NEGATIVE = -1e30
EPSILON = 1e-05
MESH = pl.DeviceIdType.MESH
F32 = jnp.float32
BF16 = jnp.bfloat16


def mm(a, b):
    return jnp.dot(a, b, preferred_element_type=F32)


def mm_nt(a, b):
    return lax.dot_general(a, b, (((1,), (1,)), ((), ())), preferred_element_type=F32)


def mm_tn(a, b):
    return lax.dot_general(a, b, (((0,), (0,)), ((), ())), preferred_element_type=F32)


def iota(shape, dim):
    return lax.broadcasted_iota(jnp.int32, shape, dim)


def attention_kernel(
    fs, vs,
    q_ref, nk_ref, nv_ref, table_ref, length_ref, serve_ref, parent_ref, resid_ref, ow_ref, gain_ref,
    pk_ref, pv_ref, wg_ref, wu_ref, wd_ref,
    normed_ref, cols_ref, wg2_ref, wu2_ref, wd2_ref,
    kbuf, vbuf, s_scr, lim_scr, rq_scr, wt_scr, qsend, qrecv, msend, mrecv, osend, orecv, tsend, trecv,
    pown, psend, precv, hsend,
    local_sem, w_sem, q_sem, m_sem, o_sem, t_sem, p_sem, n_sem, h_sem,
):
    requests, pages_each = table_ref.shape
    tree = parent_ref.shape[1]
    features = q_ref.shape[1]
    heads = features // HEAD_DIM
    page_rows = pk_ref.shape[1]
    local_pages = pk_ref.shape[0] // 2
    pool_pages = pk_ref.shape[0]
    rows = heads * tree
    wide = 256
    width = ow_ref.shape[1]
    owners = resid_ref.shape[0]
    me = lax.axis_index("fsdp")
    ve = lax.axis_index("vocab")
    twin = me + 1 - 2 * lax.rem(me, 2)

    barrier = pltpu.get_barrier_semaphore()

    def hail_fsdp(k, carry):
        pl.semaphore_signal(barrier, inc=1, device_id={"fsdp": lax.rem(me + k, fs)}, device_id_type=MESH)
        return carry

    def hail_vocab(k, carry):
        pl.semaphore_signal(barrier, inc=1, device_id={"vocab": lax.rem(ve + k, vs)}, device_id_type=MESH)
        return carry

    lax.fori_loop(1, fs, hail_fsdp, 0)
    lax.fori_loop(1, vs, hail_vocab, 0)
    half = local_pages
    pool_copies = [
        pltpu.make_async_copy(src.at[pl.ds(at, half)], dst.at[pl.ds(at, half)], local_sem.at[i])
        for i, (src, dst, at) in enumerate(
            ((pk_ref, kbuf, 0), (pv_ref, vbuf, 0), (pk_ref, kbuf, half), (pv_ref, vbuf, half))
        )
    ]
    for copy in pool_copies:
        copy.start()

    lane = iota((local_pages, pages_each), 1)
    sub = iota((local_pages, pages_each), 0)
    counts = [jnp.clip(length_ref[r] - page_rows * lane, 0, page_rows) for r in range(requests)]

    def lookup(target):
        hits = [table_ref[r : r + 1, :] == target for r in range(requests)]
        seen = [jnp.sum(jnp.where(h, c, 0).astype(F32), axis=1, keepdims=True) for h, c in zip(hits, counts)]
        return seen, jnp.sum(jnp.where(hits[1], 1.0, 0.0), axis=1, keepdims=True)

    (seen0, seen1), _ = lookup(sub)
    lane_w = iota((local_pages, 2 * wide), 1)
    lim_scr[...] = jnp.where(lane_w < wide, seen0, seen1).astype(jnp.int32)
    holder = lax.rem(sub + me, fs)
    (far0, far1), far_rq = lookup(holder + pool_pages)
    rq_scr[...] = jnp.broadcast_to(far_rq, rq_scr.shape)
    msend[...] = jnp.broadcast_to((far0 + far1)[:, :, None], msend.shape)

    pl.semaphore_wait(barrier, fs - 1 + vs - 1)

    q0 = q_ref[0:tree, :].astype(F32)
    q1 = q_ref[tree : 2 * tree, :].astype(F32)

    def q_copy(k, to):
        return pltpu.make_async_remote_copy(
            src_ref=qsend.at[k], dst_ref=qrecv.at[k], send_sem=q_sem.at[0, k], recv_sem=q_sem.at[1, k],
            device_id={"fsdp": to}, device_id_type=MESH)

    def m_copy(k, to):
        return pltpu.make_async_remote_copy(
            src_ref=msend.at[k], dst_ref=mrecv.at[k], send_sem=m_sem.at[0, k], recv_sem=m_sem.at[1, k],
            device_id={"fsdp": to}, device_id_type=MESH)

    def o_copy(k, to):
        return pltpu.make_async_remote_copy(
            src_ref=osend.at[k], dst_ref=orecv.at[k], send_sem=o_sem.at[0, k], recv_sem=o_sem.at[1, k],
            device_id={"fsdp": to}, device_id_type=MESH)

    def t_copy(k, to):
        return pltpu.make_async_remote_copy(
            src_ref=tsend.at[k], dst_ref=trecv.at[k], send_sem=t_sem.at[0, k], recv_sem=t_sem.at[1, k],
            device_id={"fsdp": to}, device_id_type=MESH)

    def pick_query(k):
        pick = rq_scr[pl.ds(k, 1), :]
        return (q0 * (1.0 - pick) + q1 * pick).astype(BF16)

    def send_query(k, carry):
        qsend[k] = pick_query(k)
        to = lax.rem(me + k, fs)
        q_copy(k, to).start()
        m_copy(k, to).start()
        return carry

    lax.fori_loop(1, fs, send_query, 0)
    qrecv[0] = pick_query(0)
    mrecv[0] = msend[0]

    weight_copies = [
        pltpu.make_async_remote_copy(
            src_ref=src, dst_ref=dst, send_sem=w_sem.at[0, i], recv_sem=w_sem.at[1, i],
            device_id={"fsdp": twin}, device_id_type=MESH)
        for i, (src, dst) in enumerate(((wg_ref, wg2_ref), (wu_ref, wu2_ref), (wd_ref, wd2_ref)))
    ]
    for copy in weight_copies:
        copy.start()

    head_of = iota((1, features), 1) // HEAD_DIM
    head_masks = [jnp.where(head_of == h, 1.0, 0.0) for h in range(heads)]
    scaled_masks = [(m * HEAD_DIM**-0.5).astype(BF16) for m in head_masks]

    def spread(q):
        parts = [q * m for m in scaled_masks]
        return jnp.concatenate(parts + [jnp.zeros((wide - rows, features), BF16)], axis=0)

    def gather_heads(o):
        total = o[0:tree] * head_masks[0]
        for h in range(1, heads):
            total = total + o[h * tree : (h + 1) * tree] * head_masks[h]
        return total

    spread_q = [spread(q_ref[r * tree : (r + 1) * tree, :]) for r in range(requests)]
    both_q = jnp.concatenate(spread_q, axis=0)

    eye = jnp.where(iota((tree, tree), 0) == iota((tree, tree), 1), 1.0, 0.0)
    tile_heads = jnp.where(
        (iota((tree, wide), 1) % tree == iota((tree, wide), 0)) & (iota((tree, wide), 1) < rows), 1.0, 0.0
    ).astype(BF16)
    tree_scores = []
    for r in range(requests):
        linked = jnp.where(parent_ref[r : r + 1, :] == iota((tree, tree), 0), 1.0, 0.0)
        reach = jnp.minimum(linked + eye, 1.0)
        for _ in range(tree.bit_length()):
            half_reach = reach.astype(BF16)
            reach = jnp.minimum(mm(half_reach, half_reach), 1.0)
        seen = mm(reach.astype(BF16), tile_heads)
        scores = mm_nt(nk_ref[r * tree : (r + 1) * tree, :], spread_q[r])
        tree_scores.append(jnp.where(seen > 0.5, scores, NEGATIVE))
    top = jnp.concatenate([jnp.max(s, axis=0, keepdims=True) for s in tree_scores], axis=1)

    pool_copies[0].wait()
    key_row = iota((page_rows, 2 * wide), 0)
    chunk = 4

    def score_chunk(c, top):
        for i in range(chunk):
            page = c * chunk + i
            scores = mm_nt(kbuf[page], both_q)
            scores = jnp.where(key_row < lim_scr[pl.ds(page, 1), :], scores, NEGATIVE)
            s_scr[page] = scores
            top = jnp.maximum(top, jnp.max(scores, axis=0, keepdims=True))
        return top

    top = lax.fori_loop(0, local_pages // chunk, score_chunk, top)
    pool_copies[1].wait()

    def mix_chunk(c, carry):
        total, mixed = carry
        at = pl.ds(c * chunk, chunk)
        weights = jnp.exp(s_scr[at].reshape(chunk * page_rows, 2 * wide) - top).astype(BF16)
        total = total + jnp.sum(weights.astype(F32), axis=0, keepdims=True)
        values = vbuf[at].reshape(chunk * page_rows, features)
        return total, mixed + mm_tn(weights, values)

    total, mixed = lax.fori_loop(
        0, local_pages // chunk, mix_chunk,
        (jnp.zeros((1, 2 * wide), F32), jnp.zeros((2 * wide, features), F32)))
    own_top, own_total, own_mix = [], [], []
    for r in range(requests):
        top_r = top[:, r * wide : (r + 1) * wide]
        weights = jnp.exp(tree_scores[r] - top_r).astype(BF16)
        own_top.append(top_r)
        own_total.append(
            total[:, r * wide : (r + 1) * wide] + jnp.sum(weights.astype(F32), axis=0, keepdims=True))
        mix_r = mixed[r * wide : (r + 1) * wide] + mm_tn(weights, nv_ref[r * tree : (r + 1) * tree, :])
        own_mix.append(gather_heads(mix_r))

    pool_copies[2].wait()
    pool_copies[3].wait()
    stat_row = iota((8, 128), 0)
    held_row = iota((page_rows, wide), 0)

    def serve_one(k):
        asker = lax.rem(me - k + fs, fs)
        page = serve_ref[asker]
        limit = mrecv[k][0:1, :]
        limit = jnp.concatenate([limit, limit], axis=1)
        scores = mm_nt(kbuf[page], spread(qrecv[k]))
        scores = jnp.where(held_row < limit.astype(jnp.int32), scores, NEGATIVE)
        best = jnp.max(scores, axis=0, keepdims=True)
        weights = jnp.exp(scores - best).astype(BF16)
        amount = jnp.sum(weights.astype(F32), axis=0, keepdims=True)
        osend[k] = gather_heads(mm_tn(weights, vbuf[page])).astype(BF16)
        tsend[k] = jnp.where(
            stat_row == 0, best[:, 0:128],
            jnp.where(stat_row == 1, best[:, 128:256],
                      jnp.where(stat_row == 2, amount[:, 0:128], amount[:, 128:256])))

    group = 4

    def serve_group(first):
        base = first * group
        for i in range(group):
            k = base + i

            @pl.when(k > 0)
            def _():
                q_copy(k, me).wait_recv()
                m_copy(k, me).wait_recv()

        for i in range(group):
            serve_one(base + i)
        for i in range(group):
            k = base + i

            @pl.when(k > 0)
            def _():
                to = lax.rem(me - k + fs, fs)
                o_copy(k, to).start()
                t_copy(k, to).start()

    def serve_step(first, carry):
        serve_group(first)
        return carry

    lax.fori_loop(0, fs // group, serve_step, 0)
    orecv[0] = osend[0]
    trecv[0] = tsend[0]

    def await_stats(k, carry):
        t_copy(k, me).wait_recv()
        return carry

    lax.fori_loop(1, fs, await_stats, 0)

    pick = rq_scr[:, 0:128]
    weight_any = [jnp.zeros((fs, 128), F32), jnp.zeros((fs, 128), F32)]
    own_weight = []
    for r in range(requests):
        chosen = pick if r == 1 else 1.0 - pick
        shares = []
        for hh in range(2):
            best = jnp.where(chosen > 0.5, trecv[:, hh, :], NEGATIVE)
            amount = trecv[:, 2 + hh, :]
            mine = own_top[r][:, hh * 128 : (hh + 1) * 128]
            highest = jnp.maximum(jnp.max(best, axis=0, keepdims=True), mine)
            weights = jnp.exp(best - highest) * chosen
            own = jnp.exp(mine - highest)
            bottom = jnp.sum(weights * amount, axis=0, keepdims=True) + (
                own * own_total[r][:, hh * 128 : (hh + 1) * 128])
            weight_any[hh] = weight_any[hh] + weights / bottom
            shares.append(own / bottom)
        own_weight.append(shares)
    for hh in range(2):
        sheet = jnp.concatenate(
            [weight_any[hh]]
            + [jnp.broadcast_to(own_weight[r][hh], (8, 128)) for r in range(requests)]
            + [jnp.zeros((128 - fs - 8 * requests, 128), F32)], axis=0)
        wt_scr[hh * 128 : (hh + 1) * 128, :] = sheet.T

    def factor(col):
        out = wt_scr[0:tree, col : col + 1] * head_masks[0]
        for h in range(1, heads):
            out = out + wt_scr[h * tree : (h + 1) * tree, col : col + 1] * head_masks[h]
        return out

    def await_parts(k, carry):
        o_copy(k, me).wait_recv()
        return carry

    lax.fori_loop(1, fs, await_parts, 0)
    merged = [own_mix[r] * factor(fs + 8 * r) for r in range(requests)]
    for k in range(fs):
        part = orecv[k].astype(F32) * factor(k)
        pick_row = rq_scr[k : k + 1, :]
        merged[0] = merged[0] + part * (1.0 - pick_row)
        merged[1] = merged[1] + part * pick_row
    attended = jnp.concatenate(merged, axis=0).astype(BF16)

    per_owner = resid_ref.shape[1]
    tile = 256
    for c in range(width // tile):
        block = mm(attended, ow_ref[:, c * tile : (c + 1) * tile])
        for o in range(owners):
            piece = block[o * per_owner : (o + 1) * per_owner]
            pown[o, :, c * tile : (c + 1) * tile] = piece
            psend[o, :, c * tile : (c + 1) * tile] = piece.astype(BF16)

    def p_copy(k, to):
        return pltpu.make_async_remote_copy(
            src_ref=psend.at[to], dst_ref=precv.at[k], send_sem=p_sem.at[0, k], recv_sem=p_sem.at[1, k],
            device_id={"vocab": to}, device_id_type=MESH)

    def n_copy(k, owner, to):
        return pltpu.make_async_remote_copy(
            src_ref=normed_ref.at[owner], dst_ref=normed_ref.at[owner],
            send_sem=n_sem.at[0, k], recv_sem=n_sem.at[1, k],
            device_id={"vocab": to}, device_id_type=MESH)

    def h_copy(k, owner, to):
        return pltpu.make_async_remote_copy(
            src_ref=hsend.at[to], dst_ref=cols_ref.at[owner], send_sem=h_sem.at[0, k], recv_sem=h_sem.at[1, k],
            device_id={"vocab": to}, device_id_type=MESH)

    for k in range(1, vs):
        to = lax.rem(ve + k, vs)

        @pl.when(to < owners)
        def _():
            p_copy(k, to).start()

    @pl.when(ve < owners)
    def _():
        hidden = resid_ref[ve].astype(F32) + pown[ve]
        for k in range(1, vs):
            p_copy(k, ve).wait_recv()
            hidden = hidden + precv[k].astype(F32)
        mean = jnp.mean(hidden * hidden, axis=-1, keepdims=True)
        normed_ref[ve] = (hidden * lax.rsqrt(mean + EPSILON) * gain_ref[...]).astype(BF16)
        for k in range(1, vs):
            n_copy(k, ve, lax.rem(ve + k, vs)).start()
        columns = width // vs
        padded = hsend.shape[2]
        for v in range(vs):
            turned = hidden if v == 0 else pltpu.roll(hidden, width - v * columns, 1)
            hsend[v] = turned[:, 0:padded]
        for k in range(1, vs):
            h_copy(k, ve, lax.rem(ve + k, vs)).start()
        cols_ref[ve] = hsend[ve]

    for k in range(1, vs):
        owner = lax.rem(ve - k + vs, vs)

        @pl.when(owner < owners)
        def _():
            n_copy(k, owner, ve).wait_recv()
            h_copy(k, owner, ve).wait_recv()

    def await_sends(k, carry):
        q_copy(k, me).wait_send()
        m_copy(k, me).wait_send()
        o_copy(k, me).wait_send()
        t_copy(k, me).wait_send()
        return carry

    lax.fori_loop(1, fs, await_sends, 0)
    for k in range(1, vs):
        to = lax.rem(ve + k, vs)

        @pl.when(to < owners)
        def _():
            p_copy(k, to).wait_send()

    @pl.when(ve < owners)
    def _():
        for k in range(1, vs):
            to = lax.rem(ve + k, vs)
            n_copy(k, ve, to).wait_send()
            h_copy(k, ve, to).wait_send()

    for copy in weight_copies:
        copy.wait()


def expert_kernel(
    fs, vs, zs,
    normed_ref, cols_ref, routes_ref, router_ref, wg_ref, wu_ref, wd_ref, wg2_ref, wu2_ref, wd2_ref,
    out_ref,
    wg, wu, wd, xbuf, obuf, sbuf, rbuf, ysend, yrecv, yback, yhome, fsend, frecv,
    w_sem, ag_sem, rs_sem, y_sem, b_sem, f_sem,
):
    tokens, width = normed_ref.shape
    pair = xbuf.shape[1]
    block = pair // 2
    slots = ysend.shape[0]
    me = lax.axis_index("fsdp")
    ve = lax.axis_index("vocab")
    core = lax.rem(me, 2)
    z = lax.rem(me // 2, zs)
    yhi = me // (2 * zs)
    right = (yhi * zs + lax.rem(z + 1, zs)) * 2 + core
    left = (yhi * zs + lax.rem(z + zs - 1, zs)) * 2 + core
    across = ((1 - yhi) * zs + z) * 2 + core

    barrier = pltpu.get_barrier_semaphore()
    for peer in (left, right, across):
        pl.semaphore_signal(barrier, inc=1, device_id={"fsdp": peer}, device_id_type=MESH)
    for k in range(1, vs):
        pl.semaphore_signal(barrier, inc=1, device_id={"vocab": lax.rem(ve + k, vs)}, device_id_type=MESH)
    loads = []
    for i, (src, dst) in enumerate(
        ((wg_ref, wg.at[0]), (wg2_ref, wg.at[1]), (wu_ref, wu.at[0]), (wu2_ref, wu.at[1]),
         (wd_ref, wd.at[0]), (wd2_ref, wd.at[1]))):
        loads.append(pltpu.make_async_copy(src, dst, w_sem.at[i]))
    for load in loads:
        load.start()

    lane = iota((tokens, 128), 1)
    first, second = routes_ref[:, 0:1], routes_ref[:, 1:2]
    hits = jnp.where((first == lane) | (second == lane), 1.0, 0.0)
    below = jnp.where(iota((tokens, tokens), 1) < iota((tokens, tokens), 0), 1.0, 0.0).astype(BF16)
    ranks = mm(below, hits.astype(BF16))
    my_hit = jnp.sum(jnp.where(lane == ve, hits, 0.0), axis=1, keepdims=True)
    my_rank = jnp.sum(jnp.where(lane == ve, ranks, 0.0), axis=1, keepdims=True)
    mine = jnp.where((my_hit > 0.5) & (my_rank == lane.astype(F32)), 1.0, 0.0)
    mine_half = mine.astype(BF16)

    picked = mm_tn(mine_half, normed_ref[...])
    ysend[...] = picked[0:slots].astype(BF16)
    pl.semaphore_wait(barrier, 3 + vs - 1)
    y_out = pltpu.make_async_remote_copy(
        src_ref=ysend, dst_ref=yrecv, send_sem=y_sem.at[0], recv_sem=y_sem.at[1],
        device_id={"fsdp": across}, device_id_type=MESH)
    y_out.start()

    logits = mm(normed_ref[...], router_ref[...])
    lane8 = iota(logits.shape, 1)
    chosen0 = jnp.sum(jnp.where(lane8 == first, logits, 0.0), axis=1, keepdims=True)
    chosen1 = jnp.sum(jnp.where(lane8 == second, logits, 0.0), axis=1, keepdims=True)
    gate0 = 1.0 / (1.0 + jnp.exp(chosen1 - chosen0))
    gate1 = 1.0 / (1.0 + jnp.exp(chosen0 - chosen1))
    my_gate = jnp.where(first == ve, gate0, jnp.where(second == ve, gate1, 0.0))
    slot_gate = jnp.sum((mine * my_gate).T, axis=1, keepdims=True)[0:slots]
    spread_e = jnp.where(iota((128, vs * slots), 0) == iota((128, vs * slots), 1) // slots, 1.0, 0.0).astype(BF16)
    all_hits = mm(hits.astype(BF16), spread_e)
    all_ranks = mm(ranks.astype(BF16), spread_e)
    slot_at = (iota((tokens, vs * slots), 1) % slots).astype(F32)
    back = jnp.where((all_hits > 0.5) & (all_ranks == slot_at), 1.0, 0.0).astype(BF16)

    y_out.wait_recv()
    xbuf[0] = jnp.concatenate([picked[0:block], yrecv[...].astype(F32)[0:block]], axis=0).astype(BF16)

    cut = width // 2
    ways = (right, left)
    steps = zs // 2

    def halves(step, way):
        return (way,) if step == steps - 1 else (0, 1)

    def gather_copy(way, step, h):
        src = 0 if step == 0 else 2 * step - 1 + way
        dst = zs - 1 if step == steps - 1 else 2 * step + 1 + way
        at = pl.ds(h * cut, cut)
        return pltpu.make_async_remote_copy(
            src_ref=xbuf.at[src, :, at], dst_ref=xbuf.at[dst, :, at],
            send_sem=ag_sem.at[0, way, step, h], recv_sem=ag_sem.at[1, way, step, h],
            device_id={"fsdp": ways[way]}, device_id_type=MESH)

    def expert(first_block, count):
        rows = xbuf[first_block : first_block + count].reshape(count * pair, width)
        acts = []
        for j in range(2):
            gate = mm(rows, wg[j])
            acts.append((gate / (1.0 + jnp.exp(-gate)) * mm(rows, wu[j])).astype(BF16))
        tile = width // 3
        for c in range(3):
            at = pl.ds(c * tile, tile)
            out = mm(acts[0], wd[0, :, at]) + mm(acts[1], wd[1, :, at])
            obuf[first_block : first_block + count, :, at] = out.reshape(count, pair, tile)

    for step in range(steps):
        for way in range(2):
            for h in (0, 1):
                if step > 0:
                    gather_copy(way, step - 1, h).wait_recv()
                if h in halves(step, way):
                    gather_copy(way, step, h).start()
        if step == 0:
            for load in loads:
                load.wait()
            expert(0, 1)
        else:
            expert(2 * step - 1, 2)
    for way in range(2):
        gather_copy(way, steps - 1, way).wait_recv()
    expert(zs - 1, 1)

    def sum_copy(way, step, h):
        at = pl.ds(h * cut, cut)
        return pltpu.make_async_remote_copy(
            src_ref=sbuf.at[way, step, :, at], dst_ref=rbuf.at[way, step, :, at],
            send_sem=rs_sem.at[0, way, step, h], recv_sem=rs_sem.at[1, way, step, h],
            device_id={"fsdp": ways[way]}, device_id_type=MESH)

    for step in range(steps):
        for h in (0, 1):
            for way in range(2):
                at = pl.ds(h * cut, cut)
                if step == 0:
                    if h != way:
                        continue
                    sbuf[way, 0, :, at] = obuf[zs - 1, :, at].astype(BF16)
                else:
                    source = 2 * (steps - step) - way
                    value = obuf[source, :, at]
                    if step > 1 or h == way:
                        sum_copy(way, step - 1, h).wait_recv()
                        value = value + rbuf[way, step - 1, :, at].astype(F32)
                    sbuf[way, step, :, at] = value.astype(BF16)
                sum_copy(way, step, h).start()
    for way in range(2):
        for h in (0, 1):
            sum_copy(way, steps - 1, h).wait_recv()
    whole = obuf[0] + rbuf[0, steps - 1].astype(F32) + rbuf[1, steps - 1].astype(F32)
    yback[...] = jnp.concatenate(
        [whole[block:pair], jnp.zeros((slots - block, width), F32)], axis=0).astype(BF16)
    b_out = pltpu.make_async_remote_copy(
        src_ref=yback, dst_ref=yhome, send_sem=b_sem.at[0], recv_sem=b_sem.at[1],
        device_id={"fsdp": across}, device_id_type=MESH)
    b_out.start()
    b_out.wait_recv()
    gated = (whole[0:slots] + yhome[...].astype(F32)) * slot_gate

    columns = width // vs
    padded = fsend.shape[2]

    def f_copy(k, to, slot):
        return pltpu.make_async_remote_copy(
            src_ref=fsend.at[to], dst_ref=frecv.at[slot], send_sem=f_sem.at[0, k], recv_sem=f_sem.at[1, k],
            device_id={"vocab": to}, device_id_type=MESH)

    for v in range(vs):
        turned = gated if v == 0 else pltpu.roll(gated, width - v * columns, 1)
        fsend[v] = turned[:, 0:padded].astype(BF16)
    for k in range(1, vs):
        f_copy(k, lax.rem(ve + k, vs), ve).start()
    frecv[ve] = fsend[ve]
    for k in range(1, vs):
        f_copy(k, ve, lax.rem(ve - k + vs, vs)).wait_recv()
    mixture = mm(back, frecv[...].reshape(vs * slots, padded))
    out_ref[...] = (cols_ref[...] + mixture)[:, 0:columns].astype(BF16)

    y_out.wait_send()
    b_out.wait_send()
    for step in range(steps):
        for way in range(2):
            for h in halves(step, way):
                gather_copy(way, step, h).wait_send()
    for step in range(steps):
        for way in range(2):
            for h in (0, 1):
                if step > 0 or h == way:
                    sum_copy(way, step, h).wait_send()
    for k in range(1, vs):
        f_copy(k, lax.rem(ve + k, vs), ve).wait_send()


def per_device(
    resid, queries, new_keys, new_values, pool_keys, pool_values, page_table, serve_pages, cache_lengths, parents,
    out_weight, norm_gain, router, routes, gate_weight, up_weight, down_weight,
):
    fs, vs = lax.axis_size("fsdp"), lax.axis_size("vocab")
    zs = fs // 4
    tokens, width = resid.shape
    features = queries.shape[1]
    tree = parents.shape[1]
    pool_pages, page_rows, _ = pool_keys.shape
    hidden = gate_weight.shape[2]
    vmem = pl.BlockSpec(memory_space=pltpu.VMEM)
    smem = pl.BlockSpec(memory_space=pltpu.SMEM)
    hbm = pl.BlockSpec(memory_space=pl.ANY)
    dma = pltpu.SemaphoreType.DMA
    padded = -(-(width // vs) // 128) * 128
    per_owner = 16
    owners = tokens // per_owner
    wg, wu, wd = gate_weight[0], up_weight[0], down_weight[0]
    like = lambda a: jax.ShapeDtypeStruct(a.shape, a.dtype)
    normed, cols, wg2, wu2, wd2 = pl.pallas_call(
        functools.partial(attention_kernel, fs, vs),
        out_shape=(
            jax.ShapeDtypeStruct((owners, per_owner, width), BF16),
            jax.ShapeDtypeStruct((owners, per_owner, padded), F32),
            like(wg), like(wu), like(wd)),
        in_specs=[vmem] * 4 + [smem] * 2 + [vmem] * 4 + [hbm] * 5,
        out_specs=(vmem, vmem, hbm, hbm, hbm),
        scratch_shapes=[
            pltpu.VMEM(pool_keys.shape, BF16),
            pltpu.VMEM(pool_values.shape, BF16),
            pltpu.VMEM((pool_pages // 2, page_rows, 512), F32),
            pltpu.VMEM((pool_pages // 2, 512), jnp.int32),
            pltpu.VMEM((fs, features), F32),
            pltpu.VMEM((256, 128), F32),
            pltpu.VMEM((fs, tree, features), BF16),
            pltpu.VMEM((fs, tree, features), BF16),
            pltpu.VMEM((fs, 8, 128), F32),
            pltpu.VMEM((fs, 8, 128), F32),
            pltpu.VMEM((fs, tree, features), BF16),
            pltpu.VMEM((fs, tree, features), BF16),
            pltpu.VMEM((fs, 8, 128), F32),
            pltpu.VMEM((fs, 8, 128), F32),
            pltpu.VMEM((owners, per_owner, width), F32),
            pltpu.VMEM((owners, per_owner, width), BF16),
            pltpu.VMEM((vs, per_owner, width), BF16),
            pltpu.VMEM((vs, per_owner, padded), F32),
            dma((4,)), dma((2, 3)), dma((2, fs)), dma((2, fs)), dma((2, fs)), dma((2, fs)),
            dma((2, vs)), dma((2, vs)), dma((2, vs)),
        ],
        compiler_params=pltpu.CompilerParams(
            collective_id=1, has_side_effects=True, vmem_limit_bytes=56 * 2**20),
        name="attention",
    )(
        queries, new_keys, new_values, page_table, cache_lengths, serve_pages.reshape(-1), parents,
        resid.reshape(owners, per_owner, width), out_weight, norm_gain.reshape(1, width),
        pool_keys, pool_values, wg, wu, wd)
    pair, slots = 80, 48
    return pl.pallas_call(
        functools.partial(expert_kernel, fs, vs, zs),
        out_shape=jax.ShapeDtypeStruct((tokens, width // vs), BF16),
        in_specs=[vmem] * 4 + [hbm] * 6,
        out_specs=vmem,
        scratch_shapes=[
            pltpu.VMEM((2, width, hidden), BF16),
            pltpu.VMEM((2, width, hidden), BF16),
            pltpu.VMEM((2, hidden, width), BF16),
            pltpu.VMEM((zs, pair, width), BF16),
            pltpu.VMEM((zs, pair, width), F32),
            pltpu.VMEM((2, zs // 2, pair, width), BF16),
            pltpu.VMEM((2, zs // 2, pair, width), BF16),
            pltpu.VMEM((slots, width), BF16),
            pltpu.VMEM((slots, width), BF16),
            pltpu.VMEM((slots, width), BF16),
            pltpu.VMEM((slots, width), BF16),
            pltpu.VMEM((vs, slots, padded), BF16),
            pltpu.VMEM((vs, slots, padded), BF16),
            dma((6,)), dma((2, 2, zs // 2, 2)), dma((2, 2, zs // 2, 2)), dma((2,)), dma((2,)), dma((2, vs)),
        ],
        compiler_params=pltpu.CompilerParams(
            collective_id=2, has_side_effects=True, vmem_limit_bytes=56 * 2**20),
        name="experts",
    )(normed.reshape(tokens, width), cols.reshape(tokens, padded), routes, router, wg, wu, wd, wg2, wu2, wd2)


def solution(mesh):
    in_specs = (
        P("fsdp", None), P("fsdp", "vocab"), P("fsdp", "vocab"), P("fsdp", "vocab"),
        P("fsdp", None, "vocab"), P("fsdp", None, "vocab"), P("fsdp", None), P("fsdp", None, None),
        P("fsdp"), P("fsdp", None), P("vocab", None), P(), P(), P("fsdp", None),
        P("vocab", None, "fsdp"), P("vocab", None, "fsdp"), P("vocab", "fsdp", None),
    )
    return jax.shard_map(
        per_device, mesh=mesh, in_specs=in_specs, out_specs=P("fsdp", "vocab"), check_vma=False
    )
```

```python
import functools

import jax
import jax.numpy as jnp
from jax import lax
from jax.experimental import pallas as pl
from jax.experimental.pallas import tpu as pltpu
from jax.sharding import PartitionSpec as P

HEAD_DIM = 64
CAPACITY = 36
NEGATIVE = -1e30
EPSILON = 1e-05
MESH = pl.DeviceIdType.MESH
F32 = jnp.float32
BF16 = jnp.bfloat16


def mm(a, b):
    return jnp.dot(a, b, preferred_element_type=F32)


def mm_nt(a, b):
    return lax.dot_general(a, b, (((1,), (1,)), ((), ())), preferred_element_type=F32)


def mm_tn(a, b):
    return lax.dot_general(a, b, (((0,), (0,)), ((), ())), preferred_element_type=F32)


def iota(shape, dim):
    return lax.broadcasted_iota(jnp.int32, shape, dim)


def attention_kernel(
    fs, vs,
    q_ref, nk_ref, nv_ref, table_ref, length_ref, serve_ref, parent_ref, resid_ref, ow_ref, gain_ref,
    pk_ref, pv_ref, wg_ref, wu_ref,
    normed_ref, cols_ref, more_ref,
    kbuf, vbuf, s_scr, lim_scr, rq_scr, wt_scr, qsend, qrecv, msend, mrecv, osend, orecv, tsend, trecv,
    pown, psend, precv, hsend,
    local_sem, w_sem, q_sem, m_sem, o_sem, t_sem, p_sem, n_sem, h_sem,
):
    requests, pages_each = table_ref.shape
    tree = parent_ref.shape[1]
    features = q_ref.shape[1]
    heads = features // HEAD_DIM
    page_rows = pk_ref.shape[1]
    local_pages = pk_ref.shape[0] // 2
    pool_pages = pk_ref.shape[0]
    rows = heads * tree
    wide = 256
    width = ow_ref.shape[1]
    owners = resid_ref.shape[0]
    me = lax.axis_index("fsdp")
    ve = lax.axis_index("vocab")
    twin = me + 1 - 2 * lax.rem(me, 2)
    across = lax.rem(me + fs // 2, fs)

    barrier = pltpu.get_barrier_semaphore()

    def hail_fsdp(k, carry):
        pl.semaphore_signal(barrier, inc=1, device_id={"fsdp": lax.rem(me + k, fs)}, device_id_type=MESH)
        return carry

    def hail_vocab(k, carry):
        pl.semaphore_signal(barrier, inc=1, device_id={"vocab": lax.rem(ve + k, vs)}, device_id_type=MESH)
        return carry

    lax.fori_loop(1, fs, hail_fsdp, 0)
    lax.fori_loop(1, vs, hail_vocab, 0)
    half = local_pages
    pool_copies = [
        pltpu.make_async_copy(src.at[pl.ds(at, half)], dst.at[pl.ds(at, half)], local_sem.at[i])
        for i, (src, dst, at) in enumerate(
            ((pk_ref, kbuf, 0), (pv_ref, vbuf, 0), (pk_ref, kbuf, half), (pv_ref, vbuf, half))
        )
    ]
    for copy in pool_copies:
        copy.start()

    lane = iota((local_pages, pages_each), 1)
    sub = iota((local_pages, pages_each), 0)
    counts = [jnp.clip(length_ref[r] - page_rows * lane, 0, page_rows) for r in range(requests)]

    def lookup(target):
        hits = [table_ref[r : r + 1, :] == target for r in range(requests)]
        seen = [jnp.sum(jnp.where(h, c, 0).astype(F32), axis=1, keepdims=True) for h, c in zip(hits, counts)]
        return seen, jnp.sum(jnp.where(hits[1], 1.0, 0.0), axis=1, keepdims=True)

    (seen0, seen1), _ = lookup(sub)
    lane_w = iota((local_pages, 2 * wide), 1)
    lim_scr[...] = jnp.where(lane_w < wide, seen0, seen1).astype(jnp.int32)
    holder = lax.rem(sub + me, fs)
    (far0, far1), far_rq = lookup(holder + pool_pages)
    rq_scr[...] = jnp.broadcast_to(far_rq, rq_scr.shape)
    msend[...] = jnp.broadcast_to((far0 + far1)[:, :, None], msend.shape)

    pl.semaphore_wait(barrier, fs - 1 + vs - 1)

    q0 = q_ref[0:tree, :].astype(F32)
    q1 = q_ref[tree : 2 * tree, :].astype(F32)

    def q_copy(k, to):
        return pltpu.make_async_remote_copy(
            src_ref=qsend.at[k], dst_ref=qrecv.at[k], send_sem=q_sem.at[0, k], recv_sem=q_sem.at[1, k],
            device_id={"fsdp": to}, device_id_type=MESH)

    def m_copy(k, to):
        return pltpu.make_async_remote_copy(
            src_ref=msend.at[k], dst_ref=mrecv.at[k], send_sem=m_sem.at[0, k], recv_sem=m_sem.at[1, k],
            device_id={"fsdp": to}, device_id_type=MESH)

    def o_copy(k, to):
        return pltpu.make_async_remote_copy(
            src_ref=osend.at[k], dst_ref=orecv.at[k], send_sem=o_sem.at[0, k], recv_sem=o_sem.at[1, k],
            device_id={"fsdp": to}, device_id_type=MESH)

    def t_copy(k, to):
        return pltpu.make_async_remote_copy(
            src_ref=tsend.at[k], dst_ref=trecv.at[k], send_sem=t_sem.at[0, k], recv_sem=t_sem.at[1, k],
            device_id={"fsdp": to}, device_id_type=MESH)

    def pick_query(k):
        pick = rq_scr[pl.ds(k, 1), :]
        return (q0 * (1.0 - pick) + q1 * pick).astype(BF16)

    def send_query(k, carry):
        qsend[k] = pick_query(k)
        to = lax.rem(me + k, fs)
        q_copy(k, to).start()
        m_copy(k, to).start()
        return carry

    lax.fori_loop(1, fs, send_query, 0)
    qrecv[0] = pick_query(0)
    mrecv[0] = msend[0]

    kinds = (wg_ref, wu_ref)

    def weight_copy(src, at, to):
        return pltpu.make_async_remote_copy(
            src_ref=src, dst_ref=more_ref.at[at], send_sem=w_sem.at[0, at], recv_sem=w_sem.at[1, at],
            device_id={"fsdp": to}, device_id_type=MESH)

    far_copies = [weight_copy(src, 2 + i, across) for i, src in enumerate(kinds)]
    near_copies = [weight_copy(src, i, twin) for i, src in enumerate(kinds)]
    pass_copies = [weight_copy(more_ref.at[2 + i], 4 + i, twin) for i in range(2)]
    for copy in far_copies + near_copies:
        copy.start()

    head_of = iota((1, features), 1) // HEAD_DIM
    head_masks = [jnp.where(head_of == h, 1.0, 0.0) for h in range(heads)]
    scaled_masks = [(m * HEAD_DIM**-0.5).astype(BF16) for m in head_masks]

    def spread(q):
        parts = [q * m for m in scaled_masks]
        return jnp.concatenate(parts + [jnp.zeros((wide - rows, features), BF16)], axis=0)

    def gather_heads(o):
        total = o[0:tree] * head_masks[0]
        for h in range(1, heads):
            total = total + o[h * tree : (h + 1) * tree] * head_masks[h]
        return total

    spread_q = [spread(q_ref[r * tree : (r + 1) * tree, :]) for r in range(requests)]
    both_q = jnp.concatenate(spread_q, axis=0)

    eye = jnp.where(iota((tree, tree), 0) == iota((tree, tree), 1), 1.0, 0.0)
    tile_heads = jnp.where(
        (iota((tree, wide), 1) % tree == iota((tree, wide), 0)) & (iota((tree, wide), 1) < rows), 1.0, 0.0
    ).astype(BF16)
    tree_scores = []
    for r in range(requests):
        linked = jnp.where(parent_ref[r : r + 1, :] == iota((tree, tree), 0), 1.0, 0.0)
        reach = jnp.minimum(linked + eye, 1.0)
        for _ in range(tree.bit_length()):
            half_reach = reach.astype(BF16)
            reach = jnp.minimum(mm(half_reach, half_reach), 1.0)
        seen = mm(reach.astype(BF16), tile_heads)
        scores = mm_nt(nk_ref[r * tree : (r + 1) * tree, :], spread_q[r])
        tree_scores.append(jnp.where(seen > 0.5, scores, NEGATIVE))
    top = jnp.concatenate([jnp.max(s, axis=0, keepdims=True) for s in tree_scores], axis=1)

    pool_copies[0].wait()
    key_row = iota((page_rows, 2 * wide), 0)
    chunk = 4

    def score_chunk(c, top):
        for i in range(chunk):
            page = c * chunk + i
            scores = mm_nt(kbuf[page], both_q)
            scores = jnp.where(key_row < lim_scr[pl.ds(page, 1), :], scores, NEGATIVE)
            s_scr[page] = scores
            top = jnp.maximum(top, jnp.max(scores, axis=0, keepdims=True))
        return top

    top = lax.fori_loop(0, local_pages // chunk, score_chunk, top)
    pool_copies[1].wait()

    def mix_chunk(c, carry):
        total, mixed = carry
        at = pl.ds(c * chunk, chunk)
        weights = jnp.exp(s_scr[at].reshape(chunk * page_rows, 2 * wide) - top).astype(BF16)
        total = total + jnp.sum(weights.astype(F32), axis=0, keepdims=True)
        values = vbuf[at].reshape(chunk * page_rows, features)
        return total, mixed + mm_tn(weights, values)

    total, mixed = lax.fori_loop(
        0, local_pages // chunk, mix_chunk,
        (jnp.zeros((1, 2 * wide), F32), jnp.zeros((2 * wide, features), F32)))
    own_top, own_total, own_mix = [], [], []
    for r in range(requests):
        top_r = top[:, r * wide : (r + 1) * wide]
        weights = jnp.exp(tree_scores[r] - top_r).astype(BF16)
        own_top.append(top_r)
        own_total.append(
            total[:, r * wide : (r + 1) * wide] + jnp.sum(weights.astype(F32), axis=0, keepdims=True))
        mix_r = mixed[r * wide : (r + 1) * wide] + mm_tn(weights, nv_ref[r * tree : (r + 1) * tree, :])
        own_mix.append(gather_heads(mix_r))

    pool_copies[2].wait()
    pool_copies[3].wait()
    stat_row = iota((4, 128), 0)
    held_row = iota((page_rows, wide), 0)

    def serve_one(k):
        asker = lax.rem(me - k + fs, fs)
        page = serve_ref[asker]
        limit = mrecv[k]
        limit = jnp.concatenate([limit, limit], axis=1)
        scores = mm_nt(kbuf[page], spread(qrecv[k]))
        scores = jnp.where(held_row < limit.astype(jnp.int32), scores, NEGATIVE)
        best = jnp.max(scores, axis=0, keepdims=True)
        weights = jnp.exp(scores - best).astype(BF16)
        amount = jnp.sum(weights.astype(F32), axis=0, keepdims=True)
        osend[k] = gather_heads(mm_tn(weights, vbuf[page])).astype(BF16)
        tsend[k] = jnp.where(
            stat_row == 0, best[:, 0:128],
            jnp.where(stat_row == 1, best[:, 128:256],
                      jnp.where(stat_row == 2, amount[:, 0:128], amount[:, 128:256])))

    group = 4

    def serve_group(first):
        base = first * group
        for i in range(group):
            k = base + i

            @pl.when(k > 0)
            def _():
                q_copy(k, me).wait_recv()
                m_copy(k, me).wait_recv()

        for i in range(group):
            serve_one(base + i)
        for i in range(group):
            k = base + i

            @pl.when(k > 0)
            def _():
                to = lax.rem(me - k + fs, fs)
                o_copy(k, to).start()
                t_copy(k, to).start()

    def serve_step(first, carry):
        serve_group(first)
        return carry

    lax.fori_loop(0, fs // group, serve_step, 0)
    orecv[0] = osend[0]
    trecv[0] = tsend[0]

    def await_stats(k, carry):
        t_copy(k, me).wait_recv()
        return carry

    lax.fori_loop(1, fs, await_stats, 0)

    pick = rq_scr[:, 0:128]
    weight_any = [jnp.zeros((fs, 128), F32), jnp.zeros((fs, 128), F32)]
    own_weight = []
    for r in range(requests):
        chosen = pick if r == 1 else 1.0 - pick
        shares = []
        for hh in range(2):
            best = jnp.where(chosen > 0.5, trecv[:, hh, :], NEGATIVE)
            amount = trecv[:, 2 + hh, :]
            mine = own_top[r][:, hh * 128 : (hh + 1) * 128]
            highest = jnp.maximum(jnp.max(best, axis=0, keepdims=True), mine)
            weights = jnp.exp(best - highest) * chosen
            own = jnp.exp(mine - highest)
            bottom = jnp.sum(weights * amount, axis=0, keepdims=True) + (
                own * own_total[r][:, hh * 128 : (hh + 1) * 128])
            weight_any[hh] = weight_any[hh] + weights / bottom
            shares.append(own / bottom)
        own_weight.append(shares)
    for hh in range(2):
        sheet = jnp.concatenate(
            [weight_any[hh]]
            + [jnp.broadcast_to(own_weight[r][hh], (8, 128)) for r in range(requests)]
            + [jnp.zeros((128 - fs - 8 * requests, 128), F32)], axis=0)
        wt_scr[hh * 128 : (hh + 1) * 128, :] = sheet.T

    def factor(col):
        out = wt_scr[0:tree, col : col + 1] * head_masks[0]
        for h in range(1, heads):
            out = out + wt_scr[h * tree : (h + 1) * tree, col : col + 1] * head_masks[h]
        return out

    def await_parts(k, carry):
        o_copy(k, me).wait_recv()
        return carry

    lax.fori_loop(1, fs, await_parts, 0)
    merged = [own_mix[r] * factor(fs + 8 * r) for r in range(requests)]
    for k in range(fs):
        part = orecv[k].astype(F32) * factor(k)
        pick_row = rq_scr[k : k + 1, :]
        merged[0] = merged[0] + part * (1.0 - pick_row)
        merged[1] = merged[1] + part * pick_row
    attended = jnp.concatenate(merged, axis=0).astype(BF16)

    side, per_side = vs // 2, owners // 2

    def owns(v):
        return lax.rem(v, side) < per_side

    def share(v):
        return v // side * per_side + lax.rem(v, side)

    own = share(ve)
    per_owner = resid_ref.shape[1]
    tile = 256
    for c in range(width // tile):
        block = mm(attended, ow_ref[:, c * tile : (c + 1) * tile])
        for o in range(owners):
            piece = block[o * per_owner : (o + 1) * per_owner]
            pown[o, :, c * tile : (c + 1) * tile] = piece
            psend[o, :, c * tile : (c + 1) * tile] = piece.astype(BF16)

    def p_copy(k, to):
        return pltpu.make_async_remote_copy(
            src_ref=psend.at[share(to)], dst_ref=precv.at[k], send_sem=p_sem.at[0, k], recv_sem=p_sem.at[1, k],
            device_id={"vocab": to}, device_id_type=MESH)

    def n_copy(k, owner, to):
        return pltpu.make_async_remote_copy(
            src_ref=normed_ref.at[owner], dst_ref=normed_ref.at[owner],
            send_sem=n_sem.at[0, k], recv_sem=n_sem.at[1, k],
            device_id={"vocab": to}, device_id_type=MESH)

    def h_copy(k, owner, to):
        return pltpu.make_async_remote_copy(
            src_ref=hsend.at[to], dst_ref=cols_ref.at[owner], send_sem=h_sem.at[0, k], recv_sem=h_sem.at[1, k],
            device_id={"vocab": to}, device_id_type=MESH)

    for k in range(1, vs):
        to = lax.rem(ve + k, vs)

        @pl.when(owns(to))
        def _():
            p_copy(k, to).start()

    for far, onward in zip(far_copies, pass_copies):
        far.wait_recv()
        onward.start()

    @pl.when(owns(ve))
    def _():
        hidden = resid_ref[own].astype(F32) + pown[own]
        for k in range(1, vs):
            p_copy(k, ve).wait_recv()
            hidden = hidden + precv[k].astype(F32)
        mean = jnp.mean(hidden * hidden, axis=-1, keepdims=True)
        normed_ref[own] = (hidden * lax.rsqrt(mean + EPSILON) * gain_ref[...].reshape(1, width)).astype(BF16)
        for k in range(1, vs):
            n_copy(k, own, lax.rem(ve + k, vs)).start()
        columns = width // vs
        padded = hsend.shape[2]
        for v in range(vs):
            turned = hidden if v == 0 else pltpu.roll(hidden, width - v * columns, 1)
            hsend[v] = turned[:, 0:padded]
        for k in range(1, vs):
            h_copy(k, own, lax.rem(ve + k, vs)).start()
        cols_ref[own] = hsend[ve]

    for k in range(1, vs):
        owner = lax.rem(ve - k + vs, vs)

        @pl.when(owns(owner))
        def _():
            n_copy(k, share(owner), ve).wait_recv()
            h_copy(k, share(owner), ve).wait_recv()

    def await_sends(k, carry):
        q_copy(k, me).wait_send()
        m_copy(k, me).wait_send()
        o_copy(k, me).wait_send()
        t_copy(k, me).wait_send()
        return carry

    lax.fori_loop(1, fs, await_sends, 0)
    for k in range(1, vs):
        to = lax.rem(ve + k, vs)

        @pl.when(owns(to))
        def _():
            p_copy(k, to).wait_send()

    @pl.when(owns(ve))
    def _():
        for k in range(1, vs):
            to = lax.rem(ve + k, vs)
            n_copy(k, own, to).wait_send()
            h_copy(k, own, to).wait_send()

    for copy in far_copies:
        copy.wait_send()
    for copy in near_copies + pass_copies:
        copy.wait()


def expert_kernel(
    fs, vs, zs,
    normed_ref, cols_ref, routes_ref, router_ref, wg_ref, wu_ref, wd_ref, more_ref,
    out_ref,
    wraw, weights, rt_scr, xbuf, obuf, sbuf, rbuf, fsend, frecv,
    w_sem, d_sem, ag_sem, rs_sem, f_sem,
):
    tokens, width = normed_ref.shape
    block = xbuf.shape[1] // 2
    cut = xbuf.shape[2]
    slots = fsend.shape[1]
    kinds, sources = 3, wraw.shape[0] // 3
    hidden = wraw.shape[1]
    pitch = weights.shape[1]
    me = lax.axis_index("fsdp")
    ve = lax.axis_index("vocab")
    core = lax.rem(me, 2)
    z = lax.rem(me // 2, zs)
    yhi = me // (2 * zs)
    right = (yhi * zs + lax.rem(z + 1, zs)) * 2 + core
    left = (yhi * zs + lax.rem(z + zs - 1, zs)) * 2 + core
    twin = me + 1 - 2 * core
    across = lax.rem(me + fs // 2, fs)

    barrier = pltpu.get_barrier_semaphore()
    for peer in (left, right, twin, across):
        pl.semaphore_signal(barrier, inc=1, device_id={"fsdp": peer}, device_id_type=MESH)
    for k in range(1, vs):
        pl.semaphore_signal(barrier, inc=1, device_id={"vocab": lax.rem(ve + k, vs)}, device_id_type=MESH)
    loads = []
    for i, src in enumerate((wg_ref, wu_ref, wd_ref)):
        loads.append(pltpu.make_async_copy(src, wraw.at[i * sources], w_sem.at[i * sources]))
        for j in range(1, sources if i < 2 else 1):
            loads.append(pltpu.make_async_copy(
                more_ref.at[(j - 1) * 2 + i], wraw.at[i * sources + j], w_sem.at[i * sources + j]))
    for load in loads:
        load.start()

    rt_scr[...] = jnp.zeros(rt_scr.shape, F32)
    rt_scr[0:2, 0:tokens] = routes_ref[...].astype(F32)
    columns_of = rt_scr[...].T[0:tokens].astype(jnp.int32)
    lane = iota((tokens, 128), 1)
    first, second = columns_of[:, 0:1], columns_of[:, 1:2]
    hits = jnp.where((first == lane) | (second == lane), 1.0, 0.0)
    below = jnp.where(iota((tokens, tokens), 1) < iota((tokens, tokens), 0), 1.0, 0.0).astype(BF16)
    ranks = mm(below, hits.astype(BF16))
    my_hit = jnp.sum(jnp.where(lane == ve, hits, 0.0), axis=1, keepdims=True)
    my_rank = jnp.sum(jnp.where(lane == ve, ranks, 0.0), axis=1, keepdims=True)
    mine = jnp.where((my_hit > 0.5) & (my_rank == lane.astype(F32)), 1.0, 0.0)

    picked = mm_tn(mine.astype(BF16), normed_ref[...])[0:block]
    xbuf[0] = jnp.concatenate([picked[:, 0:cut], picked[:, cut:width]], axis=0).astype(BF16)
    pl.semaphore_wait(barrier, 4 + vs - 1)

    ways = (right, left)
    steps = zs // 2
    middle = (cut // 128 + 1) // 2 * 128
    spans = (pl.ds(0, middle), pl.ds(middle, cut - middle))

    def halves(step, way):
        return (way,) if step == steps - 1 else (0, 1)

    def gather_copy(way, step, h):
        src = 0 if step == 0 else 2 * step - 1 + way
        dst = zs - 1 if step == steps - 1 else 2 * step + 1 + way
        return pltpu.make_async_remote_copy(
            src_ref=xbuf.at[src, :, spans[h]], dst_ref=xbuf.at[dst, :, spans[h]],
            send_sem=ag_sem.at[0, way, step, h], recv_sem=ag_sem.at[1, way, step, h],
            device_id={"fsdp": ways[way]}, device_id_type=MESH)

    def gather_step(step):
        for h in (0, 1):
            for way in range(2):
                if step > 0:
                    gather_copy(way, step - 1, h).wait_recv()
                if h in halves(step, way):
                    gather_copy(way, step, h).start()

    def expert_up(first_block, count):
        blocks = range(first_block, first_block + count)
        sides = [
            jnp.concatenate([xbuf[b, at : at + block, :].astype(F32) for b in blocks], axis=0)
            for at in (0, block)
        ]
        rows = jnp.concatenate(sides, axis=1).astype(BF16)
        gate = mm_nt(rows, weights[0:sources].reshape(sources * pitch, width))
        lifted = mm_nt(rows, weights[sources : 2 * sources].reshape(sources * pitch, width))
        return (gate / (1.0 + jnp.exp(-gate)) * lifted).astype(BF16)

    def expert_down(acts, first_block, count):
        tile = cut // 3
        for side in range(2):
            for c in range(3):
                down = weights[2 * sources : 3 * sources, :, side * cut + c * tile : side * cut + (c + 1) * tile]
                out = mm(acts, down.reshape(sources * pitch, tile))
                for i in range(count):
                    obuf[first_block + i, side * block : (side + 1) * block, c * tile : (c + 1) * tile] = (
                        out[i * block : (i + 1) * block])

    def down_copy(src, j, to):
        return pltpu.make_async_remote_copy(
            src_ref=src, dst_ref=wraw.at[2 * sources + j], send_sem=d_sem.at[0, j], recv_sem=d_sem.at[1, j],
            device_id={"fsdp": to}, device_id_type=MESH)

    down_far = down_copy(wd_ref, 2, across)
    down_near = down_copy(wd_ref, 1, twin)
    down_pass = down_copy(wraw.at[2 * sources + 2], 3, twin)
    gather_step(0)
    down_far.start()
    down_near.start()
    logits = mm_nt(normed_ref[...], router_ref[...])
    lane8 = iota(logits.shape, 1)
    chosen0 = jnp.sum(jnp.where(lane8 == first, logits, 0.0), axis=1, keepdims=True)
    chosen1 = jnp.sum(jnp.where(lane8 == second, logits, 0.0), axis=1, keepdims=True)
    gate0 = 1.0 / (1.0 + jnp.exp(chosen1 - chosen0))
    gate1 = 1.0 / (1.0 + jnp.exp(chosen0 - chosen1))
    my_gate = jnp.where(first == ve, gate0, jnp.where(second == ve, gate1, 0.0))
    slot_gate = jnp.sum((mine * my_gate).T, axis=1, keepdims=True)[0:block]
    spread_e = jnp.where(iota((128, vs * slots), 0) == iota((128, vs * slots), 1) // slots, 1.0, 0.0).astype(BF16)
    all_hits = mm(hits.astype(BF16), spread_e)
    all_ranks = mm(ranks.astype(BF16), spread_e)
    slot_at = (iota((tokens, vs * slots), 1) % slots).astype(F32)
    back = jnp.where((all_hits > 0.5) & (all_ranks == slot_at), 1.0, 0.0).astype(BF16)

    for load in loads:
        load.wait()

    def settle(i, carry):
        weights[i, pitch - 16 : pitch, :] = jnp.zeros((16, width), BF16)
        weights[i, 0:hidden, :] = wraw[i]
        return carry

    lax.fori_loop(0, 2 * sources, settle, 0)
    for step in range(1, steps):
        gather_step(step)
        if step == 2:
            near_acts = expert_up(0, 5)
    for way in range(2):
        gather_copy(way, steps - 1, way).wait_recv()
    far_acts = expert_up(5, 3)
    down_far.wait_recv()
    down_pass.start()
    down_near.wait_recv()
    down_pass.wait_recv()
    lax.fori_loop(2 * sources, 3 * sources, settle, 0)
    expert_down(far_acts, 5, 3)

    def sum_copy(way, step, h):
        return pltpu.make_async_remote_copy(
            src_ref=sbuf.at[way, step, :, spans[h]], dst_ref=rbuf.at[way, step, :, spans[h]],
            send_sem=rs_sem.at[0, way, step, h], recv_sem=rs_sem.at[1, way, step, h],
            device_id={"fsdp": ways[way]}, device_id_type=MESH)

    for step in range(steps):
        for h in (0, 1):
            at = spans[h]
            for way in range(2):
                if step == 0:
                    if h != way:
                        continue
                    sbuf[way, 0, :, at] = obuf[zs - 1, :, at].astype(BF16)
                else:
                    source = 2 * (steps - step) - way
                    value = obuf[source, :, at]
                    if step > 1 or h == way:
                        sum_copy(way, step - 1, h).wait_recv()
                        value = value + rbuf[way, step - 1, :, at].astype(F32)
                    sbuf[way, step, :, at] = value.astype(BF16)
                sum_copy(way, step, h).start()
        if step == 0:
            expert_down(near_acts, 0, 5)
    for way in range(2):
        for h in (0, 1):
            sum_copy(way, steps - 1, h).wait_recv()
    whole = obuf[0] + rbuf[0, steps - 1].astype(F32) + rbuf[1, steps - 1].astype(F32)
    gated = [whole[side * block : (side + 1) * block] * slot_gate for side in range(2)]

    columns = width // vs
    padded = fsend.shape[2]
    empty = jnp.zeros((slots - block, padded), F32)

    def f_copy(k, to, slot):
        return pltpu.make_async_remote_copy(
            src_ref=fsend.at[to], dst_ref=frecv.at[slot], send_sem=f_sem.at[0, k], recv_sem=f_sem.at[1, k],
            device_id={"vocab": to}, device_id_type=MESH)

    for v in range(vs):
        side, at = divmod(v * columns, cut)
        turned = gated[side] if at == 0 else pltpu.roll(gated[side], cut - at, 1)
        fsend[v] = jnp.concatenate([turned[:, 0:padded], empty], axis=0).astype(BF16)
    for k in range(1, vs):
        f_copy(k, lax.rem(ve + k, vs), ve).start()
    frecv[ve] = fsend[ve]
    for k in range(1, vs):
        f_copy(k, ve, lax.rem(ve - k + vs, vs)).wait_recv()
    mixture = mm(back, frecv[...].reshape(vs * slots, padded))
    out_ref[...] = (cols_ref[...] + mixture)[:, 0:columns].astype(BF16)

    for copy in (down_far, down_near, down_pass):
        copy.wait_send()
    for step in range(steps):
        for way in range(2):
            for h in halves(step, way):
                gather_copy(way, step, h).wait_send()
    for step in range(steps):
        for way in range(2):
            for h in (0, 1):
                if step > 0 or h == way:
                    sum_copy(way, step, h).wait_send()
    for k in range(1, vs):
        f_copy(k, lax.rem(ve + k, vs), ve).wait_send()


def per_device(
    resid, queries, new_keys, new_values, pool_keys, pool_values, page_table, serve_pages, cache_lengths, parents,
    out_weight, norm_gain, router, routes, gate_weight, up_weight, down_weight,
):
    fs, vs = lax.axis_size("fsdp"), lax.axis_size("vocab")
    zs = fs // 4
    tokens, width = resid.shape
    features = queries.shape[1]
    tree = parents.shape[1]
    pool_pages, page_rows, _ = pool_keys.shape
    hidden = gate_weight.shape[2]
    pitch = -(-hidden // 64) * 64
    vmem = pl.BlockSpec(memory_space=pltpu.VMEM)
    smem = pl.BlockSpec(memory_space=pltpu.SMEM)
    hbm = pl.BlockSpec(memory_space=pl.ANY)
    dma = pltpu.SemaphoreType.DMA
    padded = -(-(width // vs) // 128) * 128
    per_owner = 16
    owners = tokens // per_owner
    wg, wu, wd = gate_weight[0].T, up_weight[0].T, down_weight[0]
    normed, cols, more = pl.pallas_call(
        functools.partial(attention_kernel, fs, vs),
        out_shape=(
            jax.ShapeDtypeStruct((owners, per_owner, width), BF16),
            jax.ShapeDtypeStruct((owners, per_owner, padded), F32),
            jax.ShapeDtypeStruct((6, hidden, width), BF16)),
        in_specs=[vmem] * 4 + [smem] * 2 + [vmem] * 4 + [hbm] * 4,
        out_specs=(vmem, vmem, hbm),
        scratch_shapes=[
            pltpu.VMEM(pool_keys.shape, BF16),
            pltpu.VMEM(pool_values.shape, BF16),
            pltpu.VMEM((pool_pages // 2, page_rows, 512), F32),
            pltpu.VMEM((pool_pages // 2, 512), jnp.int32),
            pltpu.VMEM((fs, features), F32),
            pltpu.VMEM((256, 128), F32),
            pltpu.VMEM((fs, tree, features), BF16),
            pltpu.VMEM((fs, tree, features), BF16),
            pltpu.VMEM((fs, 1, 128), F32),
            pltpu.VMEM((fs, 1, 128), F32),
            pltpu.VMEM((fs, tree, features), BF16),
            pltpu.VMEM((fs, tree, features), BF16),
            pltpu.VMEM((fs, 4, 128), F32),
            pltpu.VMEM((fs, 4, 128), F32),
            pltpu.VMEM((owners, per_owner, width), F32),
            pltpu.VMEM((owners, per_owner, width), BF16),
            pltpu.VMEM((vs, per_owner, width), BF16),
            pltpu.VMEM((vs, per_owner, padded), F32),
            dma((4,)), dma((2, 6)), dma((2, fs)), dma((2, fs)), dma((2, fs)), dma((2, fs)),
            dma((2, vs)), dma((2, vs)), dma((2, vs)),
        ],
        compiler_params=pltpu.CompilerParams(
            collective_id=1, has_side_effects=True, vmem_limit_bytes=56 * 2**20),
        name="attention",
    )(
        queries, new_keys, new_values, page_table, cache_lengths, serve_pages.reshape(-1), parents,
        resid.reshape(owners, per_owner, width), out_weight, norm_gain,
        pool_keys, pool_values, wg, wu)
    block, slots = 40, 48
    return pl.pallas_call(
        functools.partial(expert_kernel, fs, vs, zs),
        out_shape=jax.ShapeDtypeStruct((tokens, width // vs), BF16),
        in_specs=[vmem] * 4 + [hbm] * 4,
        out_specs=vmem,
        scratch_shapes=[
            pltpu.VMEM((12, hidden, width), BF16),
            pltpu.VMEM((12, pitch, width), BF16),
            pltpu.VMEM((128, 128), F32),
            pltpu.VMEM((zs, 2 * block, width // 2), BF16),
            pltpu.VMEM((zs, 2 * block, width // 2), F32),
            pltpu.VMEM((2, zs // 2, 2 * block, width // 2), BF16),
            pltpu.VMEM((2, zs // 2, 2 * block, width // 2), BF16),
            pltpu.VMEM((vs, slots, padded), BF16),
            pltpu.VMEM((vs, slots, padded), BF16),
            dma((12,)), dma((2, 4)), dma((2, 2, zs // 2, 2)), dma((2, 2, zs // 2, 2)), dma((2, vs)),
        ],
        compiler_params=pltpu.CompilerParams(
            collective_id=2, has_side_effects=True, vmem_limit_bytes=56 * 2**20),
        name="experts",
    )(normed.reshape(tokens, width), cols.reshape(tokens, padded), routes.T, router.T, wg, wu, wd, more)


def solution(mesh):
    in_specs = (
        P("fsdp", None), P("fsdp", "vocab"), P("fsdp", "vocab"), P("fsdp", "vocab"),
        P("fsdp", None, "vocab"), P("fsdp", None, "vocab"), P("fsdp", None), P("fsdp", None, None),
        P("fsdp"), P("fsdp", None), P("vocab", None), P(), P(), P("fsdp", None),
        P("vocab", None, "fsdp"), P("vocab", None, "fsdp"), P("vocab", "fsdp", None),
    )
    return jax.shard_map(
        per_device, mesh=mesh, in_specs=in_specs, out_specs=P("fsdp", "vocab"), check_vma=False
    )
```

```python
import functools

import jax
import jax.numpy as jnp
from jax import lax
from jax.experimental import pallas as pl
from jax.experimental.pallas import tpu as pltpu
from jax.sharding import PartitionSpec as P

HEAD_DIM = 64
CAPACITY = 36
NEGATIVE = -1e30
EPSILON = 1e-05
MESH = pl.DeviceIdType.MESH
F32 = jnp.float32
BF16 = jnp.bfloat16


def mm(a, b):
    return jnp.dot(a, b, preferred_element_type=F32)


def mm_nt(a, b):
    return lax.dot_general(a, b, (((1,), (1,)), ((), ())), preferred_element_type=F32)


def mm_tn(a, b):
    return lax.dot_general(a, b, (((0,), (0,)), ((), ())), preferred_element_type=F32)


def iota(shape, dim):
    return lax.broadcasted_iota(jnp.int32, shape, dim)


def attention_kernel(
    fs, vs, zs,
    q_ref, nk_ref, nv_ref, table_ref, length_ref, serve_ref, parent_ref, resid_ref, ow_ref, gain_ref,
    pk_ref, pv_ref, wg_ref, wu_ref,
    normed_ref, cols_ref, more_ref,
    kbuf, vbuf, s_scr, lim_scr, rq_scr, wt_scr, qall, msend, mrecv, osend, orecv, tsend, trecv,
    pown, psend, precv, hsend,
    local_sem, w_sem, q_sem, y_sem, r_sem, c_sem, m_sem, o_sem, t_sem, p_sem, n_sem, h_sem,
):
    requests, pages_each = table_ref.shape
    tree = parent_ref.shape[1]
    features = q_ref.shape[1]
    heads = features // HEAD_DIM
    page_rows = pk_ref.shape[1]
    local_pages = pk_ref.shape[0] // 2
    pool_pages = pk_ref.shape[0]
    rows = heads * tree
    wide = 256
    width = ow_ref.shape[1]
    owners = resid_ref.shape[0]
    me = lax.axis_index("fsdp")
    ve = lax.axis_index("vocab")
    twin = me + 1 - 2 * lax.rem(me, 2)
    across = lax.rem(me + fs // 2, fs)
    core = lax.rem(me, 2)
    z = lax.rem(me // 2, zs)
    yhi = me // (2 * zs)
    right = (yhi * zs + lax.rem(z + 1, zs)) * 2 + core
    left = (yhi * zs + lax.rem(z + zs - 1, zs)) * 2 + core

    def device_at(slot):
        step = slot // 4
        odd = step % 2
        dz = (step // 2) * (1 - odd) - ((step + 1) // 2) * odd
        return (((yhi + (slot // 2) % 2) % 2) * zs + (z + dz + zs) % zs) * 2 + (core + slot % 2) % 2

    def mirrored(slot):
        step = slot // 4
        turned = jnp.minimum(jnp.maximum(step - 1 + 2 * (step % 2), 0), zs - 1)
        return 4 * turned + slot % 4

    barrier = pltpu.get_barrier_semaphore()

    def hail_fsdp(k, carry):
        pl.semaphore_signal(barrier, inc=1, device_id={"fsdp": lax.rem(me + k, fs)}, device_id_type=MESH)
        return carry

    def hail_vocab(k, carry):
        pl.semaphore_signal(barrier, inc=1, device_id={"vocab": lax.rem(ve + k, vs)}, device_id_type=MESH)
        return carry

    lax.fori_loop(1, fs, hail_fsdp, 0)
    lax.fori_loop(1, vs, hail_vocab, 0)
    half = local_pages
    pool_copies = [
        pltpu.make_async_copy(src.at[pl.ds(at, half)], dst.at[pl.ds(at, half)], local_sem.at[i])
        for i, (src, dst, at) in enumerate(
            ((pk_ref, kbuf, half), (pv_ref, vbuf, half), (pk_ref, kbuf, 0), (pv_ref, vbuf, 0))
        )
    ]
    for copy in pool_copies:
        copy.start()

    lane = iota((local_pages, pages_each), 1)
    sub = iota((local_pages, pages_each), 0)
    counts = [jnp.clip(length_ref[r] - page_rows * lane, 0, page_rows) for r in range(requests)]

    def lookup(target):
        hits = [table_ref[r : r + 1, :] == target for r in range(requests)]
        seen = [jnp.sum(jnp.where(h, c, 0).astype(F32), axis=1, keepdims=True) for h, c in zip(hits, counts)]
        return seen, jnp.sum(jnp.where(hits[1], 1.0, 0.0), axis=1, keepdims=True)

    (seen0, seen1), _ = lookup(sub)
    lane_w = iota((local_pages, 2 * wide), 1)
    lim_scr[...] = jnp.where(lane_w < wide, seen0, seen1).astype(jnp.int32)
    (far0, far1), far_rq = lookup(device_at(sub) + pool_pages)
    rq_scr[...] = jnp.broadcast_to(far_rq, rq_scr.shape)
    msend[...] = jnp.where(iota(msend.shape, 1) == 0, (far0 + far1)[:, :, None], far_rq[:, :, None])
    qall[0] = q_ref[...]

    pl.semaphore_wait(barrier, fs - 1 + vs - 1)

    def q_copy(src, dst, send_sem, to):
        return pltpu.make_async_remote_copy(
            src_ref=qall.at[src], dst_ref=qall.at[dst], send_sem=send_sem, recv_sem=q_sem.at[dst],
            device_id={"fsdp": to}, device_id_type=MESH)

    y_copy = q_copy(0, 2, y_sem.at[0], across)
    last = zs // 2 - 1

    def ring_copy(way, step, dy):
        src = 0 if step == 0 else 2 * step - 1 + way
        dst = zs - 1 if step == last else 2 * step + 1 + way
        return q_copy(4 * src + 2 * dy, 4 * dst + 2 * dy, r_sem.at[way, step, dy], (right, left)[way])

    def twin_copy(slot):
        return q_copy(slot, slot + 1, c_sem.at[slot // 2], twin)

    def arrived(slot):
        q_copy(slot, slot, y_sem.at[0], me).wait_recv()

    def ring_step(step, dy):
        for way in range(2):
            if step > 0:
                arrived(4 * (2 * step - 1 + way) + 2 * dy)
            if step < last or way == dy:
                ring_copy(way, step, dy).start()
            if step > 0:
                twin_copy(4 * (2 * step - 1 + way) + 2 * dy).start()

    def parts_copy(send, recv, sem, src, dst, to):
        return pltpu.make_async_remote_copy(
            src_ref=send.at[src], dst_ref=recv.at[dst], send_sem=sem.at[0, src], recv_sem=sem.at[1, dst],
            device_id={"fsdp": to}, device_id_type=MESH)

    def m_copy(src, dst, to):
        return parts_copy(msend, mrecv, m_sem, src, dst, to)

    def o_copy(src, dst, to):
        return parts_copy(osend, orecv, o_sem, src, dst, to)

    def t_copy(src, dst, to):
        return parts_copy(tsend, trecv, t_sem, src, dst, to)

    y_copy.start()
    ring_step(0, 0)
    twin_copy(0).start()

    def send_limits(k, carry):
        m_copy(k, mirrored(k), device_at(k)).start()
        return carry

    lax.fori_loop(1, fs, send_limits, 0)
    mrecv[0] = msend[0]
    arrived(2)
    ring_step(0, 1)
    twin_copy(2).start()

    kinds = (wg_ref, wu_ref)

    def weight_copy(src, at, to):
        return pltpu.make_async_remote_copy(
            src_ref=src, dst_ref=more_ref.at[at], send_sem=w_sem.at[0, at], recv_sem=w_sem.at[1, at],
            device_id={"fsdp": to}, device_id_type=MESH)

    far_copies = [weight_copy(src, 2 + i, across) for i, src in enumerate(kinds)]
    near_copies = [weight_copy(src, i, twin) for i, src in enumerate(kinds)]
    for copy in far_copies[:1] + near_copies:
        copy.start()

    head_of = iota((1, features), 1) // HEAD_DIM
    head_masks = [jnp.where(head_of == h, 1.0, 0.0) for h in range(heads)]
    scaled_masks = [(m * HEAD_DIM**-0.5).astype(BF16) for m in head_masks]

    def spread(q):
        parts = [q * m for m in scaled_masks]
        return jnp.concatenate(parts + [jnp.zeros((wide - rows, features), BF16)], axis=0)

    def gather_heads(o):
        total = o[0:tree] * head_masks[0]
        for h in range(1, heads):
            total = total + o[h * tree : (h + 1) * tree] * head_masks[h]
        return total

    spread_q = [spread(q_ref[r * tree : (r + 1) * tree, :]) for r in range(requests)]
    both_q = jnp.concatenate(spread_q, axis=0)

    for copy in pool_copies:
        copy.wait()
    stat_row = iota((4, 128), 0)
    held_row = iota((page_rows, wide), 0)

    def serve_one(k):
        page = serve_ref[device_at(k)]
        told = mrecv[k]
        told = jnp.concatenate([told, told], axis=1)
        limit, pick = told[0:1], told[1:2]
        asked = qall[k].astype(F32)
        query = (asked[0:tree] * (1.0 - pick) + asked[tree : 2 * tree] * pick).astype(BF16)
        scores = mm_nt(kbuf[page], spread(query))
        scores = jnp.where(held_row < limit.astype(jnp.int32), scores, NEGATIVE)
        best = jnp.max(scores, axis=0, keepdims=True)
        weights = jnp.exp(scores - best).astype(BF16)
        amount = jnp.sum(weights.astype(F32), axis=0, keepdims=True)
        osend[k] = gather_heads(mm_tn(weights, vbuf[page])).astype(BF16)
        tsend[k] = jnp.where(
            stat_row == 0, best[:, 0:128],
            jnp.where(stat_row == 1, best[:, 128:256],
                      jnp.where(stat_row == 2, amount[:, 0:128], amount[:, 128:256])))

    group = 4

    def serve_step(step, carry):
        for i in range(group):
            k = step * group + i

            @pl.when(k > 0)
            def _():
                m_copy(k, k, me).wait_recv()

            if i % 2 == 1:
                arrived(k)
        for i in range(group):
            serve_one(step * group + i)
        for i in range(group):
            k = step * group + i

            @pl.when(k > 0)
            def _():
                o_copy(k, mirrored(k), device_at(k)).start()
                t_copy(k, mirrored(k), device_at(k)).start()

        return carry

    for step in range(1, last + 1):
        for dy in range(2):
            ring_step(step, dy)
        lax.fori_loop(max(0, 2 * step - 3), 2 * step - 1, serve_step, 0)
    for dy in range(2):
        arrived(4 * (zs - 1) + 2 * dy)
        twin_copy(4 * (zs - 1) + 2 * dy).start()
    lax.fori_loop(2 * last - 1, zs, serve_step, 0)
    far_copies[1].start()

    eye = jnp.where(iota((tree, tree), 0) == iota((tree, tree), 1), 1.0, 0.0)
    tile_heads = jnp.where(
        (iota((tree, wide), 1) % tree == iota((tree, wide), 0)) & (iota((tree, wide), 1) < rows), 1.0, 0.0
    ).astype(BF16)
    tree_scores = []
    for r in range(requests):
        linked = jnp.where(parent_ref[r : r + 1, :] == iota((tree, tree), 0), 1.0, 0.0)
        reach = jnp.minimum(linked + eye, 1.0)
        for _ in range(tree.bit_length()):
            half_reach = reach.astype(BF16)
            reach = jnp.minimum(mm(half_reach, half_reach), 1.0)
        seen = mm(reach.astype(BF16), tile_heads)
        scores = mm_nt(nk_ref[r * tree : (r + 1) * tree, :], spread_q[r])
        tree_scores.append(jnp.where(seen > 0.5, scores, NEGATIVE))
    top = jnp.concatenate([jnp.max(s, axis=0, keepdims=True) for s in tree_scores], axis=1)

    key_row = iota((page_rows, 2 * wide), 0)
    chunk = 4

    def score_chunk(c, top):
        for i in range(chunk):
            page = c * chunk + i
            scores = mm_nt(kbuf[page], both_q)
            scores = jnp.where(key_row < lim_scr[pl.ds(page, 1), :], scores, NEGATIVE)
            s_scr[page] = scores
            top = jnp.maximum(top, jnp.max(scores, axis=0, keepdims=True))
        return top

    chunks = local_pages // chunk
    top = lax.fori_loop(0, chunks, score_chunk, top)

    def mix_chunk(c, carry):
        total, mixed = carry
        at = pl.ds(c * chunk, chunk)
        weights = jnp.exp(s_scr[at].reshape(chunk * page_rows, 2 * wide) - top).astype(BF16)
        total = total + jnp.sum(weights.astype(F32), axis=0, keepdims=True)
        values = vbuf[at].reshape(chunk * page_rows, features)
        return total, mixed + mm_tn(weights, values)

    total, mixed = lax.fori_loop(
        0, chunks, mix_chunk,
        (jnp.zeros((1, 2 * wide), F32), jnp.zeros((2 * wide, features), F32)))
    own_top, own_total, own_mix = [], [], []
    for r in range(requests):
        top_r = top[:, r * wide : (r + 1) * wide]
        weights = jnp.exp(tree_scores[r] - top_r).astype(BF16)
        own_top.append(top_r)
        own_total.append(
            total[:, r * wide : (r + 1) * wide] + jnp.sum(weights.astype(F32), axis=0, keepdims=True))
        mix_r = mixed[r * wide : (r + 1) * wide] + mm_tn(weights, nv_ref[r * tree : (r + 1) * tree, :])
        own_mix.append(gather_heads(mix_r))

    orecv[0] = osend[0]
    trecv[0] = tsend[0]

    def await_stats(k, carry):
        t_copy(k, k, me).wait_recv()
        return carry

    lax.fori_loop(1, fs, await_stats, 0)

    pick = rq_scr[:, 0:128]
    weight_any = [jnp.zeros((fs, 128), F32), jnp.zeros((fs, 128), F32)]
    own_weight = []
    for r in range(requests):
        chosen = pick if r == 1 else 1.0 - pick
        shares = []
        for hh in range(2):
            best = jnp.where(chosen > 0.5, trecv[:, hh, :], NEGATIVE)
            amount = trecv[:, 2 + hh, :]
            mine = own_top[r][:, hh * 128 : (hh + 1) * 128]
            highest = jnp.maximum(jnp.max(best, axis=0, keepdims=True), mine)
            weights = jnp.exp(best - highest) * chosen
            own = jnp.exp(mine - highest)
            bottom = jnp.sum(weights * amount, axis=0, keepdims=True) + (
                own * own_total[r][:, hh * 128 : (hh + 1) * 128])
            weight_any[hh] = weight_any[hh] + weights / bottom
            shares.append(own / bottom)
        own_weight.append(shares)
    for hh in range(2):
        sheet = jnp.concatenate(
            [weight_any[hh]]
            + [jnp.broadcast_to(own_weight[r][hh], (8, 128)) for r in range(requests)]
            + [jnp.zeros((128 - fs - 8 * requests, 128), F32)], axis=0)
        wt_scr[hh * 128 : (hh + 1) * 128, :] = sheet.T

    def factor(col):
        out = wt_scr[0:tree, col : col + 1] * head_masks[0]
        for h in range(1, heads):
            out = out + wt_scr[h * tree : (h + 1) * tree, col : col + 1] * head_masks[h]
        return out

    def await_parts(k, carry):
        o_copy(k, k, me).wait_recv()
        return carry

    lax.fori_loop(1, fs, await_parts, 0)
    merged = [own_mix[r] * factor(fs + 8 * r) for r in range(requests)]
    for k in range(fs):
        part = orecv[k].astype(F32) * factor(k)
        pick_row = rq_scr[k : k + 1, :]
        merged[0] = merged[0] + part * (1.0 - pick_row)
        merged[1] = merged[1] + part * pick_row
    attended = jnp.concatenate(merged, axis=0).astype(BF16)

    side, per_side = vs // 2, owners // 2

    def owns(v):
        return lax.rem(v, side) < per_side

    def share(v):
        return v // side * per_side + lax.rem(v, side)

    own = share(ve)
    per_owner = resid_ref.shape[1]
    tile = 256
    for c in range(width // tile):
        block = mm(attended, ow_ref[:, c * tile : (c + 1) * tile])
        for o in range(owners):
            piece = block[o * per_owner : (o + 1) * per_owner]
            pown[o, :, c * tile : (c + 1) * tile] = piece
            psend[o, :, c * tile : (c + 1) * tile] = piece.astype(BF16)

    def p_copy(k, to):
        return pltpu.make_async_remote_copy(
            src_ref=psend.at[share(to)], dst_ref=precv.at[k], send_sem=p_sem.at[0, k], recv_sem=p_sem.at[1, k],
            device_id={"vocab": to}, device_id_type=MESH)

    def n_copy(k, owner, to):
        return pltpu.make_async_remote_copy(
            src_ref=normed_ref.at[owner], dst_ref=normed_ref.at[owner],
            send_sem=n_sem.at[0, k], recv_sem=n_sem.at[1, k],
            device_id={"vocab": to}, device_id_type=MESH)

    def h_copy(k, owner, to):
        return pltpu.make_async_remote_copy(
            src_ref=hsend.at[to], dst_ref=cols_ref.at[owner], send_sem=h_sem.at[0, k], recv_sem=h_sem.at[1, k],
            device_id={"vocab": to}, device_id_type=MESH)

    for k in range(1, vs):
        to = lax.rem(ve + k, vs)

        @pl.when(owns(to))
        def _():
            p_copy(k, to).start()

    @pl.when(owns(ve))
    def _():
        hidden = resid_ref[own].astype(F32) + pown[own]
        for k in range(1, vs):
            p_copy(k, ve).wait_recv()
            hidden = hidden + precv[k].astype(F32)
        mean = jnp.mean(hidden * hidden, axis=-1, keepdims=True)
        normed_ref[own] = (hidden * lax.rsqrt(mean + EPSILON) * gain_ref[...].reshape(1, width)).astype(BF16)
        for k in range(1, vs):
            n_copy(k, own, lax.rem(ve + k, vs)).start()
        columns = width // vs
        padded = hsend.shape[2]
        for v in range(vs):
            turned = hidden if v == 0 else pltpu.roll(hidden, width - v * columns, 1)
            hsend[v] = turned[:, 0:padded]
        for k in range(1, vs):
            h_copy(k, own, lax.rem(ve + k, vs)).start()
        cols_ref[own] = hsend[ve]

    for k in range(1, vs):
        owner = lax.rem(ve - k + vs, vs)

        @pl.when(owns(owner))
        def _():
            n_copy(k, share(owner), ve).wait_recv()
            h_copy(k, share(owner), ve).wait_recv()

    def await_sends(k, carry):
        m_copy(k, k, me).wait_send()
        o_copy(k, k, me).wait_send()
        t_copy(k, k, me).wait_send()
        return carry

    lax.fori_loop(1, fs, await_sends, 0)
    y_copy.wait_send()
    for step in range(zs):
        for dy in range(2):
            twin_copy(4 * step + 2 * dy).wait_send()
    for step in range(last + 1):
        for way in range(2):
            for dy in range(2):
                if step < last or way == dy:
                    ring_copy(way, step, dy).wait_send()
    for k in range(1, vs):
        to = lax.rem(ve + k, vs)

        @pl.when(owns(to))
        def _():
            p_copy(k, to).wait_send()

    @pl.when(owns(ve))
    def _():
        for k in range(1, vs):
            to = lax.rem(ve + k, vs)
            n_copy(k, own, to).wait_send()
            h_copy(k, own, to).wait_send()

    for copy in far_copies + near_copies:
        copy.wait()


def expert_kernel(
    fs, vs, zs,
    normed_ref, cols_ref, routes_ref, router_ref, wg_ref, wu_ref, wd_ref, more_ref,
    out_ref,
    wraw, weights, rt_scr, xbuf, obuf, sbuf, rbuf, fsend, frecv,
    w_sem, d_sem, p_sem, ag_sem, rs_sem, f_sem,
):
    tokens, width = normed_ref.shape
    block = xbuf.shape[1] // 2
    cut = xbuf.shape[2]
    slots = fsend.shape[1]
    kinds, sources = 3, wraw.shape[0] // 3
    hidden = wraw.shape[1]
    pitch = weights.shape[1]
    me = lax.axis_index("fsdp")
    ve = lax.axis_index("vocab")
    core = lax.rem(me, 2)
    z = lax.rem(me // 2, zs)
    yhi = me // (2 * zs)
    right = (yhi * zs + lax.rem(z + 1, zs)) * 2 + core
    left = (yhi * zs + lax.rem(z + zs - 1, zs)) * 2 + core
    twin = me + 1 - 2 * core
    across = lax.rem(me + fs // 2, fs)

    barrier = pltpu.get_barrier_semaphore()
    for peer in (left, right, twin, across):
        pl.semaphore_signal(barrier, inc=1, device_id={"fsdp": peer}, device_id_type=MESH)
    for k in range(1, vs):
        pl.semaphore_signal(barrier, inc=1, device_id={"vocab": lax.rem(ve + k, vs)}, device_id_type=MESH)
    loads = []
    for i, src in enumerate((wg_ref, wu_ref, wd_ref)):
        loads.append(pltpu.make_async_copy(src, wraw.at[i * sources], w_sem.at[i * sources]))
        for j in range(1, sources - 1 if i < 2 else 1):
            loads.append(pltpu.make_async_copy(
                more_ref.at[(j - 1) * 2 + i], wraw.at[i * sources + j], w_sem.at[i * sources + j]))
    for load in loads:
        load.start()

    rt_scr[...] = jnp.zeros(rt_scr.shape, F32)
    rt_scr[0:2, 0:tokens] = routes_ref[...].astype(F32)
    columns_of = rt_scr[...].T[0:tokens].astype(jnp.int32)
    lane = iota((tokens, 128), 1)
    first, second = columns_of[:, 0:1], columns_of[:, 1:2]
    hits = jnp.where((first == lane) | (second == lane), 1.0, 0.0)
    below = jnp.where(iota((tokens, tokens), 1) < iota((tokens, tokens), 0), 1.0, 0.0).astype(BF16)
    ranks = mm(below, hits.astype(BF16))
    my_hit = jnp.sum(jnp.where(lane == ve, hits, 0.0), axis=1, keepdims=True)
    my_rank = jnp.sum(jnp.where(lane == ve, ranks, 0.0), axis=1, keepdims=True)
    mine = jnp.where((my_hit > 0.5) & (my_rank == lane.astype(F32)), 1.0, 0.0)

    picked = mm_tn(mine.astype(BF16), normed_ref[...])[0:block]
    xbuf[0] = jnp.concatenate([picked[:, 0:cut], picked[:, cut:width]], axis=0).astype(BF16)
    pl.semaphore_wait(barrier, 4 + vs - 1)

    ways = (right, left)
    steps = zs // 2
    middle = (cut // 128 + 1) // 2 * 128
    spans = (pl.ds(0, middle), pl.ds(middle, cut - middle))

    def halves(step, way):
        return (way,) if step == steps - 1 else (0, 1)

    def gather_copy(way, step, h):
        src = 0 if step == 0 else 2 * step - 1 + way
        dst = zs - 1 if step == steps - 1 else 2 * step + 1 + way
        return pltpu.make_async_remote_copy(
            src_ref=xbuf.at[src, :, spans[h]], dst_ref=xbuf.at[dst, :, spans[h]],
            send_sem=ag_sem.at[0, way, step, h], recv_sem=ag_sem.at[1, way, step, h],
            device_id={"fsdp": ways[way]}, device_id_type=MESH)

    def gather_step(step):
        for h in (0, 1):
            for way in range(2):
                if step > 0:
                    gather_copy(way, step - 1, h).wait_recv()
                if h in halves(step, way):
                    gather_copy(way, step, h).start()

    def expert_up(first_block, count):
        blocks = range(first_block, first_block + count)
        sides = [
            jnp.concatenate([xbuf[b, at : at + block, :].astype(F32) for b in blocks], axis=0)
            for at in (0, block)
        ]
        rows = jnp.concatenate(sides, axis=1).astype(BF16)
        gate = mm_nt(rows, weights[0:sources].reshape(sources * pitch, width))
        lifted = mm_nt(rows, weights[sources : 2 * sources].reshape(sources * pitch, width))
        return (gate / (1.0 + jnp.exp(-gate)) * lifted).astype(BF16)

    def expert_down(acts, first_block, count):
        tile = cut // 3
        for side in range(2):
            for c in range(3):
                down = weights[2 * sources : 3 * sources, :, side * cut + c * tile : side * cut + (c + 1) * tile]
                out = mm(acts, down.reshape(sources * pitch, tile))
                for i in range(count):
                    obuf[first_block + i, side * block : (side + 1) * block, c * tile : (c + 1) * tile] = (
                        out[i * block : (i + 1) * block])

    def down_copy(src, j, to):
        return pltpu.make_async_remote_copy(
            src_ref=src, dst_ref=wraw.at[2 * sources + j], send_sem=d_sem.at[0, j], recv_sem=d_sem.at[1, j],
            device_id={"fsdp": to}, device_id_type=MESH)

    down_far = down_copy(wd_ref, 2, across)
    down_near = down_copy(wd_ref, 1, twin)
    down_pass = down_copy(wraw.at[2 * sources + 2], 3, twin)
    up_pass = [
        pltpu.make_async_remote_copy(
            src_ref=more_ref.at[2 + i], dst_ref=wraw.at[i * sources + 3],
            send_sem=p_sem.at[0, i], recv_sem=p_sem.at[1, i], device_id={"fsdp": twin}, device_id_type=MESH)
        for i in range(2)
    ]
    gather_step(0)
    for copy in up_pass:
        copy.start()
    down_far.start()
    down_near.start()
    logits = mm_nt(normed_ref[...], router_ref[...])
    lane8 = iota(logits.shape, 1)
    chosen0 = jnp.sum(jnp.where(lane8 == first, logits, 0.0), axis=1, keepdims=True)
    chosen1 = jnp.sum(jnp.where(lane8 == second, logits, 0.0), axis=1, keepdims=True)
    gate0 = 1.0 / (1.0 + jnp.exp(chosen1 - chosen0))
    gate1 = 1.0 / (1.0 + jnp.exp(chosen0 - chosen1))
    my_gate = jnp.where(first == ve, gate0, jnp.where(second == ve, gate1, 0.0))
    slot_gate = jnp.sum((mine * my_gate).T, axis=1, keepdims=True)[0:block]
    spread_e = jnp.where(iota((128, vs * slots), 0) == iota((128, vs * slots), 1) // slots, 1.0, 0.0).astype(BF16)
    all_hits = mm(hits.astype(BF16), spread_e)
    all_ranks = mm(ranks.astype(BF16), spread_e)
    slot_at = (iota((tokens, vs * slots), 1) % slots).astype(F32)
    back = jnp.where((all_hits > 0.5) & (all_ranks == slot_at), 1.0, 0.0).astype(BF16)

    for load in loads:
        load.wait()
    for copy in up_pass:
        copy.wait_recv()

    def settle(i, carry):
        weights[i, pitch - 16 : pitch, :] = jnp.zeros((16, width), BF16)
        weights[i, 0:hidden, :] = wraw[i]
        return carry

    lax.fori_loop(0, 2 * sources, settle, 0)
    for step in range(1, steps):
        gather_step(step)
        if step == 2:
            near_acts = expert_up(0, 5)
    for way in range(2):
        gather_copy(way, steps - 1, way).wait_recv()
    far_acts = expert_up(5, 3)
    down_far.wait_recv()
    down_pass.start()
    down_near.wait_recv()
    down_pass.wait_recv()
    lax.fori_loop(2 * sources, 3 * sources, settle, 0)
    expert_down(far_acts, 5, 3)

    def sum_copy(way, step, h):
        return pltpu.make_async_remote_copy(
            src_ref=sbuf.at[way, step, :, spans[h]], dst_ref=rbuf.at[way, step, :, spans[h]],
            send_sem=rs_sem.at[0, way, step, h], recv_sem=rs_sem.at[1, way, step, h],
            device_id={"fsdp": ways[way]}, device_id_type=MESH)

    for step in range(steps):
        for h in (0, 1):
            at = spans[h]
            for way in range(2):
                if step == 0:
                    if h != way:
                        continue
                    sbuf[way, 0, :, at] = obuf[zs - 1, :, at].astype(BF16)
                else:
                    source = 2 * (steps - step) - way
                    value = obuf[source, :, at]
                    if step > 1 or h == way:
                        sum_copy(way, step - 1, h).wait_recv()
                        value = value + rbuf[way, step - 1, :, at].astype(F32)
                    sbuf[way, step, :, at] = value.astype(BF16)
                sum_copy(way, step, h).start()
        if step == 0:
            expert_down(near_acts, 0, 5)
    for way in range(2):
        for h in (0, 1):
            sum_copy(way, steps - 1, h).wait_recv()
    whole = obuf[0] + rbuf[0, steps - 1].astype(F32) + rbuf[1, steps - 1].astype(F32)
    gated = [whole[side * block : (side + 1) * block] * slot_gate for side in range(2)]

    columns = width // vs
    padded = fsend.shape[2]
    empty = jnp.zeros((slots - block, padded), F32)

    def f_copy(k, to, slot):
        return pltpu.make_async_remote_copy(
            src_ref=fsend.at[to], dst_ref=frecv.at[slot], send_sem=f_sem.at[0, k], recv_sem=f_sem.at[1, k],
            device_id={"vocab": to}, device_id_type=MESH)

    for v in range(vs):
        side, at = divmod(v * columns, cut)
        turned = gated[side] if at == 0 else pltpu.roll(gated[side], cut - at, 1)
        fsend[v] = jnp.concatenate([turned[:, 0:padded], empty], axis=0).astype(BF16)
    for k in range(1, vs):
        f_copy(k, lax.rem(ve + k, vs), ve).start()
    frecv[ve] = fsend[ve]
    for k in range(1, vs):
        f_copy(k, ve, lax.rem(ve - k + vs, vs)).wait_recv()
    mixture = mm(back, frecv[...].reshape(vs * slots, padded))
    out_ref[...] = (cols_ref[...] + mixture)[:, 0:columns].astype(BF16)

    for copy in (down_far, down_near, down_pass, *up_pass):
        copy.wait_send()
    for step in range(steps):
        for way in range(2):
            for h in halves(step, way):
                gather_copy(way, step, h).wait_send()
    for step in range(steps):
        for way in range(2):
            for h in (0, 1):
                if step > 0 or h == way:
                    sum_copy(way, step, h).wait_send()
    for k in range(1, vs):
        f_copy(k, lax.rem(ve + k, vs), ve).wait_send()


def per_device(
    resid, queries, new_keys, new_values, pool_keys, pool_values, page_table, serve_pages, cache_lengths, parents,
    out_weight, norm_gain, router, routes, gate_weight, up_weight, down_weight,
):
    fs, vs = lax.axis_size("fsdp"), lax.axis_size("vocab")
    zs = fs // 4
    tokens, width = resid.shape
    features = queries.shape[1]
    tree = parents.shape[1]
    pool_pages, page_rows, _ = pool_keys.shape
    hidden = gate_weight.shape[2]
    pitch = -(-hidden // 64) * 64
    vmem = pl.BlockSpec(memory_space=pltpu.VMEM)
    smem = pl.BlockSpec(memory_space=pltpu.SMEM)
    hbm = pl.BlockSpec(memory_space=pl.ANY)
    dma = pltpu.SemaphoreType.DMA
    padded = -(-(width // vs) // 128) * 128
    per_owner = 16
    owners = tokens // per_owner
    wg, wu, wd = gate_weight[0].T, up_weight[0].T, down_weight[0]
    normed, cols, more = pl.pallas_call(
        functools.partial(attention_kernel, fs, vs, zs),
        out_shape=(
            jax.ShapeDtypeStruct((owners, per_owner, width), BF16),
            jax.ShapeDtypeStruct((owners, per_owner, padded), F32),
            jax.ShapeDtypeStruct((4, hidden, width), BF16)),
        in_specs=[vmem] * 4 + [smem] * 2 + [vmem] * 4 + [hbm] * 4,
        out_specs=(vmem, vmem, hbm),
        scratch_shapes=[
            pltpu.VMEM(pool_keys.shape, BF16),
            pltpu.VMEM(pool_values.shape, BF16),
            pltpu.VMEM((pool_pages // 2, page_rows, 512), F32),
            pltpu.VMEM((pool_pages // 2, 512), jnp.int32),
            pltpu.VMEM((fs, features), F32),
            pltpu.VMEM((256, 128), F32),
            pltpu.VMEM((fs, 2 * tree, features), BF16),
            pltpu.VMEM((fs, 2, 128), F32),
            pltpu.VMEM((fs, 2, 128), F32),
            pltpu.VMEM((fs, tree, features), BF16),
            pltpu.VMEM((fs, tree, features), BF16),
            pltpu.VMEM((fs, 4, 128), F32),
            pltpu.VMEM((fs, 4, 128), F32),
            pltpu.VMEM((owners, per_owner, width), F32),
            pltpu.VMEM((owners, per_owner, width), BF16),
            pltpu.VMEM((vs, per_owner, width), BF16),
            pltpu.VMEM((vs, per_owner, padded), F32),
            dma((4,)), dma((2, 4)), dma((fs,)), dma((1,)), dma((2, zs // 2, 2)), dma((fs // 2,)),
            dma((2, fs)), dma((2, fs)), dma((2, fs)),
            dma((2, vs)), dma((2, vs)), dma((2, vs)),
        ],
        compiler_params=pltpu.CompilerParams(
            collective_id=1, has_side_effects=True, vmem_limit_bytes=56 * 2**20),
        name="attention",
    )(
        queries, new_keys, new_values, page_table, cache_lengths, serve_pages.reshape(-1), parents,
        resid.reshape(owners, per_owner, width), out_weight, norm_gain,
        pool_keys, pool_values, wg, wu)
    block, slots = 40, 48
    return pl.pallas_call(
        functools.partial(expert_kernel, fs, vs, zs),
        out_shape=jax.ShapeDtypeStruct((tokens, width // vs), BF16),
        in_specs=[vmem] * 4 + [hbm] * 4,
        out_specs=vmem,
        scratch_shapes=[
            pltpu.VMEM((12, hidden, width), BF16),
            pltpu.VMEM((12, pitch, width), BF16),
            pltpu.VMEM((128, 128), F32),
            pltpu.VMEM((zs, 2 * block, width // 2), BF16),
            pltpu.VMEM((zs, 2 * block, width // 2), F32),
            pltpu.VMEM((2, zs // 2, 2 * block, width // 2), BF16),
            pltpu.VMEM((2, zs // 2, 2 * block, width // 2), BF16),
            pltpu.VMEM((vs, slots, padded), BF16),
            pltpu.VMEM((vs, slots, padded), BF16),
            dma((12,)), dma((2, 4)), dma((2, 2)), dma((2, 2, zs // 2, 2)), dma((2, 2, zs // 2, 2)), dma((2, vs)),
        ],
        compiler_params=pltpu.CompilerParams(
            collective_id=2, has_side_effects=True, vmem_limit_bytes=56 * 2**20),
        name="experts",
    )(normed.reshape(tokens, width), cols.reshape(tokens, padded), routes.T, router.T, wg, wu, wd, more)


def solution(mesh):
    in_specs = (
        P("fsdp", None), P("fsdp", "vocab"), P("fsdp", "vocab"), P("fsdp", "vocab"),
        P("fsdp", None, "vocab"), P("fsdp", None, "vocab"), P("fsdp", None), P("fsdp", None, None),
        P("fsdp"), P("fsdp", None), P("vocab", None), P(), P(), P("fsdp", None),
        P("vocab", None, "fsdp"), P("vocab", None, "fsdp"), P("vocab", "fsdp", None),
    )
    return jax.shard_map(
        per_device, mesh=mesh, in_specs=in_specs, out_specs=P("fsdp", "vocab"), check_vma=False
    )
```

```python
import functools

import jax
import jax.numpy as jnp
from jax import lax
from jax.experimental import pallas as pl
from jax.experimental.pallas import tpu as pltpu
from jax.sharding import PartitionSpec as P

HEAD_DIM = 64
CAPACITY = 36
NEGATIVE = -1e30
EPSILON = 1e-05
MESH = pl.DeviceIdType.MESH
F32 = jnp.float32
BF16 = jnp.bfloat16


def mm(a, b):
    return jnp.dot(a, b, preferred_element_type=F32)


def mm_nt(a, b):
    return lax.dot_general(a, b, (((1,), (1,)), ((), ())), preferred_element_type=F32)


def mm_tn(a, b):
    return lax.dot_general(a, b, (((0,), (0,)), ((), ())), preferred_element_type=F32)


def iota(shape, dim):
    return lax.broadcasted_iota(jnp.int32, shape, dim)


def attention_part(
    fs, vs, zs,
    q_ref, nk_ref, nv_ref, table_ref, length_ref, serve_ref, parent_ref, resid_ref, ow_ref, gain_ref,
    pk_ref, pv_ref, wg_ref, wu_ref, wd_ref, wraw,
    normed_ref, cols_ref,
    kbuf, vbuf, s_scr, lim_scr, rq_scr, wt_scr, qall, msend, mrecv, osend, orecv, tsend, trecv,
    pown, psend, precv, hsend,
    local_sem, w_sem, q_sem, y_sem, r_sem, c_sem, m_sem, o_sem, t_sem, p_sem, n_sem, h_sem,
):
    requests, pages_each = table_ref.shape
    tree = parent_ref.shape[1]
    features = q_ref.shape[1]
    heads = features // HEAD_DIM
    page_rows = pk_ref.shape[1]
    local_pages = pk_ref.shape[0] // 2
    pool_pages = pk_ref.shape[0]
    rows = heads * tree
    wide = 256
    width = ow_ref.shape[1]
    owners = resid_ref.shape[0]
    me = lax.axis_index("fsdp")
    ve = lax.axis_index("vocab")
    twin = me + 1 - 2 * lax.rem(me, 2)
    across = lax.rem(me + fs // 2, fs)
    core = lax.rem(me, 2)
    z = lax.rem(me // 2, zs)
    yhi = me // (2 * zs)
    right = (yhi * zs + lax.rem(z + 1, zs)) * 2 + core
    left = (yhi * zs + lax.rem(z + zs - 1, zs)) * 2 + core

    def device_at(slot):
        step = slot // 4
        odd = step % 2
        dz = (step // 2) * (1 - odd) - ((step + 1) // 2) * odd
        return (((yhi + (slot // 2) % 2) % 2) * zs + (z + dz + zs) % zs) * 2 + (core + slot % 2) % 2

    def mirrored(slot):
        step = slot // 4
        turned = jnp.minimum(jnp.maximum(step - 1 + 2 * (step % 2), 0), zs - 1)
        return 4 * turned + slot % 4

    barrier = pltpu.get_barrier_semaphore()

    def hail_fsdp(k, carry):
        pl.semaphore_signal(barrier, inc=1, device_id={"fsdp": lax.rem(me + k, fs)}, device_id_type=MESH)
        return carry

    def hail_vocab(k, carry):
        pl.semaphore_signal(barrier, inc=1, device_id={"vocab": lax.rem(ve + k, vs)}, device_id_type=MESH)
        return carry

    lax.fori_loop(1, fs, hail_fsdp, 0)
    lax.fori_loop(1, vs, hail_vocab, 0)
    half = local_pages
    pool_copies = [
        pltpu.make_async_copy(src.at[pl.ds(at, half)], dst.at[pl.ds(at, half)], local_sem.at[i])
        for i, (src, dst, at) in enumerate(
            ((pk_ref, kbuf, half), (pv_ref, vbuf, half), (pk_ref, kbuf, 0), (pv_ref, vbuf, 0))
        )
    ]
    for copy in pool_copies:
        copy.start()

    lane = iota((local_pages, pages_each), 1)
    sub = iota((local_pages, pages_each), 0)
    counts = [jnp.clip(length_ref[r] - page_rows * lane, 0, page_rows) for r in range(requests)]

    def lookup(target):
        hits = [table_ref[r : r + 1, :] == target for r in range(requests)]
        seen = [jnp.sum(jnp.where(h, c, 0).astype(F32), axis=1, keepdims=True) for h, c in zip(hits, counts)]
        return seen, jnp.sum(jnp.where(hits[1], 1.0, 0.0), axis=1, keepdims=True)

    (seen0, seen1), _ = lookup(sub)
    lane_w = iota((local_pages, 2 * wide), 1)
    lim_scr[...] = jnp.where(lane_w < wide, seen0, seen1).astype(jnp.int32)
    (far0, far1), far_rq = lookup(device_at(sub) + pool_pages)
    rq_scr[...] = jnp.broadcast_to(far_rq, rq_scr.shape)
    msend[...] = jnp.where(iota(msend.shape, 1) == 0, (far0 + far1)[:, :, None], far_rq[:, :, None])
    qall[0] = q_ref[...]

    pl.semaphore_wait(barrier, fs - 1 + vs - 1)

    def q_copy(src, dst, send_sem, to):
        return pltpu.make_async_remote_copy(
            src_ref=qall.at[src], dst_ref=qall.at[dst], send_sem=send_sem, recv_sem=q_sem.at[dst],
            device_id={"fsdp": to}, device_id_type=MESH)

    y_copy = q_copy(0, 2, y_sem.at[0], across)
    last = zs // 2 - 1

    def ring_copy(way, step, dy):
        src = 0 if step == 0 else 2 * step - 1 + way
        dst = zs - 1 if step == last else 2 * step + 1 + way
        return q_copy(4 * src + 2 * dy, 4 * dst + 2 * dy, r_sem.at[way, step, dy], (right, left)[way])

    def twin_copy(slot):
        return q_copy(slot, slot + 1, c_sem.at[slot // 2], twin)

    def arrived(slot):
        q_copy(slot, slot, y_sem.at[0], me).wait_recv()

    def ring_step(step, dy):
        for way in range(2):
            if step > 0:
                arrived(4 * (2 * step - 1 + way) + 2 * dy)
            if step < last or way == dy:
                ring_copy(way, step, dy).start()
            if step > 0:
                twin_copy(4 * (2 * step - 1 + way) + 2 * dy).start()

    def parts_copy(send, recv, sem, src, dst, to):
        return pltpu.make_async_remote_copy(
            src_ref=send.at[src], dst_ref=recv.at[dst], send_sem=sem.at[0, src], recv_sem=sem.at[1, dst],
            device_id={"fsdp": to}, device_id_type=MESH)

    def m_copy(src, dst, to):
        return parts_copy(msend, mrecv, m_sem, src, dst, to)

    def o_copy(src, dst, to):
        return parts_copy(osend, orecv, o_sem, src, dst, to)

    def t_copy(src, dst, to):
        return parts_copy(tsend, trecv, t_sem, src, dst, to)

    y_copy.start()
    ring_step(0, 0)
    twin_copy(0).start()

    def send_limits(k, carry):
        m_copy(k, mirrored(k), device_at(k)).start()
        return carry

    lax.fori_loop(1, fs, send_limits, 0)
    mrecv[0] = msend[0]
    arrived(2)
    ring_step(0, 1)
    twin_copy(2).start()

    kinds = (wg_ref, wu_ref, wd_ref)

    def weight_copy(src, at, to):
        return pltpu.make_async_remote_copy(
            src_ref=src, dst_ref=wraw.at[at], send_sem=w_sem.at[0, at], recv_sem=w_sem.at[1, at],
            device_id={"fsdp": to}, device_id_type=MESH)

    own_loads = [pltpu.make_async_copy(src, wraw.at[4 * i], w_sem.at[0, 4 * i]) for i, src in enumerate(kinds)]
    near_copies = [weight_copy(src, 4 * i + 1, twin) for i, src in enumerate(kinds)]
    far_copies = [weight_copy(src, 4 * i + 2, across) for i, src in enumerate(kinds)]
    pass_copies = [weight_copy(wraw.at[4 * i + 2], 4 * i + 3, twin) for i in range(3)]
    for copy in far_copies[:1] + near_copies + own_loads:
        copy.start()

    head_of = iota((1, features), 1) // HEAD_DIM
    head_masks = [jnp.where(head_of == h, 1.0, 0.0) for h in range(heads)]
    scaled_masks = [(m * HEAD_DIM**-0.5).astype(BF16) for m in head_masks]

    def spread(q):
        parts = [q * m for m in scaled_masks]
        return jnp.concatenate(parts + [jnp.zeros((wide - rows, features), BF16)], axis=0)

    def gather_heads(o):
        total = o[0:tree] * head_masks[0]
        for h in range(1, heads):
            total = total + o[h * tree : (h + 1) * tree] * head_masks[h]
        return total

    spread_q = [spread(q_ref[r * tree : (r + 1) * tree, :]) for r in range(requests)]
    both_q = jnp.concatenate(spread_q, axis=0)

    for copy in pool_copies:
        copy.wait()
    stat_row = iota((4, 128), 0)
    held_row = iota((page_rows, wide), 0)

    def serve_one(k):
        page = serve_ref[device_at(k)]
        told = mrecv[k]
        told = jnp.concatenate([told, told], axis=1)
        limit, pick = told[0:1], told[1:2]
        asked = qall[k].astype(F32)
        query = (asked[0:tree] * (1.0 - pick) + asked[tree : 2 * tree] * pick).astype(BF16)
        scores = mm_nt(kbuf[page], spread(query))
        scores = jnp.where(held_row < limit.astype(jnp.int32), scores, NEGATIVE)
        best = jnp.max(scores, axis=0, keepdims=True)
        weights = jnp.exp(scores - best).astype(BF16)
        amount = jnp.sum(weights.astype(F32), axis=0, keepdims=True)
        osend[k] = gather_heads(mm_tn(weights, vbuf[page])).astype(BF16)
        tsend[k] = jnp.where(
            stat_row == 0, best[:, 0:128],
            jnp.where(stat_row == 1, best[:, 128:256],
                      jnp.where(stat_row == 2, amount[:, 0:128], amount[:, 128:256])))

    group = 4

    def serve_step(step, carry):
        for i in range(group):
            k = step * group + i

            @pl.when(k > 0)
            def _():
                m_copy(k, k, me).wait_recv()

            if i % 2 == 1:
                arrived(k)
        for i in range(group):
            serve_one(step * group + i)
        for i in range(group):
            k = step * group + i

            @pl.when(k > 0)
            def _():
                o_copy(k, mirrored(k), device_at(k)).start()
                t_copy(k, mirrored(k), device_at(k)).start()

        return carry

    for step in range(1, last + 1):
        for dy in range(2):
            ring_step(step, dy)
        lax.fori_loop(max(0, 2 * step - 3), 2 * step - 1, serve_step, 0)
    for dy in range(2):
        arrived(4 * (zs - 1) + 2 * dy)
        twin_copy(4 * (zs - 1) + 2 * dy).start()
    lax.fori_loop(2 * last - 1, zs, serve_step, 0)
    far_copies[1].start()

    eye = jnp.where(iota((tree, tree), 0) == iota((tree, tree), 1), 1.0, 0.0)
    tile_heads = jnp.where(
        (iota((tree, wide), 1) % tree == iota((tree, wide), 0)) & (iota((tree, wide), 1) < rows), 1.0, 0.0
    ).astype(BF16)
    tree_scores = []
    for r in range(requests):
        linked = jnp.where(parent_ref[r : r + 1, :] == iota((tree, tree), 0), 1.0, 0.0)
        reach = jnp.minimum(linked + eye, 1.0)
        for _ in range(tree.bit_length()):
            half_reach = reach.astype(BF16)
            reach = jnp.minimum(mm(half_reach, half_reach), 1.0)
        seen = mm(reach.astype(BF16), tile_heads)
        scores = mm_nt(nk_ref[r * tree : (r + 1) * tree, :], spread_q[r])
        tree_scores.append(jnp.where(seen > 0.5, scores, NEGATIVE))
    top = jnp.concatenate([jnp.max(s, axis=0, keepdims=True) for s in tree_scores], axis=1)

    key_row = iota((page_rows, 2 * wide), 0)
    chunk = 4

    def score_chunk(c, top):
        for i in range(chunk):
            page = c * chunk + i
            scores = mm_nt(kbuf[page], both_q)
            scores = jnp.where(key_row < lim_scr[pl.ds(page, 1), :], scores, NEGATIVE)
            s_scr[page] = scores
            top = jnp.maximum(top, jnp.max(scores, axis=0, keepdims=True))
        return top

    chunks = local_pages // chunk
    top = lax.fori_loop(0, chunks, score_chunk, top)

    def mix_chunk(c, carry):
        total, mixed = carry
        at = pl.ds(c * chunk, chunk)
        weights = jnp.exp(s_scr[at].reshape(chunk * page_rows, 2 * wide) - top).astype(BF16)
        total = total + jnp.sum(weights.astype(F32), axis=0, keepdims=True)
        values = vbuf[at].reshape(chunk * page_rows, features)
        return total, mixed + mm_tn(weights, values)

    total, mixed = lax.fori_loop(
        0, chunks, mix_chunk,
        (jnp.zeros((1, 2 * wide), F32), jnp.zeros((2 * wide, features), F32)))
    own_top, own_total, own_mix = [], [], []
    for r in range(requests):
        top_r = top[:, r * wide : (r + 1) * wide]
        weights = jnp.exp(tree_scores[r] - top_r).astype(BF16)
        own_top.append(top_r)
        own_total.append(
            total[:, r * wide : (r + 1) * wide] + jnp.sum(weights.astype(F32), axis=0, keepdims=True))
        mix_r = mixed[r * wide : (r + 1) * wide] + mm_tn(weights, nv_ref[r * tree : (r + 1) * tree, :])
        own_mix.append(gather_heads(mix_r))

    orecv[0] = osend[0]
    trecv[0] = tsend[0]

    def await_stats(k, carry):
        t_copy(k, k, me).wait_recv()
        return carry

    lax.fori_loop(1, fs, await_stats, 0)

    pick = rq_scr[:, 0:128]
    weight_any = [jnp.zeros((fs, 128), F32), jnp.zeros((fs, 128), F32)]
    own_weight = []
    for r in range(requests):
        chosen = pick if r == 1 else 1.0 - pick
        shares = []
        for hh in range(2):
            best = jnp.where(chosen > 0.5, trecv[:, hh, :], NEGATIVE)
            amount = trecv[:, 2 + hh, :]
            mine = own_top[r][:, hh * 128 : (hh + 1) * 128]
            highest = jnp.maximum(jnp.max(best, axis=0, keepdims=True), mine)
            weights = jnp.exp(best - highest) * chosen
            own = jnp.exp(mine - highest)
            bottom = jnp.sum(weights * amount, axis=0, keepdims=True) + (
                own * own_total[r][:, hh * 128 : (hh + 1) * 128])
            weight_any[hh] = weight_any[hh] + weights / bottom
            shares.append(own / bottom)
        own_weight.append(shares)
    for hh in range(2):
        sheet = jnp.concatenate(
            [weight_any[hh]]
            + [jnp.broadcast_to(own_weight[r][hh], (8, 128)) for r in range(requests)]
            + [jnp.zeros((128 - fs - 8 * requests, 128), F32)], axis=0)
        wt_scr[hh * 128 : (hh + 1) * 128, :] = sheet.T

    def factor(col):
        out = wt_scr[0:tree, col : col + 1] * head_masks[0]
        for h in range(1, heads):
            out = out + wt_scr[h * tree : (h + 1) * tree, col : col + 1] * head_masks[h]
        return out

    def await_parts(k, carry):
        o_copy(k, k, me).wait_recv()
        return carry

    lax.fori_loop(1, fs, await_parts, 0)
    merged = [own_mix[r] * factor(fs + 8 * r) for r in range(requests)]
    for k in range(fs):
        part = orecv[k].astype(F32) * factor(k)
        pick_row = rq_scr[k : k + 1, :]
        merged[0] = merged[0] + part * (1.0 - pick_row)
        merged[1] = merged[1] + part * pick_row
    attended = jnp.concatenate(merged, axis=0).astype(BF16)
    far_copies[0].wait_recv()
    pass_copies[0].start()

    side, per_side = vs // 2, owners // 2

    def owns(v):
        return lax.rem(v, side) < per_side

    def share(v):
        return v // side * per_side + lax.rem(v, side)

    own = share(ve)
    per_owner = resid_ref.shape[1]
    tile = 256
    for c in range(width // tile):
        block = mm(attended, ow_ref[:, c * tile : (c + 1) * tile])
        for o in range(owners):
            piece = block[o * per_owner : (o + 1) * per_owner]
            pown[o, :, c * tile : (c + 1) * tile] = piece
            psend[o, :, c * tile : (c + 1) * tile] = piece.astype(BF16)

    def p_copy(k, to):
        return pltpu.make_async_remote_copy(
            src_ref=psend.at[share(to)], dst_ref=precv.at[k], send_sem=p_sem.at[0, k], recv_sem=p_sem.at[1, k],
            device_id={"vocab": to}, device_id_type=MESH)

    def n_copy(k, owner, to):
        return pltpu.make_async_remote_copy(
            src_ref=normed_ref.at[owner], dst_ref=normed_ref.at[owner],
            send_sem=n_sem.at[0, k], recv_sem=n_sem.at[1, k],
            device_id={"vocab": to}, device_id_type=MESH)

    def h_copy(k, owner, to):
        return pltpu.make_async_remote_copy(
            src_ref=hsend.at[to], dst_ref=cols_ref.at[owner], send_sem=h_sem.at[0, k], recv_sem=h_sem.at[1, k],
            device_id={"vocab": to}, device_id_type=MESH)

    for k in range(1, vs):
        to = lax.rem(ve + k, vs)

        @pl.when(owns(to))
        def _():
            p_copy(k, to).start()

    @pl.when(owns(ve))
    def _():
        hidden = resid_ref[own].astype(F32) + pown[own]
        for k in range(1, vs):
            p_copy(k, ve).wait_recv()
            hidden = hidden + precv[k].astype(F32)
        mean = jnp.mean(hidden * hidden, axis=-1, keepdims=True)
        normed_ref[own] = (hidden * lax.rsqrt(mean + EPSILON) * gain_ref[...].reshape(1, width)).astype(BF16)
        for k in range(1, vs):
            n_copy(k, own, lax.rem(ve + k, vs)).start()
        columns = width // vs
        padded = hsend.shape[2]
        for v in range(vs):
            turned = hidden if v == 0 else pltpu.roll(hidden, width - v * columns, 1)
            hsend[v] = turned[:, 0:padded]
        for k in range(1, vs):
            h_copy(k, own, lax.rem(ve + k, vs)).start()
        cols_ref[own] = hsend[ve]

    for k in range(1, vs):
        owner = lax.rem(ve - k + vs, vs)

        @pl.when(owns(owner))
        def _():
            n_copy(k, share(owner), ve).wait_recv()
            h_copy(k, share(owner), ve).wait_recv()

    def finish():
        def await_sends(k, carry):
            m_copy(k, k, me).wait_send()
            o_copy(k, k, me).wait_send()
            t_copy(k, k, me).wait_send()
            return carry

        lax.fori_loop(1, fs, await_sends, 0)
        y_copy.wait_send()
        for step in range(zs):
            for dy in range(2):
                twin_copy(4 * step + 2 * dy).wait_send()
        for step in range(last + 1):
            for way in range(2):
                for dy in range(2):
                    if step < last or way == dy:
                        ring_copy(way, step, dy).wait_send()
        for k in range(1, vs):
            to = lax.rem(ve + k, vs)

            @pl.when(owns(to))
            def _():
                p_copy(k, to).wait_send()

        @pl.when(owns(ve))
        def _():
            for k in range(1, vs):
                to = lax.rem(ve + k, vs)
                n_copy(k, own, to).wait_send()
                h_copy(k, own, to).wait_send()

        for copy in far_copies + near_copies + pass_copies:
            copy.wait_send()

    return finish, own_loads, near_copies, far_copies, pass_copies


def expert_part(
    fs, vs, zs, own_loads, near_copies, far_copies, pass_copies,
    normed_ref, cols_ref, routes_ref, router_ref,
    out_ref,
    wraw, weights, rt_scr, xbuf, obuf, sbuf, rbuf, fsend, frecv,
    ag_sem, rs_sem, f_sem,
):
    owners, per_owner, width = normed_ref.shape
    tokens = owners * per_owner
    normed = normed_ref[...].reshape(tokens, width)
    block = xbuf.shape[1] // 2
    cut = xbuf.shape[2]
    slots = fsend.shape[1]
    kinds, sources = 3, wraw.shape[0] // 3
    hidden = wraw.shape[1]
    pitch = weights.shape[1]
    me = lax.axis_index("fsdp")
    ve = lax.axis_index("vocab")
    core = lax.rem(me, 2)
    z = lax.rem(me // 2, zs)
    yhi = me // (2 * zs)
    right = (yhi * zs + lax.rem(z + 1, zs)) * 2 + core
    left = (yhi * zs + lax.rem(z + zs - 1, zs)) * 2 + core

    rt_scr[...] = jnp.zeros(rt_scr.shape, F32)
    rt_scr[0:2, 0:tokens] = routes_ref[...].astype(F32)
    columns_of = rt_scr[...].T[0:tokens].astype(jnp.int32)
    lane = iota((tokens, 128), 1)
    first, second = columns_of[:, 0:1], columns_of[:, 1:2]
    hits = jnp.where((first == lane) | (second == lane), 1.0, 0.0)
    below = jnp.where(iota((tokens, tokens), 1) < iota((tokens, tokens), 0), 1.0, 0.0).astype(BF16)
    ranks = mm(below, hits.astype(BF16))
    my_hit = jnp.sum(jnp.where(lane == ve, hits, 0.0), axis=1, keepdims=True)
    my_rank = jnp.sum(jnp.where(lane == ve, ranks, 0.0), axis=1, keepdims=True)
    mine = jnp.where((my_hit > 0.5) & (my_rank == lane.astype(F32)), 1.0, 0.0)

    picked = mm_tn(mine.astype(BF16), normed)[0:block]
    xbuf[0] = jnp.concatenate([picked[:, 0:cut], picked[:, cut:width]], axis=0).astype(BF16)

    ways = (right, left)
    steps = zs // 2
    middle = (cut // 128 + 1) // 2 * 128
    spans = (pl.ds(0, middle), pl.ds(middle, cut - middle))

    def halves(step, way):
        return (way,) if step == steps - 1 else (0, 1)

    def gather_copy(way, step, h):
        src = 0 if step == 0 else 2 * step - 1 + way
        dst = zs - 1 if step == steps - 1 else 2 * step + 1 + way
        return pltpu.make_async_remote_copy(
            src_ref=xbuf.at[src, :, spans[h]], dst_ref=xbuf.at[dst, :, spans[h]],
            send_sem=ag_sem.at[0, way, step, h], recv_sem=ag_sem.at[1, way, step, h],
            device_id={"fsdp": ways[way]}, device_id_type=MESH)

    def gather_step(step):
        for h in (0, 1):
            for way in range(2):
                if step > 0:
                    gather_copy(way, step - 1, h).wait_recv()
                if h in halves(step, way):
                    gather_copy(way, step, h).start()

    def expert_up(first_block, count):
        blocks = range(first_block, first_block + count)
        sides = [
            jnp.concatenate([xbuf[b, at : at + block, :].astype(F32) for b in blocks], axis=0)
            for at in (0, block)
        ]
        rows = jnp.concatenate(sides, axis=1).astype(BF16)
        gate = mm_nt(rows, weights[0:sources].reshape(sources * pitch, width))
        lifted = mm_nt(rows, weights[sources : 2 * sources].reshape(sources * pitch, width))
        return (gate / (1.0 + jnp.exp(-gate)) * lifted).astype(BF16)

    def expert_down(acts, first_block, count):
        tile = cut // 3
        for side in range(2):
            for c in range(3):
                down = weights[2 * sources : 3 * sources, :, side * cut + c * tile : side * cut + (c + 1) * tile]
                out = mm(acts, down.reshape(sources * pitch, tile))
                for i in range(count):
                    obuf[first_block + i, side * block : (side + 1) * block, c * tile : (c + 1) * tile] = (
                        out[i * block : (i + 1) * block])

    gather_step(0)
    far_copies[2].start()
    far_copies[1].wait_recv()
    pass_copies[1].start()
    logits = mm_nt(normed, router_ref[...])
    lane8 = iota(logits.shape, 1)
    chosen0 = jnp.sum(jnp.where(lane8 == first, logits, 0.0), axis=1, keepdims=True)
    chosen1 = jnp.sum(jnp.where(lane8 == second, logits, 0.0), axis=1, keepdims=True)
    gate0 = 1.0 / (1.0 + jnp.exp(chosen1 - chosen0))
    gate1 = 1.0 / (1.0 + jnp.exp(chosen0 - chosen1))
    my_gate = jnp.where(first == ve, gate0, jnp.where(second == ve, gate1, 0.0))
    slot_gate = jnp.sum((mine * my_gate).T, axis=1, keepdims=True)[0:block]
    spread_e = jnp.where(iota((128, vs * slots), 0) == iota((128, vs * slots), 1) // slots, 1.0, 0.0).astype(BF16)
    all_hits = mm(hits.astype(BF16), spread_e)
    all_ranks = mm(ranks.astype(BF16), spread_e)
    slot_at = (iota((tokens, vs * slots), 1) % slots).astype(F32)
    back = jnp.where((all_hits > 0.5) & (all_ranks == slot_at), 1.0, 0.0).astype(BF16)

    def settle(i, carry):
        weights[i, pitch - 16 : pitch, :] = jnp.zeros((16, width), BF16)
        weights[i, 0:hidden, :] = wraw[i]
        return carry

    for load, near in zip(own_loads, near_copies):
        load.wait()
        near.wait_recv()
    pass_copies[0].wait_recv()
    lax.fori_loop(0, sources, settle, 0)
    lax.fori_loop(2 * sources, 2 * sources + 2, settle, 0)
    pass_copies[1].wait_recv()
    lax.fori_loop(sources, 2 * sources, settle, 0)
    for step in range(1, steps):
        gather_step(step)
        if step == 2:
            near_acts = expert_up(0, 5)
    for way in range(2):
        gather_copy(way, steps - 1, way).wait_recv()
    far_acts = expert_up(5, 3)
    far_copies[2].wait_recv()
    pass_copies[2].start()
    lax.fori_loop(2 * sources + 2, 2 * sources + 3, settle, 0)
    pass_copies[2].wait_recv()
    lax.fori_loop(2 * sources + 3, 3 * sources, settle, 0)
    expert_down(far_acts, 5, 3)

    def sum_copy(way, step, h):
        return pltpu.make_async_remote_copy(
            src_ref=sbuf.at[way, step, :, spans[h]], dst_ref=rbuf.at[way, step, :, spans[h]],
            send_sem=rs_sem.at[0, way, step, h], recv_sem=rs_sem.at[1, way, step, h],
            device_id={"fsdp": ways[way]}, device_id_type=MESH)

    for step in range(steps):
        for h in (0, 1):
            at = spans[h]
            for way in range(2):
                if step == 0:
                    if h != way:
                        continue
                    sbuf[way, 0, :, at] = obuf[zs - 1, :, at].astype(BF16)
                else:
                    source = 2 * (steps - step) - way
                    value = obuf[source, :, at]
                    if step > 1 or h == way:
                        sum_copy(way, step - 1, h).wait_recv()
                        value = value + rbuf[way, step - 1, :, at].astype(F32)
                    sbuf[way, step, :, at] = value.astype(BF16)
                sum_copy(way, step, h).start()
        if step == 0:
            expert_down(near_acts, 0, 5)
    for way in range(2):
        for h in (0, 1):
            sum_copy(way, steps - 1, h).wait_recv()
    whole = obuf[0] + rbuf[0, steps - 1].astype(F32) + rbuf[1, steps - 1].astype(F32)
    gated = [whole[side * block : (side + 1) * block] * slot_gate for side in range(2)]

    columns = width // vs
    padded = fsend.shape[2]
    empty = jnp.zeros((slots - block, padded), F32)

    def f_copy(k, to, slot):
        return pltpu.make_async_remote_copy(
            src_ref=fsend.at[to], dst_ref=frecv.at[slot], send_sem=f_sem.at[0, k], recv_sem=f_sem.at[1, k],
            device_id={"vocab": to}, device_id_type=MESH)

    for v in range(vs):
        side, at = divmod(v * columns, cut)
        turned = gated[side] if at == 0 else pltpu.roll(gated[side], cut - at, 1)
        fsend[v] = jnp.concatenate([turned[:, 0:padded], empty], axis=0).astype(BF16)
    for k in range(1, vs):
        f_copy(k, lax.rem(ve + k, vs), ve).start()
    frecv[ve] = fsend[ve]
    for k in range(1, vs):
        f_copy(k, ve, lax.rem(ve - k + vs, vs)).wait_recv()
    mixture = mm(back, frecv[...].reshape(vs * slots, padded))
    out_ref[...] = (cols_ref[...].reshape(tokens, padded) + mixture)[:, 0:columns].astype(BF16)

    for step in range(steps):
        for way in range(2):
            for h in halves(step, way):
                gather_copy(way, step, h).wait_send()
    for step in range(steps):
        for way in range(2):
            for h in (0, 1):
                if step > 0 or h == way:
                    sum_copy(way, step, h).wait_send()
    for k in range(1, vs):
        f_copy(k, lax.rem(ve + k, vs), ve).wait_send()


def layer_kernel(fs, vs, zs, *refs):
    inputs, rest = refs[:12], refs[12:]
    routes_ref, router_ref = rest[:2]
    weight_refs, out_ref, rest = rest[2:5], rest[5], rest[6:]
    normed_ref, cols_ref = rest[:2]
    attention_scratch, expert_scratch, rest = rest[2:19], rest[19:28], rest[28:]
    attention_sems, expert_sems = rest[:12], rest[12:]
    finish, *copies = attention_part(
        fs, vs, zs, *inputs, *weight_refs, expert_scratch[0], normed_ref, cols_ref,
        *attention_scratch, *attention_sems)
    expert_part(
        fs, vs, zs, *copies, normed_ref, cols_ref, routes_ref, router_ref, out_ref,
        *expert_scratch, *expert_sems)
    finish()


def per_device(
    resid, queries, new_keys, new_values, pool_keys, pool_values, page_table, serve_pages, cache_lengths, parents,
    out_weight, norm_gain, router, routes, gate_weight, up_weight, down_weight,
):
    fs, vs = lax.axis_size("fsdp"), lax.axis_size("vocab")
    zs = fs // 4
    tokens, width = resid.shape
    features = queries.shape[1]
    tree = parents.shape[1]
    pool_pages, page_rows, _ = pool_keys.shape
    hidden = gate_weight.shape[2]
    pitch = -(-hidden // 64) * 64
    vmem = pl.BlockSpec(memory_space=pltpu.VMEM)
    smem = pl.BlockSpec(memory_space=pltpu.SMEM)
    hbm = pl.BlockSpec(memory_space=pl.ANY)
    dma = pltpu.SemaphoreType.DMA
    padded = -(-(width // vs) // 128) * 128
    per_owner = 16
    owners = tokens // per_owner
    wg, wu, wd = gate_weight[0].T, up_weight[0].T, down_weight[0]
    block, slots = 40, 48
    return pl.pallas_call(
        functools.partial(layer_kernel, fs, vs, zs),
        out_shape=jax.ShapeDtypeStruct((tokens, width // vs), BF16),
        in_specs=[vmem] * 4 + [smem] * 2 + [vmem] * 4 + [hbm] * 2 + [vmem] * 2 + [hbm] * 3,
        out_specs=vmem,
        scratch_shapes=[
            pltpu.VMEM((owners, per_owner, width), BF16),
            pltpu.VMEM((owners, per_owner, padded), F32),
            pltpu.VMEM(pool_keys.shape, BF16),
            pltpu.VMEM(pool_values.shape, BF16),
            pltpu.VMEM((pool_pages // 2, page_rows, 512), F32),
            pltpu.VMEM((pool_pages // 2, 512), jnp.int32),
            pltpu.VMEM((fs, features), F32),
            pltpu.VMEM((256, 128), F32),
            pltpu.VMEM((fs, 2 * tree, features), BF16),
            pltpu.VMEM((fs, 2, 128), F32),
            pltpu.VMEM((fs, 2, 128), F32),
            pltpu.VMEM((fs, tree, features), BF16),
            pltpu.VMEM((fs, tree, features), BF16),
            pltpu.VMEM((fs, 4, 128), F32),
            pltpu.VMEM((fs, 4, 128), F32),
            pltpu.VMEM((owners, per_owner, width), F32),
            pltpu.VMEM((owners, per_owner, width), BF16),
            pltpu.VMEM((vs, per_owner, width), BF16),
            pltpu.VMEM((vs, per_owner, padded), F32),
            pltpu.VMEM((12, hidden, width), BF16),
            pltpu.VMEM((12, pitch, width), BF16),
            pltpu.VMEM((128, 128), F32),
            pltpu.VMEM((zs, 2 * block, width // 2), BF16),
            pltpu.VMEM((zs, 2 * block, width // 2), F32),
            pltpu.VMEM((2, zs // 2, 2 * block, width // 2), BF16),
            pltpu.VMEM((2, zs // 2, 2 * block, width // 2), BF16),
            pltpu.VMEM((vs, slots, padded), BF16),
            pltpu.VMEM((vs, slots, padded), BF16),
            dma((4,)), dma((2, 12)), dma((fs,)), dma((1,)), dma((2, zs // 2, 2)), dma((fs // 2,)),
            dma((2, fs)), dma((2, fs)), dma((2, fs)), dma((2, vs)), dma((2, vs)), dma((2, vs)),
            dma((2, 2, zs // 2, 2)), dma((2, 2, zs // 2, 2)), dma((2, vs)),
        ],
        compiler_params=pltpu.CompilerParams(
            collective_id=1, has_side_effects=True, vmem_limit_bytes=60 * 2**20),
        name="layer",
    )(
        queries, new_keys, new_values, page_table, cache_lengths, serve_pages.reshape(-1), parents,
        resid.reshape(owners, per_owner, width), out_weight, norm_gain, pool_keys, pool_values,
        routes.T, router.T, wg, wu, wd)


def solution(mesh):
    in_specs = (
        P("fsdp", None), P("fsdp", "vocab"), P("fsdp", "vocab"), P("fsdp", "vocab"),
        P("fsdp", None, "vocab"), P("fsdp", None, "vocab"), P("fsdp", None), P("fsdp", None, None),
        P("fsdp"), P("fsdp", None), P("vocab", None), P(), P(), P("fsdp", None),
        P("vocab", None, "fsdp"), P("vocab", None, "fsdp"), P("vocab", "fsdp", None),
    )
    return jax.shard_map(
        per_device, mesh=mesh, in_specs=in_specs, out_specs=P("fsdp", "vocab"), check_vma=False
    )
```

```python
import functools

import jax
import jax.numpy as jnp
from jax import lax
from jax.experimental import pallas as pl
from jax.experimental.pallas import tpu as pltpu
from jax.sharding import PartitionSpec as P

HEAD_DIM = 64
CAPACITY = 36
NEGATIVE = -1e30
EPSILON = 1e-05
MESH = pl.DeviceIdType.MESH
F32 = jnp.float32
BF16 = jnp.bfloat16


def mm(a, b):
    return jnp.dot(a, b, preferred_element_type=F32)


def mm_nt(a, b):
    return lax.dot_general(a, b, (((1,), (1,)), ((), ())), preferred_element_type=F32)


def mm_tn(a, b):
    return lax.dot_general(a, b, (((0,), (0,)), ((), ())), preferred_element_type=F32)


def iota(shape, dim):
    return lax.broadcasted_iota(jnp.int32, shape, dim)


def attention_part(
    fs, vs, zs,
    q_ref, nk_ref, nv_ref, table_ref, length_ref, serve_ref, parent_ref, resid_ref, ow_ref, gain_ref,
    pk_ref, pv_ref, wg_ref, wu_ref, wd_ref, wraw, packed,
    normed_ref, cols_ref,
    kbuf, vbuf, s_scr, lim_scr, rq_scr, wt_scr, qall, msend, mrecv, osend, orecv, tsend, trecv,
    pown, psend, precv, hsend,
    local_sem, w_sem, q_sem, y_sem, r_sem, c_sem, m_sem, o_sem, t_sem, p_sem, n_sem, h_sem,
):
    requests, pages_each = table_ref.shape
    tree = parent_ref.shape[1]
    features = q_ref.shape[1]
    heads = features // HEAD_DIM
    page_rows = pk_ref.shape[1]
    local_pages = pk_ref.shape[0] // 2
    pool_pages = pk_ref.shape[0]
    rows = heads * tree
    wide = 256
    width = ow_ref.shape[1]
    owners = resid_ref.shape[0]
    me = lax.axis_index("fsdp")
    ve = lax.axis_index("vocab")
    twin = me + 1 - 2 * lax.rem(me, 2)
    across = lax.rem(me + fs // 2, fs)
    core = lax.rem(me, 2)
    z = lax.rem(me // 2, zs)
    yhi = me // (2 * zs)
    right = (yhi * zs + lax.rem(z + 1, zs)) * 2 + core
    left = (yhi * zs + lax.rem(z + zs - 1, zs)) * 2 + core

    def device_at(slot):
        step = slot // 4
        odd = step % 2
        dz = (step // 2) * (1 - odd) - ((step + 1) // 2) * odd
        return (((yhi + (slot // 2) % 2) % 2) * zs + (z + dz + zs) % zs) * 2 + (core + slot % 2) % 2

    def mirrored(slot):
        step = slot // 4
        turned = jnp.minimum(jnp.maximum(step - 1 + 2 * (step % 2), 0), zs - 1)
        return 4 * turned + slot % 4

    barrier = pltpu.get_barrier_semaphore()

    def hail_fsdp(k, carry):
        pl.semaphore_signal(barrier, inc=1, device_id={"fsdp": lax.rem(me + k, fs)}, device_id_type=MESH)
        return carry

    def hail_vocab(k, carry):
        pl.semaphore_signal(barrier, inc=1, device_id={"vocab": lax.rem(ve + k, vs)}, device_id_type=MESH)
        return carry

    lax.fori_loop(1, fs, hail_fsdp, 0)
    lax.fori_loop(1, vs, hail_vocab, 0)
    half = local_pages
    pool_copies = [
        pltpu.make_async_copy(src.at[pl.ds(at, half)], dst.at[pl.ds(at, half)], local_sem.at[i])
        for i, (src, dst, at) in enumerate(
            ((pk_ref, kbuf, half), (pv_ref, vbuf, half), (pk_ref, kbuf, 0), (pv_ref, vbuf, 0))
        )
    ]
    for copy in pool_copies:
        copy.start()

    lane = iota((local_pages, pages_each), 1)
    sub = iota((local_pages, pages_each), 0)
    counts = [jnp.clip(length_ref[r] - page_rows * lane, 0, page_rows) for r in range(requests)]

    def lookup(target):
        hits = [table_ref[r : r + 1, :] == target for r in range(requests)]
        seen = [jnp.sum(jnp.where(h, c, 0).astype(F32), axis=1, keepdims=True) for h, c in zip(hits, counts)]
        return seen, jnp.sum(jnp.where(hits[1], 1.0, 0.0), axis=1, keepdims=True)

    (seen0, seen1), _ = lookup(sub)
    lane_w = iota((local_pages, 2 * wide), 1)
    lim_scr[...] = jnp.where(lane_w < wide, seen0, seen1).astype(jnp.int32)
    (far0, far1), far_rq = lookup(device_at(sub) + pool_pages)
    rq_scr[...] = jnp.broadcast_to(far_rq, rq_scr.shape)
    msend[...] = jnp.where(iota(msend.shape, 1) == 0, (far0 + far1)[:, :, None], far_rq[:, :, None])
    qall[0] = q_ref[...]

    pl.semaphore_wait(barrier, fs - 1 + vs - 1)

    def q_copy(src, dst, send_sem, to):
        return pltpu.make_async_remote_copy(
            src_ref=qall.at[src], dst_ref=qall.at[dst], send_sem=send_sem, recv_sem=q_sem.at[dst],
            device_id={"fsdp": to}, device_id_type=MESH)

    y_copy = q_copy(0, 2, y_sem.at[0], across)
    last = zs // 2 - 1

    def ring_copy(way, step, dy):
        src = 0 if step == 0 else 2 * step - 1 + way
        dst = zs - 1 if step == last else 2 * step + 1 + way
        return q_copy(4 * src + 2 * dy, 4 * dst + 2 * dy, r_sem.at[way, step, dy], (right, left)[way])

    def twin_copy(slot):
        return q_copy(slot, slot + 1, c_sem.at[slot // 2], twin)

    def arrived(slot):
        q_copy(slot, slot, y_sem.at[0], me).wait_recv()

    def ring_step(step, dy):
        for way in range(2):
            if step > 0:
                arrived(4 * (2 * step - 1 + way) + 2 * dy)
            if step < last or way == dy:
                ring_copy(way, step, dy).start()
            if step > 0:
                twin_copy(4 * (2 * step - 1 + way) + 2 * dy).start()

    def parts_copy(send, recv, sem, src, dst, to):
        return pltpu.make_async_remote_copy(
            src_ref=send.at[src], dst_ref=recv.at[dst], send_sem=sem.at[0, src], recv_sem=sem.at[1, dst],
            device_id={"fsdp": to}, device_id_type=MESH)

    def m_copy(src, dst, to):
        return parts_copy(msend, mrecv, m_sem, src, dst, to)

    def o_copy(src, dst, to):
        return parts_copy(osend, orecv, o_sem, src, dst, to)

    def t_copy(src, dst, to):
        return parts_copy(tsend, trecv, t_sem, src, dst, to)

    y_copy.start()
    ring_step(0, 0)
    twin_copy(0).start()

    def send_limits(k, carry):
        m_copy(k, mirrored(k), device_at(k)).start()
        return carry

    lax.fori_loop(1, fs, send_limits, 0)
    mrecv[0] = msend[0]
    arrived(2)
    ring_step(0, 1)
    twin_copy(2).start()

    kinds = (wg_ref, wu_ref, wd_ref)

    def weight_copy(src, at, to):
        return pltpu.make_async_remote_copy(
            src_ref=src, dst_ref=wraw.at[at], send_sem=w_sem.at[0, at], recv_sem=w_sem.at[1, at],
            device_id={"fsdp": to}, device_id_type=MESH)

    own_loads = [pltpu.make_async_copy(src, wraw.at[4 * i], w_sem.at[0, 4 * i]) for i, src in enumerate(kinds)]
    near_copies = [weight_copy(src, 4 * i + 1, twin) for i, src in enumerate(kinds)]
    far_copies = [weight_copy(src, 4 * i + 2, across) for i, src in enumerate(kinds)]
    pass_copies = [weight_copy(wraw.at[4 * i + 2], 4 * i + 3, twin) for i in range(3)]
    for copy in far_copies[:1] + near_copies + own_loads:
        copy.start()

    head_of = iota((1, features), 1) // HEAD_DIM
    head_masks = [jnp.where(head_of == h, 1.0, 0.0) for h in range(heads)]
    scaled_masks = [(m * HEAD_DIM**-0.5).astype(BF16) for m in head_masks]

    def spread(q):
        parts = [q * m for m in scaled_masks]
        return jnp.concatenate(parts + [jnp.zeros((wide - rows, features), BF16)], axis=0)

    def gather_heads(o):
        total = o[0:tree] * head_masks[0]
        for h in range(1, heads):
            total = total + o[h * tree : (h + 1) * tree] * head_masks[h]
        return total

    spread_q = [spread(q_ref[r * tree : (r + 1) * tree, :]) for r in range(requests)]
    both_q = jnp.concatenate(spread_q, axis=0)

    for copy in pool_copies:
        copy.wait()
    stat_row = iota((4, 128), 0)
    held_row = iota((page_rows, wide), 0)

    def serve_one(k):
        page = serve_ref[device_at(k)]
        told = mrecv[k]
        told = jnp.concatenate([told, told], axis=1)
        limit, pick = told[0:1], told[1:2]
        asked = qall[k].astype(F32)
        query = (asked[0:tree] * (1.0 - pick) + asked[tree : 2 * tree] * pick).astype(BF16)
        scores = mm_nt(kbuf[page], spread(query))
        scores = jnp.where(held_row < limit.astype(jnp.int32), scores, NEGATIVE)
        best = jnp.max(scores, axis=0, keepdims=True)
        weights = jnp.exp(scores - best).astype(BF16)
        amount = jnp.sum(weights.astype(F32), axis=0, keepdims=True)
        osend[k] = gather_heads(mm_tn(weights, vbuf[page])).astype(BF16)
        tsend[k] = jnp.where(
            stat_row == 0, best[:, 0:128],
            jnp.where(stat_row == 1, best[:, 128:256],
                      jnp.where(stat_row == 2, amount[:, 0:128], amount[:, 128:256])))

    group = 4

    def serve_step(step, carry):
        for i in range(group):
            k = step * group + i

            @pl.when(k > 0)
            def _():
                m_copy(k, k, me).wait_recv()

            if i % 2 == 1:
                arrived(k)
        for i in range(group):
            serve_one(step * group + i)
        for i in range(group):
            k = step * group + i

            @pl.when(k > 0)
            def _():
                o_copy(k, mirrored(k), device_at(k)).start()
                t_copy(k, mirrored(k), device_at(k)).start()

        return carry

    for step in range(1, last + 1):
        for dy in range(2):
            ring_step(step, dy)
        lax.fori_loop(max(0, 2 * step - 3), 2 * step - 1, serve_step, 0)
    for dy in range(2):
        arrived(4 * (zs - 1) + 2 * dy)
        twin_copy(4 * (zs - 1) + 2 * dy).start()
    lax.fori_loop(2 * last - 1, zs, serve_step, 0)
    far_copies[1].start()

    eye = jnp.where(iota((tree, tree), 0) == iota((tree, tree), 1), 1.0, 0.0)
    tile_heads = jnp.where(
        (iota((tree, wide), 1) % tree == iota((tree, wide), 0)) & (iota((tree, wide), 1) < rows), 1.0, 0.0
    ).astype(BF16)
    tree_scores = []
    for r in range(requests):
        linked = jnp.where(parent_ref[r : r + 1, :] == iota((tree, tree), 0), 1.0, 0.0)
        reach = jnp.minimum(linked + eye, 1.0)
        for _ in range(tree.bit_length()):
            half_reach = reach.astype(BF16)
            reach = jnp.minimum(mm(half_reach, half_reach), 1.0)
        seen = mm(reach.astype(BF16), tile_heads)
        scores = mm_nt(nk_ref[r * tree : (r + 1) * tree, :], spread_q[r])
        tree_scores.append(jnp.where(seen > 0.5, scores, NEGATIVE))
    top = jnp.concatenate([jnp.max(s, axis=0, keepdims=True) for s in tree_scores], axis=1)

    key_row = iota((page_rows, 2 * wide), 0)
    chunk = 4

    def score_chunk(c, top):
        for i in range(chunk):
            page = c * chunk + i
            scores = mm_nt(kbuf[page], both_q)
            scores = jnp.where(key_row < lim_scr[pl.ds(page, 1), :], scores, NEGATIVE)
            s_scr[page] = scores
            top = jnp.maximum(top, jnp.max(scores, axis=0, keepdims=True))
        return top

    chunks = local_pages // chunk
    top = lax.fori_loop(0, chunks, score_chunk, top)

    def mix_chunk(c, carry):
        total, mixed = carry
        at = pl.ds(c * chunk, chunk)
        weights = jnp.exp(s_scr[at].reshape(chunk * page_rows, 2 * wide) - top).astype(BF16)
        total = total + jnp.sum(weights.astype(F32), axis=0, keepdims=True)
        values = vbuf[at].reshape(chunk * page_rows, features)
        return total, mixed + mm_tn(weights, values)

    total, mixed = lax.fori_loop(
        0, chunks, mix_chunk,
        (jnp.zeros((1, 2 * wide), F32), jnp.zeros((2 * wide, features), F32)))
    own_top, own_total, own_mix = [], [], []
    for r in range(requests):
        top_r = top[:, r * wide : (r + 1) * wide]
        weights = jnp.exp(tree_scores[r] - top_r).astype(BF16)
        own_top.append(top_r)
        own_total.append(
            total[:, r * wide : (r + 1) * wide] + jnp.sum(weights.astype(F32), axis=0, keepdims=True))
        mix_r = mixed[r * wide : (r + 1) * wide] + mm_tn(weights, nv_ref[r * tree : (r + 1) * tree, :])
        own_mix.append(gather_heads(mix_r))

    orecv[0] = osend[0]
    trecv[0] = tsend[0]

    def await_stats(k, carry):
        t_copy(k, k, me).wait_recv()
        return carry

    lax.fori_loop(1, fs, await_stats, 0)

    pick = rq_scr[:, 0:128]
    weight_any = [jnp.zeros((fs, 128), F32), jnp.zeros((fs, 128), F32)]
    own_weight = []
    for r in range(requests):
        chosen = pick if r == 1 else 1.0 - pick
        shares = []
        for hh in range(2):
            best = jnp.where(chosen > 0.5, trecv[:, hh, :], NEGATIVE)
            amount = trecv[:, 2 + hh, :]
            mine = own_top[r][:, hh * 128 : (hh + 1) * 128]
            highest = jnp.maximum(jnp.max(best, axis=0, keepdims=True), mine)
            weights = jnp.exp(best - highest) * chosen
            own = jnp.exp(mine - highest)
            bottom = jnp.sum(weights * amount, axis=0, keepdims=True) + (
                own * own_total[r][:, hh * 128 : (hh + 1) * 128])
            weight_any[hh] = weight_any[hh] + weights / bottom
            shares.append(own / bottom)
        own_weight.append(shares)
    for hh in range(2):
        sheet = jnp.concatenate(
            [weight_any[hh]]
            + [jnp.broadcast_to(own_weight[r][hh], (8, 128)) for r in range(requests)]
            + [jnp.zeros((128 - fs - 8 * requests, 128), F32)], axis=0)
        wt_scr[hh * 128 : (hh + 1) * 128, :] = sheet.T

    def factor(col):
        out = wt_scr[0:tree, col : col + 1] * head_masks[0]
        for h in range(1, heads):
            out = out + wt_scr[h * tree : (h + 1) * tree, col : col + 1] * head_masks[h]
        return out

    def await_parts(k, carry):
        o_copy(k, k, me).wait_recv()
        return carry

    lax.fori_loop(1, fs, await_parts, 0)
    merged = [own_mix[r] * factor(fs + 8 * r) for r in range(requests)]
    for k in range(fs):
        part = orecv[k].astype(F32) * factor(k)
        pick_row = rq_scr[k : k + 1, :]
        merged[0] = merged[0] + part * (1.0 - pick_row)
        merged[1] = merged[1] + part * pick_row
    attended = jnp.concatenate(merged, axis=0).astype(BF16)
    far_copies[0].wait_recv()
    pass_copies[0].start()

    side, per_side = vs // 2, owners // 2

    def owns(v):
        return lax.rem(v, side) < per_side

    def share(v):
        return v // side * per_side + lax.rem(v, side)

    own = share(ve)
    per_owner = resid_ref.shape[1]
    tile = 256
    for c in range(width // tile):
        block = mm(attended, ow_ref[:, c * tile : (c + 1) * tile])
        for o in range(owners):
            piece = block[o * per_owner : (o + 1) * per_owner]
            pown[o, :, c * tile : (c + 1) * tile] = piece
            psend[o, :, c * tile : (c + 1) * tile] = piece.astype(BF16)

    def p_copy(k, to):
        return pltpu.make_async_remote_copy(
            src_ref=psend.at[share(to)], dst_ref=precv.at[k], send_sem=p_sem.at[0, k], recv_sem=p_sem.at[1, k],
            device_id={"vocab": to}, device_id_type=MESH)

    def n_copy(k, owner, to):
        return pltpu.make_async_remote_copy(
            src_ref=normed_ref.at[owner], dst_ref=normed_ref.at[owner],
            send_sem=n_sem.at[0, k], recv_sem=n_sem.at[1, k],
            device_id={"vocab": to}, device_id_type=MESH)

    def h_copy(k, owner, to):
        return pltpu.make_async_remote_copy(
            src_ref=hsend.at[to], dst_ref=cols_ref.at[owner], send_sem=h_sem.at[0, k], recv_sem=h_sem.at[1, k],
            device_id={"vocab": to}, device_id_type=MESH)

    for k in range(1, vs):
        to = lax.rem(ve + k, vs)

        @pl.when(owns(to))
        def _():
            p_copy(k, to).start()

    hidden_units, pitch = wraw.shape[1], packed.shape[1]

    def settle(i, carry):
        packed[i, pitch - 16 : pitch, :] = jnp.zeros((16, width), BF16)
        packed[i, 0:hidden_units, :] = wraw[i]
        return carry

    for i in range(3):
        own_loads[i].wait()
        near_copies[i].wait_recv()
        lax.fori_loop(4 * i, 4 * i + (3 if i == 0 else 2), settle, 0)

    @pl.when(owns(ve))
    def _():
        hidden = resid_ref[own].astype(F32) + pown[own]
        for k in range(1, vs):
            p_copy(k, ve).wait_recv()
            hidden = hidden + precv[k].astype(F32)
        mean = jnp.mean(hidden * hidden, axis=-1, keepdims=True)
        normed_ref[own] = (hidden * lax.rsqrt(mean + EPSILON) * gain_ref[...].reshape(1, width)).astype(BF16)
        for k in range(1, vs):
            n_copy(k, own, lax.rem(ve + k, vs)).start()
        columns = width // vs
        padded = hsend.shape[2]
        for v in range(vs):
            turned = hidden if v == 0 else pltpu.roll(hidden, width - v * columns, 1)
            hsend[v] = turned[:, 0:padded]
        for k in range(1, vs):
            h_copy(k, own, lax.rem(ve + k, vs)).start()
        cols_ref[own] = hsend[ve]

    pass_copies[0].wait_recv()
    lax.fori_loop(3, 4, settle, 0)
    far_copies[1].wait_recv()
    pass_copies[1].start()
    lax.fori_loop(6, 7, settle, 0)

    for k in range(1, vs):
        owner = lax.rem(ve - k + vs, vs)

        @pl.when(owns(owner))
        def _():
            n_copy(k, share(owner), ve).wait_recv()

    far_copies[2].start()

    def await_columns():
        for k in range(1, vs):
            owner = lax.rem(ve - k + vs, vs)

            @pl.when(owns(owner))
            def _():
                h_copy(k, share(owner), ve).wait_recv()

    def finish():
        def await_sends(k, carry):
            m_copy(k, k, me).wait_send()
            o_copy(k, k, me).wait_send()
            t_copy(k, k, me).wait_send()
            return carry

        lax.fori_loop(1, fs, await_sends, 0)
        y_copy.wait_send()
        for step in range(zs):
            for dy in range(2):
                twin_copy(4 * step + 2 * dy).wait_send()
        for step in range(last + 1):
            for way in range(2):
                for dy in range(2):
                    if step < last or way == dy:
                        ring_copy(way, step, dy).wait_send()
        for k in range(1, vs):
            to = lax.rem(ve + k, vs)

            @pl.when(owns(to))
            def _():
                p_copy(k, to).wait_send()

        @pl.when(owns(ve))
        def _():
            for k in range(1, vs):
                to = lax.rem(ve + k, vs)
                n_copy(k, own, to).wait_send()
                h_copy(k, own, to).wait_send()

        for copy in far_copies + near_copies + pass_copies:
            copy.wait_send()

    return finish, await_columns, far_copies, pass_copies


def expert_part(
    fs, vs, zs, await_columns, far_copies, pass_copies,
    normed_ref, cols_ref, routes_ref, router_ref,
    out_ref,
    wraw, weights, rt_scr, xbuf, obuf, sbuf, rbuf, fsend, frecv,
    ag_sem, rs_sem, f_sem,
):
    owners, per_owner, width = normed_ref.shape
    tokens = owners * per_owner
    normed = normed_ref[...].reshape(tokens, width)
    block = xbuf.shape[1] // 2
    cut = xbuf.shape[2]
    slots = fsend.shape[1]
    kinds, sources = 3, wraw.shape[0] // 3
    hidden = wraw.shape[1]
    pitch = weights.shape[1]
    me = lax.axis_index("fsdp")
    ve = lax.axis_index("vocab")
    core = lax.rem(me, 2)
    z = lax.rem(me // 2, zs)
    yhi = me // (2 * zs)
    right = (yhi * zs + lax.rem(z + 1, zs)) * 2 + core
    left = (yhi * zs + lax.rem(z + zs - 1, zs)) * 2 + core

    rt_scr[...] = jnp.zeros(rt_scr.shape, F32)
    rt_scr[0:2, 0:tokens] = routes_ref[...].astype(F32)
    columns_of = rt_scr[...].T[0:tokens].astype(jnp.int32)
    lane = iota((tokens, 128), 1)
    first, second = columns_of[:, 0:1], columns_of[:, 1:2]
    hits = jnp.where((first == lane) | (second == lane), 1.0, 0.0)
    below = jnp.where(iota((tokens, tokens), 1) < iota((tokens, tokens), 0), 1.0, 0.0).astype(BF16)
    ranks = mm(below, hits.astype(BF16))
    my_hit = jnp.sum(jnp.where(lane == ve, hits, 0.0), axis=1, keepdims=True)
    my_rank = jnp.sum(jnp.where(lane == ve, ranks, 0.0), axis=1, keepdims=True)
    mine = jnp.where((my_hit > 0.5) & (my_rank == lane.astype(F32)), 1.0, 0.0)

    picked = mm_tn(mine.astype(BF16), normed)[0:block]
    xbuf[0] = jnp.concatenate([picked[:, 0:cut], picked[:, cut:width]], axis=0).astype(BF16)

    ways = (right, left)
    steps = zs // 2
    middle = (cut // 128 + 1) // 2 * 128
    spans = (pl.ds(0, middle), pl.ds(middle, cut - middle))

    def halves(step, way):
        return (way,) if step == steps - 1 else (0, 1)

    def gather_copy(way, step, h):
        src = 0 if step == 0 else 2 * step - 1 + way
        dst = zs - 1 if step == steps - 1 else 2 * step + 1 + way
        return pltpu.make_async_remote_copy(
            src_ref=xbuf.at[src, :, spans[h]], dst_ref=xbuf.at[dst, :, spans[h]],
            send_sem=ag_sem.at[0, way, step, h], recv_sem=ag_sem.at[1, way, step, h],
            device_id={"fsdp": ways[way]}, device_id_type=MESH)

    def gather_step(step):
        for h in (0, 1):
            for way in range(2):
                if step > 0:
                    gather_copy(way, step - 1, h).wait_recv()
                if h in halves(step, way):
                    gather_copy(way, step, h).start()

    def expert_up(first_block, count):
        blocks = range(first_block, first_block + count)
        sides = [
            jnp.concatenate([xbuf[b, at : at + block, :].astype(F32) for b in blocks], axis=0)
            for at in (0, block)
        ]
        rows = jnp.concatenate(sides, axis=1).astype(BF16)
        gate = mm_nt(rows, weights[0:sources].reshape(sources * pitch, width))
        lifted = mm_nt(rows, weights[sources : 2 * sources].reshape(sources * pitch, width))
        return (gate / (1.0 + jnp.exp(-gate)) * lifted).astype(BF16)

    def expert_down(acts, first_block, count):
        tile = cut // 3
        for side in range(2):
            for c in range(3):
                down = weights[2 * sources : 3 * sources, :, side * cut + c * tile : side * cut + (c + 1) * tile]
                out = mm(acts, down.reshape(sources * pitch, tile))
                for i in range(count):
                    obuf[first_block + i, side * block : (side + 1) * block, c * tile : (c + 1) * tile] = (
                        out[i * block : (i + 1) * block])

    gather_step(0)
    logits = mm_nt(normed, router_ref[...])
    lane8 = iota(logits.shape, 1)
    chosen0 = jnp.sum(jnp.where(lane8 == first, logits, 0.0), axis=1, keepdims=True)
    chosen1 = jnp.sum(jnp.where(lane8 == second, logits, 0.0), axis=1, keepdims=True)
    gate0 = 1.0 / (1.0 + jnp.exp(chosen1 - chosen0))
    gate1 = 1.0 / (1.0 + jnp.exp(chosen0 - chosen1))
    my_gate = jnp.where(first == ve, gate0, jnp.where(second == ve, gate1, 0.0))
    slot_gate = jnp.sum((mine * my_gate).T, axis=1, keepdims=True)[0:block]
    spread_e = jnp.where(iota((128, vs * slots), 0) == iota((128, vs * slots), 1) // slots, 1.0, 0.0).astype(BF16)
    all_hits = mm(hits.astype(BF16), spread_e)
    all_ranks = mm(ranks.astype(BF16), spread_e)
    slot_at = (iota((tokens, vs * slots), 1) % slots).astype(F32)
    back = jnp.where((all_hits > 0.5) & (all_ranks == slot_at), 1.0, 0.0).astype(BF16)

    def settle(i, carry):
        weights[i, pitch - 16 : pitch, :] = jnp.zeros((16, width), BF16)
        weights[i, 0:hidden, :] = wraw[i]
        return carry

    for step in range(1, steps):
        gather_step(step)
        if step == 1:
            pass_copies[1].wait_recv()
            lax.fori_loop(2 * sources - 1, 2 * sources, settle, 0)
        if step == 2:
            near_acts = expert_up(0, 5)
    for way in range(2):
        gather_copy(way, steps - 1, way).wait_recv()
    far_acts = expert_up(5, 3)
    far_copies[2].wait_recv()
    pass_copies[2].start()
    lax.fori_loop(2 * sources + 2, 2 * sources + 3, settle, 0)
    pass_copies[2].wait_recv()
    lax.fori_loop(2 * sources + 3, 3 * sources, settle, 0)
    expert_down(far_acts, 5, 3)

    def sum_copy(way, step, h):
        return pltpu.make_async_remote_copy(
            src_ref=sbuf.at[way, step, :, spans[h]], dst_ref=rbuf.at[way, step, :, spans[h]],
            send_sem=rs_sem.at[0, way, step, h], recv_sem=rs_sem.at[1, way, step, h],
            device_id={"fsdp": ways[way]}, device_id_type=MESH)

    for step in range(steps):
        for h in (0, 1):
            at = spans[h]
            for way in range(2):
                if step == 0:
                    if h != way:
                        continue
                    sbuf[way, 0, :, at] = obuf[zs - 1, :, at].astype(BF16)
                else:
                    source = 2 * (steps - step) - way
                    value = obuf[source, :, at]
                    if step > 1 or h == way:
                        sum_copy(way, step - 1, h).wait_recv()
                        value = value + rbuf[way, step - 1, :, at].astype(F32)
                    sbuf[way, step, :, at] = value.astype(BF16)
                sum_copy(way, step, h).start()
        if step == 0:
            expert_down(near_acts, 0, 5)
    for way in range(2):
        for h in (0, 1):
            sum_copy(way, steps - 1, h).wait_recv()
    whole = obuf[0] + rbuf[0, steps - 1].astype(F32) + rbuf[1, steps - 1].astype(F32)
    gated = [whole[side * block : (side + 1) * block] * slot_gate for side in range(2)]

    columns = width // vs
    padded = fsend.shape[2]
    empty = jnp.zeros((slots - block, padded), F32)

    def f_copy(k, to, slot):
        return pltpu.make_async_remote_copy(
            src_ref=fsend.at[to], dst_ref=frecv.at[slot], send_sem=f_sem.at[0, k], recv_sem=f_sem.at[1, k],
            device_id={"vocab": to}, device_id_type=MESH)

    for v in range(vs):
        side, at = divmod(v * columns, cut)
        turned = gated[side] if at == 0 else pltpu.roll(gated[side], cut - at, 1)
        fsend[v] = jnp.concatenate([turned[:, 0:padded], empty], axis=0).astype(BF16)
    for k in range(1, vs):
        f_copy(k, lax.rem(ve + k, vs), ve).start()
    frecv[ve] = fsend[ve]
    for k in range(1, vs):
        f_copy(k, ve, lax.rem(ve - k + vs, vs)).wait_recv()
    mixture = mm(back, frecv[...].reshape(vs * slots, padded))
    await_columns()
    out_ref[...] = (cols_ref[...].reshape(tokens, padded) + mixture)[:, 0:columns].astype(BF16)

    for step in range(steps):
        for way in range(2):
            for h in halves(step, way):
                gather_copy(way, step, h).wait_send()
    for step in range(steps):
        for way in range(2):
            for h in (0, 1):
                if step > 0 or h == way:
                    sum_copy(way, step, h).wait_send()
    for k in range(1, vs):
        f_copy(k, lax.rem(ve + k, vs), ve).wait_send()


def layer_kernel(fs, vs, zs, *refs):
    inputs, rest = refs[:12], refs[12:]
    routes_ref, router_ref = rest[:2]
    weight_refs, out_ref, rest = rest[2:5], rest[5], rest[6:]
    normed_ref, cols_ref = rest[:2]
    attention_scratch, expert_scratch, rest = rest[2:19], rest[19:28], rest[28:]
    attention_sems, expert_sems = rest[:12], rest[12:]
    finish, *copies = attention_part(
        fs, vs, zs, *inputs, *weight_refs, *expert_scratch[:2], normed_ref, cols_ref,
        *attention_scratch, *attention_sems)
    expert_part(
        fs, vs, zs, *copies, normed_ref, cols_ref, routes_ref, router_ref, out_ref,
        *expert_scratch, *expert_sems)
    finish()


def per_device(
    resid, queries, new_keys, new_values, pool_keys, pool_values, page_table, serve_pages, cache_lengths, parents,
    out_weight, norm_gain, router, routes, gate_weight, up_weight, down_weight,
):
    fs, vs = lax.axis_size("fsdp"), lax.axis_size("vocab")
    zs = fs // 4
    tokens, width = resid.shape
    features = queries.shape[1]
    tree = parents.shape[1]
    pool_pages, page_rows, _ = pool_keys.shape
    hidden = gate_weight.shape[2]
    pitch = -(-hidden // 64) * 64
    vmem = pl.BlockSpec(memory_space=pltpu.VMEM)
    smem = pl.BlockSpec(memory_space=pltpu.SMEM)
    hbm = pl.BlockSpec(memory_space=pl.ANY)
    dma = pltpu.SemaphoreType.DMA
    padded = -(-(width // vs) // 128) * 128
    per_owner = 16
    owners = tokens // per_owner
    wg, wu, wd = gate_weight[0].T, up_weight[0].T, down_weight[0]
    block, slots = 40, 48
    return pl.pallas_call(
        functools.partial(layer_kernel, fs, vs, zs),
        out_shape=jax.ShapeDtypeStruct((tokens, width // vs), BF16),
        in_specs=[vmem] * 4 + [smem] * 2 + [vmem] * 4 + [hbm] * 2 + [vmem] * 2 + [hbm] * 3,
        out_specs=vmem,
        scratch_shapes=[
            pltpu.VMEM((owners, per_owner, width), BF16),
            pltpu.VMEM((owners, per_owner, padded), F32),
            pltpu.VMEM(pool_keys.shape, BF16),
            pltpu.VMEM(pool_values.shape, BF16),
            pltpu.VMEM((pool_pages // 2, page_rows, 512), F32),
            pltpu.VMEM((pool_pages // 2, 512), jnp.int32),
            pltpu.VMEM((fs, features), F32),
            pltpu.VMEM((256, 128), F32),
            pltpu.VMEM((fs, 2 * tree, features), BF16),
            pltpu.VMEM((fs, 2, 128), F32),
            pltpu.VMEM((fs, 2, 128), F32),
            pltpu.VMEM((fs, tree, features), BF16),
            pltpu.VMEM((fs, tree, features), BF16),
            pltpu.VMEM((fs, 4, 128), F32),
            pltpu.VMEM((fs, 4, 128), F32),
            pltpu.VMEM((owners, per_owner, width), F32),
            pltpu.VMEM((owners, per_owner, width), BF16),
            pltpu.VMEM((vs, per_owner, width), BF16),
            pltpu.VMEM((vs, per_owner, padded), F32),
            pltpu.VMEM((12, hidden, width), BF16),
            pltpu.VMEM((12, pitch, width), BF16),
            pltpu.VMEM((128, 128), F32),
            pltpu.VMEM((zs, 2 * block, width // 2), BF16),
            pltpu.VMEM((zs, 2 * block, width // 2), F32),
            pltpu.VMEM((2, zs // 2, 2 * block, width // 2), BF16),
            pltpu.VMEM((2, zs // 2, 2 * block, width // 2), BF16),
            pltpu.VMEM((vs, slots, padded), BF16),
            pltpu.VMEM((vs, slots, padded), BF16),
            dma((4,)), dma((2, 12)), dma((fs,)), dma((1,)), dma((2, zs // 2, 2)), dma((fs // 2,)),
            dma((2, fs)), dma((2, fs)), dma((2, fs)), dma((2, vs)), dma((2, vs)), dma((2, vs)),
            dma((2, 2, zs // 2, 2)), dma((2, 2, zs // 2, 2)), dma((2, vs)),
        ],
        compiler_params=pltpu.CompilerParams(
            collective_id=1, has_side_effects=True, vmem_limit_bytes=60 * 2**20),
        name="layer",
    )(
        queries, new_keys, new_values, page_table, cache_lengths, serve_pages.reshape(-1), parents,
        resid.reshape(owners, per_owner, width), out_weight, norm_gain, pool_keys, pool_values,
        routes.T, router.T, wg, wu, wd)


def solution(mesh):
    in_specs = (
        P("fsdp", None), P("fsdp", "vocab"), P("fsdp", "vocab"), P("fsdp", "vocab"),
        P("fsdp", None, "vocab"), P("fsdp", None, "vocab"), P("fsdp", None), P("fsdp", None, None),
        P("fsdp"), P("fsdp", None), P("vocab", None), P(), P(), P("fsdp", None),
        P("vocab", None, "fsdp"), P("vocab", None, "fsdp"), P("vocab", "fsdp", None),
    )
    return jax.shard_map(
        per_device, mesh=mesh, in_specs=in_specs, out_specs=P("fsdp", "vocab"), check_vma=False
    )
```

```python
import functools

import jax
import jax.numpy as jnp
from jax import lax
from jax.experimental import pallas as pl
from jax.experimental.pallas import tpu as pltpu
from jax.sharding import PartitionSpec as P

HEAD_DIM = 64
CAPACITY = 36
NEGATIVE = -1e30
EPSILON = 1e-05
MESH = pl.DeviceIdType.MESH
F32 = jnp.float32
BF16 = jnp.bfloat16


def mm(a, b):
    return jnp.dot(a, b, preferred_element_type=F32)


def mm_nt(a, b):
    return lax.dot_general(a, b, (((1,), (1,)), ((), ())), preferred_element_type=F32)


def mm_tn(a, b):
    return lax.dot_general(a, b, (((0,), (0,)), ((), ())), preferred_element_type=F32)


def iota(shape, dim):
    return lax.broadcasted_iota(jnp.int32, shape, dim)


def attention_part(
    fs, vs, zs,
    q_ref, nk_ref, nv_ref, table_ref, length_ref, serve_ref, parent_ref, resid_ref, ow_ref, gain_ref,
    pk_ref, pv_ref, wg_ref, wu_ref, wd_ref, wraw, packed,
    normed_ref, cols_ref,
    kbuf, vbuf, s_scr, lim_scr, rq_scr, wt_scr, qall, msend, mrecv, osend, orecv, tsend, trecv,
    pown, psend, precv, hsend,
    local_sem, w_sem, q_sem, y_sem, r_sem, c_sem, m_sem, o_sem, t_sem, p_sem, n_sem, h_sem,
):
    requests, pages_each = table_ref.shape
    tree = parent_ref.shape[1]
    features = q_ref.shape[1]
    heads = features // HEAD_DIM
    page_rows = pk_ref.shape[1]
    local_pages = pk_ref.shape[0] // 2
    pool_pages = pk_ref.shape[0]
    rows = heads * tree
    wide = 256
    width = ow_ref.shape[1]
    owners = resid_ref.shape[0]
    me = lax.axis_index("fsdp")
    ve = lax.axis_index("vocab")
    twin = me + 1 - 2 * lax.rem(me, 2)
    across = lax.rem(me + fs // 2, fs)
    core = lax.rem(me, 2)
    z = lax.rem(me // 2, zs)
    yhi = me // (2 * zs)
    right = (yhi * zs + lax.rem(z + 1, zs)) * 2 + core
    left = (yhi * zs + lax.rem(z + zs - 1, zs)) * 2 + core

    def device_at(slot):
        step = slot // 4
        odd = step % 2
        dz = (step // 2) * (1 - odd) - ((step + 1) // 2) * odd
        return (((yhi + (slot // 2) % 2) % 2) * zs + (z + dz + zs) % zs) * 2 + (core + slot % 2) % 2

    def mirrored(slot):
        step = slot // 4
        turned = jnp.minimum(jnp.maximum(step - 1 + 2 * (step % 2), 0), zs - 1)
        return 4 * turned + slot % 4

    barrier = pltpu.get_barrier_semaphore()

    def hail_fsdp(k, carry):
        pl.semaphore_signal(barrier, inc=1, device_id={"fsdp": lax.rem(me + k, fs)}, device_id_type=MESH)
        return carry

    def hail_vocab(k, carry):
        pl.semaphore_signal(barrier, inc=1, device_id={"vocab": lax.rem(ve + k, vs)}, device_id_type=MESH)
        return carry

    lax.fori_loop(1, fs, hail_fsdp, 0)
    lax.fori_loop(1, vs, hail_vocab, 0)
    half = local_pages
    pool_copies = [
        pltpu.make_async_copy(src.at[pl.ds(at, half)], dst.at[pl.ds(at, half)], local_sem.at[i])
        for i, (src, dst, at) in enumerate(
            ((pk_ref, kbuf, half), (pv_ref, vbuf, half), (pk_ref, kbuf, 0), (pv_ref, vbuf, 0))
        )
    ]
    for copy in pool_copies:
        copy.start()

    lane = iota((local_pages, pages_each), 1)
    sub = iota((local_pages, pages_each), 0)
    counts = [jnp.clip(length_ref[r] - page_rows * lane, 0, page_rows) for r in range(requests)]

    def lookup(target):
        hits = [table_ref[r : r + 1, :] == target for r in range(requests)]
        seen = [jnp.sum(jnp.where(h, c, 0).astype(F32), axis=1, keepdims=True) for h, c in zip(hits, counts)]
        return seen, jnp.sum(jnp.where(hits[1], 1.0, 0.0), axis=1, keepdims=True)

    (seen0, seen1), _ = lookup(sub)
    lane_w = iota((local_pages, 2 * wide), 1)
    lim_scr[...] = jnp.where(lane_w < wide, seen0, seen1).astype(jnp.int32)
    (far0, far1), far_rq = lookup(device_at(sub) + pool_pages)
    rq_scr[...] = jnp.broadcast_to(far_rq, rq_scr.shape)
    msend[...] = jnp.where(iota(msend.shape, 1) == 0, (far0 + far1)[:, :, None], far_rq[:, :, None])
    qall[0] = q_ref[...]

    pl.semaphore_wait(barrier, fs - 1 + vs - 1)

    def q_copy(src, dst, send_sem, to):
        return pltpu.make_async_remote_copy(
            src_ref=qall.at[src], dst_ref=qall.at[dst], send_sem=send_sem, recv_sem=q_sem.at[dst],
            device_id={"fsdp": to}, device_id_type=MESH)

    y_copy = q_copy(0, 2, y_sem.at[0], across)
    last = zs // 2 - 1

    def ring_copy(way, step, dy):
        src = 0 if step == 0 else 2 * step - 1 + way
        dst = zs - 1 if step == last else 2 * step + 1 + way
        return q_copy(4 * src + 2 * dy, 4 * dst + 2 * dy, r_sem.at[way, step, dy], (right, left)[way])

    def twin_copy(slot):
        return q_copy(slot, slot + 1, c_sem.at[slot // 2], twin)

    def arrived(slot):
        q_copy(slot, slot, y_sem.at[0], me).wait_recv()

    def ring_step(step, dy):
        for way in range(2):
            if step > 0:
                arrived(4 * (2 * step - 1 + way) + 2 * dy)
            if step < last or way == dy:
                ring_copy(way, step, dy).start()
            if step > 0:
                twin_copy(4 * (2 * step - 1 + way) + 2 * dy).start()

    def parts_copy(send, recv, sem, src, dst, to):
        return pltpu.make_async_remote_copy(
            src_ref=send.at[src], dst_ref=recv.at[dst], send_sem=sem.at[0, src], recv_sem=sem.at[1, dst],
            device_id={"fsdp": to}, device_id_type=MESH)

    def m_copy(src, dst, to):
        return parts_copy(msend, mrecv, m_sem, src, dst, to)

    def o_copy(src, dst, to):
        return parts_copy(osend, orecv, o_sem, src, dst, to)

    def t_copy(src, dst, to):
        return parts_copy(tsend, trecv, t_sem, src, dst, to)

    y_copy.start()
    ring_step(0, 0)
    twin_copy(0).start()

    def send_limits(k, carry):
        m_copy(k, mirrored(k), device_at(k)).start()
        return carry

    lax.fori_loop(1, fs, send_limits, 0)
    mrecv[0] = msend[0]
    arrived(2)
    ring_step(0, 1)
    twin_copy(2).start()

    kinds = (wg_ref, wu_ref, wd_ref)

    def weight_copy(src, at, to):
        return pltpu.make_async_remote_copy(
            src_ref=src, dst_ref=wraw.at[at], send_sem=w_sem.at[0, at], recv_sem=w_sem.at[1, at],
            device_id={"fsdp": to}, device_id_type=MESH)

    own_loads = [pltpu.make_async_copy(src, wraw.at[4 * i], w_sem.at[0, 4 * i]) for i, src in enumerate(kinds)]
    near_copies = [weight_copy(src, 4 * i + 1, twin) for i, src in enumerate(kinds)]
    far_copies = [weight_copy(src, 4 * i + 2, across) for i, src in enumerate(kinds)]
    pass_copies = [weight_copy(wraw.at[4 * i + 2], 4 * i + 3, twin) for i in range(3)]
    for copy in far_copies[:1] + near_copies + own_loads:
        copy.start()

    head_of = iota((1, features), 1) // HEAD_DIM
    head_masks = [jnp.where(head_of == h, 1.0, 0.0) for h in range(heads)]
    scaled_masks = [(m * HEAD_DIM**-0.5).astype(BF16) for m in head_masks]

    def spread(q):
        parts = [q * m for m in scaled_masks]
        return jnp.concatenate(parts + [jnp.zeros((wide - rows, features), BF16)], axis=0)

    def gather_heads(o):
        total = o[0:tree] * head_masks[0]
        for h in range(1, heads):
            total = total + o[h * tree : (h + 1) * tree] * head_masks[h]
        return total

    spread_q = [spread(q_ref[r * tree : (r + 1) * tree, :]) for r in range(requests)]
    both_q = jnp.concatenate(spread_q, axis=0)

    for copy in pool_copies:
        copy.wait()
    stat_row = iota((4, 128), 0)
    held_row = iota((page_rows, wide), 0)

    def serve_one(k):
        page = serve_ref[device_at(k)]
        told = mrecv[k]
        told = jnp.concatenate([told, told], axis=1)
        limit, pick = told[0:1], told[1:2]
        asked = qall[k].astype(F32)
        query = (asked[0:tree] * (1.0 - pick) + asked[tree : 2 * tree] * pick).astype(BF16)
        scores = mm_nt(kbuf[page], spread(query))
        scores = jnp.where(held_row < limit.astype(jnp.int32), scores, NEGATIVE)
        best = jnp.max(scores, axis=0, keepdims=True)
        weights = jnp.exp(scores - best).astype(BF16)
        amount = jnp.sum(weights.astype(F32), axis=0, keepdims=True)
        osend[k] = gather_heads(mm_tn(weights, vbuf[page])).astype(BF16)
        tsend[k] = jnp.where(
            stat_row == 0, best[:, 0:128],
            jnp.where(stat_row == 1, best[:, 128:256],
                      jnp.where(stat_row == 2, amount[:, 0:128], amount[:, 128:256])))

    group = 4

    def serve_step(step, carry):
        for i in range(group):
            k = step * group + i

            @pl.when(k > 0)
            def _():
                m_copy(k, k, me).wait_recv()

            if i % 2 == 1:
                arrived(k)
        for i in range(group):
            serve_one(step * group + i)
        for i in range(group):
            k = step * group + i

            @pl.when(k > 0)
            def _():
                o_copy(k, mirrored(k), device_at(k)).start()
                t_copy(k, mirrored(k), device_at(k)).start()

        return carry

    for step in range(1, last + 1):
        for dy in range(2):
            ring_step(step, dy)
        lax.fori_loop(max(0, 2 * step - 3), 2 * step - 1, serve_step, 0)
    for dy in range(2):
        arrived(4 * (zs - 1) + 2 * dy)
        twin_copy(4 * (zs - 1) + 2 * dy).start()
    lax.fori_loop(2 * last - 1, zs, serve_step, 0)
    far_copies[1].start()

    eye = jnp.where(iota((tree, tree), 0) == iota((tree, tree), 1), 1.0, 0.0)
    tile_heads = jnp.where(
        (iota((tree, wide), 1) % tree == iota((tree, wide), 0)) & (iota((tree, wide), 1) < rows), 1.0, 0.0
    ).astype(BF16)
    tree_scores = []
    for r in range(requests):
        linked = jnp.where(parent_ref[r : r + 1, :] == iota((tree, tree), 0), 1.0, 0.0)
        reach = jnp.minimum(linked + eye, 1.0)
        for _ in range(tree.bit_length()):
            half_reach = reach.astype(BF16)
            reach = jnp.minimum(mm(half_reach, half_reach), 1.0)
        seen = mm(reach.astype(BF16), tile_heads)
        scores = mm_nt(nk_ref[r * tree : (r + 1) * tree, :], spread_q[r])
        tree_scores.append(jnp.where(seen > 0.5, scores, NEGATIVE))
    top = jnp.concatenate([jnp.max(s, axis=0, keepdims=True) for s in tree_scores], axis=1)

    key_row = iota((page_rows, 2 * wide), 0)
    chunk = 4

    def score_chunk(c, top):
        for i in range(chunk):
            page = c * chunk + i
            scores = mm_nt(kbuf[page], both_q)
            scores = jnp.where(key_row < lim_scr[pl.ds(page, 1), :], scores, NEGATIVE)
            s_scr[page] = scores
            top = jnp.maximum(top, jnp.max(scores, axis=0, keepdims=True))
        return top

    chunks = local_pages // chunk
    top = lax.fori_loop(0, chunks, score_chunk, top)

    def mix_chunk(c, carry):
        total, mixed = carry
        at = pl.ds(c * chunk, chunk)
        weights = jnp.exp(s_scr[at].reshape(chunk * page_rows, 2 * wide) - top).astype(BF16)
        total = total + jnp.sum(weights.astype(F32), axis=0, keepdims=True)
        values = vbuf[at].reshape(chunk * page_rows, features)
        return total, mixed + mm_tn(weights, values)

    total, mixed = lax.fori_loop(
        0, chunks, mix_chunk,
        (jnp.zeros((1, 2 * wide), F32), jnp.zeros((2 * wide, features), F32)))
    own_top, own_total, own_mix = [], [], []
    for r in range(requests):
        top_r = top[:, r * wide : (r + 1) * wide]
        weights = jnp.exp(tree_scores[r] - top_r).astype(BF16)
        own_top.append(top_r)
        own_total.append(
            total[:, r * wide : (r + 1) * wide] + jnp.sum(weights.astype(F32), axis=0, keepdims=True))
        mix_r = mixed[r * wide : (r + 1) * wide] + mm_tn(weights, nv_ref[r * tree : (r + 1) * tree, :])
        own_mix.append(gather_heads(mix_r))

    orecv[0] = osend[0]
    trecv[0] = tsend[0]

    def await_stats(k, carry):
        t_copy(k, k, me).wait_recv()
        return carry

    lax.fori_loop(1, fs, await_stats, 0)

    pick = rq_scr[:, 0:128]
    weight_any = [jnp.zeros((fs, 128), F32), jnp.zeros((fs, 128), F32)]
    own_weight = []
    for r in range(requests):
        chosen = pick if r == 1 else 1.0 - pick
        shares = []
        for hh in range(2):
            best = jnp.where(chosen > 0.5, trecv[:, hh, :], NEGATIVE)
            amount = trecv[:, 2 + hh, :]
            mine = own_top[r][:, hh * 128 : (hh + 1) * 128]
            highest = jnp.maximum(jnp.max(best, axis=0, keepdims=True), mine)
            weights = jnp.exp(best - highest) * chosen
            own = jnp.exp(mine - highest)
            bottom = jnp.sum(weights * amount, axis=0, keepdims=True) + (
                own * own_total[r][:, hh * 128 : (hh + 1) * 128])
            weight_any[hh] = weight_any[hh] + weights / bottom
            shares.append(own / bottom)
        own_weight.append(shares)
    for hh in range(2):
        sheet = jnp.concatenate(
            [weight_any[hh]]
            + [jnp.broadcast_to(own_weight[r][hh], (8, 128)) for r in range(requests)]
            + [jnp.zeros((128 - fs - 8 * requests, 128), F32)], axis=0)
        wt_scr[hh * 128 : (hh + 1) * 128, :] = sheet.T

    def factor(col):
        out = wt_scr[0:tree, col : col + 1] * head_masks[0]
        for h in range(1, heads):
            out = out + wt_scr[h * tree : (h + 1) * tree, col : col + 1] * head_masks[h]
        return out

    def await_parts(k, carry):
        o_copy(k, k, me).wait_recv()
        return carry

    lax.fori_loop(1, fs, await_parts, 0)
    merged = [own_mix[r] * factor(fs + 8 * r) for r in range(requests)]
    for k in range(fs):
        part = orecv[k].astype(F32) * factor(k)
        pick_row = rq_scr[k : k + 1, :]
        merged[0] = merged[0] + part * (1.0 - pick_row)
        merged[1] = merged[1] + part * pick_row
    attended = jnp.concatenate(merged, axis=0).astype(BF16)
    far_copies[0].wait_recv()
    pass_copies[0].start()

    side, per_side = vs // 2, owners // 2

    def owns(v):
        return lax.rem(v, side) < per_side

    def share(v):
        return v // side * per_side + lax.rem(v, side)

    own = share(ve)
    per_owner = resid_ref.shape[1]
    tile = 256
    for c in range(width // tile):
        block = mm(attended, ow_ref[:, c * tile : (c + 1) * tile])
        for o in range(owners):
            piece = block[o * per_owner : (o + 1) * per_owner]
            pown[o, :, c * tile : (c + 1) * tile] = piece
            psend[o, :, c * tile : (c + 1) * tile] = piece.astype(BF16)

    def p_copy(k, to):
        return pltpu.make_async_remote_copy(
            src_ref=psend.at[share(to)], dst_ref=precv.at[k], send_sem=p_sem.at[0, k], recv_sem=p_sem.at[1, k],
            device_id={"vocab": to}, device_id_type=MESH)

    def n_copy(k, owner, to):
        return pltpu.make_async_remote_copy(
            src_ref=normed_ref.at[owner], dst_ref=normed_ref.at[owner],
            send_sem=n_sem.at[0, k], recv_sem=n_sem.at[1, k],
            device_id={"vocab": to}, device_id_type=MESH)

    def h_copy(k, owner, to):
        return pltpu.make_async_remote_copy(
            src_ref=hsend.at[to], dst_ref=cols_ref.at[owner], send_sem=h_sem.at[0, k], recv_sem=h_sem.at[1, k],
            device_id={"vocab": to}, device_id_type=MESH)

    for k in range(1, vs):
        to = lax.rem(ve + k, vs)

        @pl.when(owns(to))
        def _():
            p_copy(k, to).start()

    hidden_units, pitch = wraw.shape[1], packed.shape[1]

    def settle(i, carry):
        packed[i, pitch - 16 : pitch, :] = jnp.zeros((16, width), BF16)
        packed[i, 0:hidden_units, :] = wraw[i]
        return carry

    for i in range(3):
        own_loads[i].wait()
        near_copies[i].wait_recv()
        lax.fori_loop(4 * i, 4 * i + (3 if i == 0 else 2), settle, 0)

    @pl.when(owns(ve))
    def _():
        hidden = resid_ref[own].astype(F32) + pown[own]
        for k in range(1, vs):
            p_copy(k, ve).wait_recv()
            hidden = hidden + precv[k].astype(F32)
        mean = jnp.mean(hidden * hidden, axis=-1, keepdims=True)
        normed_ref[own] = (hidden * lax.rsqrt(mean + EPSILON) * gain_ref[...].reshape(1, width)).astype(BF16)
        for k in range(1, vs):
            n_copy(k, own, lax.rem(ve + k, vs)).start()
        columns = width // vs
        padded = hsend.shape[2]
        for v in range(vs):
            turned = hidden if v == 0 else pltpu.roll(hidden, width - v * columns, 1)
            hsend[v] = turned[:, 0:padded]
        for k in range(1, vs):
            h_copy(k, own, lax.rem(ve + k, vs)).start()
        cols_ref[own] = hsend[ve]

    pass_copies[0].wait_recv()
    lax.fori_loop(3, 4, settle, 0)
    far_copies[1].wait_recv()
    pass_copies[1].start()
    lax.fori_loop(6, 7, settle, 0)

    for k in range(1, vs):
        owner = lax.rem(ve - k + vs, vs)

        @pl.when(owns(owner))
        def _():
            n_copy(k, share(owner), ve).wait_recv()

    far_copies[2].start()

    def await_columns():
        for k in range(1, vs):
            owner = lax.rem(ve - k + vs, vs)

            @pl.when(owns(owner))
            def _():
                h_copy(k, share(owner), ve).wait_recv()

    def finish():
        def await_sends(k, carry):
            m_copy(k, k, me).wait_send()
            o_copy(k, k, me).wait_send()
            t_copy(k, k, me).wait_send()
            return carry

        lax.fori_loop(1, fs, await_sends, 0)
        y_copy.wait_send()
        for step in range(zs):
            for dy in range(2):
                twin_copy(4 * step + 2 * dy).wait_send()
        for step in range(last + 1):
            for way in range(2):
                for dy in range(2):
                    if step < last or way == dy:
                        ring_copy(way, step, dy).wait_send()
        for k in range(1, vs):
            to = lax.rem(ve + k, vs)

            @pl.when(owns(to))
            def _():
                p_copy(k, to).wait_send()

        @pl.when(owns(ve))
        def _():
            for k in range(1, vs):
                to = lax.rem(ve + k, vs)
                n_copy(k, own, to).wait_send()
                h_copy(k, own, to).wait_send()

        for copy in far_copies + near_copies + pass_copies:
            copy.wait_send()

    return finish, await_columns, far_copies, pass_copies


def expert_part(
    fs, vs, zs, await_columns, far_copies, pass_copies,
    normed_ref, cols_ref, routes_ref, router_ref,
    out_ref,
    wraw, weights, rt_scr, xbuf, obuf, sbuf, rbuf, fsend, frecv,
    ag_sem, rs_sem, f_sem,
):
    owners, per_owner, width = normed_ref.shape
    tokens = owners * per_owner
    normed = normed_ref[...].reshape(tokens, width)
    block = xbuf.shape[1] // 2
    cut = xbuf.shape[2]
    slots = fsend.shape[1]
    kinds, sources = 3, wraw.shape[0] // 3
    hidden = wraw.shape[1]
    pitch = weights.shape[1]
    me = lax.axis_index("fsdp")
    ve = lax.axis_index("vocab")
    core = lax.rem(me, 2)
    z = lax.rem(me // 2, zs)
    yhi = me // (2 * zs)
    right = (yhi * zs + lax.rem(z + 1, zs)) * 2 + core
    left = (yhi * zs + lax.rem(z + zs - 1, zs)) * 2 + core

    rt_scr[...] = jnp.zeros(rt_scr.shape, F32)
    rt_scr[0:2, 0:tokens] = routes_ref[...].astype(F32)
    columns_of = rt_scr[...].T[0:tokens].astype(jnp.int32)
    lane = iota((tokens, 128), 1)
    first, second = columns_of[:, 0:1], columns_of[:, 1:2]
    hits = jnp.where((first == lane) | (second == lane), 1.0, 0.0)
    below = jnp.where(iota((tokens, tokens), 1) < iota((tokens, tokens), 0), 1.0, 0.0).astype(BF16)
    ranks = mm(below, hits.astype(BF16))
    my_hit = jnp.sum(jnp.where(lane == ve, hits, 0.0), axis=1, keepdims=True)
    my_rank = jnp.sum(jnp.where(lane == ve, ranks, 0.0), axis=1, keepdims=True)
    mine = jnp.where((my_hit > 0.5) & (my_rank == lane.astype(F32)), 1.0, 0.0)

    picked = mm_tn(mine.astype(BF16), normed)[0:block]
    xbuf[0] = jnp.concatenate([picked[:, 0:cut], picked[:, cut:width]], axis=0).astype(BF16)

    ways = (right, left)
    steps = zs // 2
    middle = (cut // 128 + 1) // 2 * 128
    spans = (pl.ds(0, middle), pl.ds(middle, cut - middle))

    def halves(step, way):
        return (way,) if step == steps - 1 else (0, 1)

    def gather_copy(way, step, h):
        src = 0 if step == 0 else 2 * step - 1 + way
        dst = zs - 1 if step == steps - 1 else 2 * step + 1 + way
        return pltpu.make_async_remote_copy(
            src_ref=xbuf.at[src, :, spans[h]], dst_ref=xbuf.at[dst, :, spans[h]],
            send_sem=ag_sem.at[0, way, step, h], recv_sem=ag_sem.at[1, way, step, h],
            device_id={"fsdp": ways[way]}, device_id_type=MESH)

    def gather_step(step):
        for h in (0, 1):
            for way in range(2):
                if step > 0:
                    gather_copy(way, step - 1, h).wait_recv()
                if h in halves(step, way):
                    gather_copy(way, step, h).start()

    def expert_up(first_block, count):
        blocks = range(first_block, first_block + count)
        sides = [
            jnp.concatenate([xbuf[b, at : at + block, :].astype(F32) for b in blocks], axis=0)
            for at in (0, block)
        ]
        rows = jnp.concatenate(sides, axis=1).astype(BF16)
        gate = mm_nt(rows, weights[0:sources].reshape(sources * pitch, width))
        lifted = mm_nt(rows, weights[sources : 2 * sources].reshape(sources * pitch, width))
        return (gate / (1.0 + jnp.exp(-gate)) * lifted).astype(BF16)

    def expert_down(acts, first_block, count):
        tile = cut // 3
        for side in range(2):
            for c in range(3):
                down = weights[2 * sources : 3 * sources, :, side * cut + c * tile : side * cut + (c + 1) * tile]
                out = mm(acts, down.reshape(sources * pitch, tile))
                for i in range(count):
                    obuf[first_block + i, side * block : (side + 1) * block, c * tile : (c + 1) * tile] = (
                        out[i * block : (i + 1) * block])

    gather_step(0)
    logits = mm_nt(normed, router_ref[...])
    lane8 = iota(logits.shape, 1)
    chosen0 = jnp.sum(jnp.where(lane8 == first, logits, 0.0), axis=1, keepdims=True)
    chosen1 = jnp.sum(jnp.where(lane8 == second, logits, 0.0), axis=1, keepdims=True)
    gate0 = 1.0 / (1.0 + jnp.exp(chosen1 - chosen0))
    gate1 = 1.0 / (1.0 + jnp.exp(chosen0 - chosen1))
    my_gate = jnp.where(first == ve, gate0, jnp.where(second == ve, gate1, 0.0))
    slot_gate = jnp.sum((mine * my_gate).T, axis=1, keepdims=True)[0:block]
    spread_e = jnp.where(iota((128, vs * slots), 0) == iota((128, vs * slots), 1) // slots, 1.0, 0.0).astype(BF16)
    all_hits = mm(hits.astype(BF16), spread_e)
    all_ranks = mm(ranks.astype(BF16), spread_e)
    slot_at = (iota((tokens, vs * slots), 1) % slots).astype(F32)
    back = jnp.where((all_hits > 0.5) & (all_ranks == slot_at), 1.0, 0.0).astype(BF16)

    def settle(i, carry):
        weights[i, pitch - 16 : pitch, :] = jnp.zeros((16, width), BF16)
        weights[i, 0:hidden, :] = wraw[i]
        return carry

    for step in range(1, steps):
        gather_step(step)
        if step == 1:
            pass_copies[1].wait_recv()
            lax.fori_loop(2 * sources - 1, 2 * sources, settle, 0)
        if step == 2:
            near_acts = expert_up(0, 5)
    third_acts = expert_up(5, 2)
    for way in range(2):
        gather_copy(way, steps - 1, way).wait_recv()
    far_acts = jnp.concatenate([third_acts, expert_up(7, 1)], axis=0)
    far_copies[2].wait_recv()
    pass_copies[2].start()
    lax.fori_loop(2 * sources + 2, 2 * sources + 3, settle, 0)
    pass_copies[2].wait_recv()
    lax.fori_loop(2 * sources + 3, 3 * sources, settle, 0)
    expert_down(far_acts, 5, 3)

    def sum_copy(way, step, h):
        return pltpu.make_async_remote_copy(
            src_ref=sbuf.at[way, step, :, spans[h]], dst_ref=rbuf.at[way, step, :, spans[h]],
            send_sem=rs_sem.at[0, way, step, h], recv_sem=rs_sem.at[1, way, step, h],
            device_id={"fsdp": ways[way]}, device_id_type=MESH)

    for step in range(steps):
        for h in (0, 1):
            at = spans[h]
            for way in range(2):
                if step == 0:
                    if h != way:
                        continue
                    sbuf[way, 0, :, at] = obuf[zs - 1, :, at].astype(BF16)
                else:
                    source = 2 * (steps - step) - way
                    value = obuf[source, :, at]
                    if step > 1 or h == way:
                        sum_copy(way, step - 1, h).wait_recv()
                        value = value + rbuf[way, step - 1, :, at].astype(F32)
                    sbuf[way, step, :, at] = value.astype(BF16)
                sum_copy(way, step, h).start()
        if step == 0:
            expert_down(near_acts, 0, 5)
    for way in range(2):
        for h in (0, 1):
            sum_copy(way, steps - 1, h).wait_recv()
    whole = obuf[0] + rbuf[0, steps - 1].astype(F32) + rbuf[1, steps - 1].astype(F32)
    gated = [whole[side * block : (side + 1) * block] * slot_gate for side in range(2)]

    columns = width // vs
    padded = fsend.shape[2]
    empty = jnp.zeros((slots - block, padded), F32)

    def f_copy(k, to, slot):
        return pltpu.make_async_remote_copy(
            src_ref=fsend.at[to], dst_ref=frecv.at[slot], send_sem=f_sem.at[0, k], recv_sem=f_sem.at[1, k],
            device_id={"vocab": to}, device_id_type=MESH)

    for v in range(vs):
        side, at = divmod(v * columns, cut)
        turned = gated[side] if at == 0 else pltpu.roll(gated[side], cut - at, 1)
        fsend[v] = jnp.concatenate([turned[:, 0:padded], empty], axis=0).astype(BF16)
    for k in range(1, vs):
        f_copy(k, lax.rem(ve + k, vs), ve).start()
    frecv[ve] = fsend[ve]
    for k in range(1, vs):
        f_copy(k, ve, lax.rem(ve - k + vs, vs)).wait_recv()
    mixture = mm(back, frecv[...].reshape(vs * slots, padded))
    await_columns()
    out_ref[...] = (cols_ref[...].reshape(tokens, padded) + mixture)[:, 0:columns].astype(BF16)

    for step in range(steps):
        for way in range(2):
            for h in halves(step, way):
                gather_copy(way, step, h).wait_send()
    for step in range(steps):
        for way in range(2):
            for h in (0, 1):
                if step > 0 or h == way:
                    sum_copy(way, step, h).wait_send()
    for k in range(1, vs):
        f_copy(k, lax.rem(ve + k, vs), ve).wait_send()


def layer_kernel(fs, vs, zs, *refs):
    inputs, rest = refs[:12], refs[12:]
    routes_ref, router_ref = rest[:2]
    weight_refs, out_ref, rest = rest[2:5], rest[5], rest[6:]
    normed_ref, cols_ref = rest[:2]
    attention_scratch, expert_scratch, rest = rest[2:19], rest[19:28], rest[28:]
    attention_sems, expert_sems = rest[:12], rest[12:]
    finish, *copies = attention_part(
        fs, vs, zs, *inputs, *weight_refs, *expert_scratch[:2], normed_ref, cols_ref,
        *attention_scratch, *attention_sems)
    expert_part(
        fs, vs, zs, *copies, normed_ref, cols_ref, routes_ref, router_ref, out_ref,
        *expert_scratch, *expert_sems)
    finish()


def per_device(
    resid, queries, new_keys, new_values, pool_keys, pool_values, page_table, serve_pages, cache_lengths, parents,
    out_weight, norm_gain, router, routes, gate_weight, up_weight, down_weight,
):
    fs, vs = lax.axis_size("fsdp"), lax.axis_size("vocab")
    zs = fs // 4
    tokens, width = resid.shape
    features = queries.shape[1]
    tree = parents.shape[1]
    pool_pages, page_rows, _ = pool_keys.shape
    hidden = gate_weight.shape[2]
    pitch = -(-hidden // 64) * 64
    vmem = pl.BlockSpec(memory_space=pltpu.VMEM)
    smem = pl.BlockSpec(memory_space=pltpu.SMEM)
    hbm = pl.BlockSpec(memory_space=pl.ANY)
    dma = pltpu.SemaphoreType.DMA
    padded = -(-(width // vs) // 128) * 128
    per_owner = 16
    owners = tokens // per_owner
    wg, wu, wd = gate_weight[0].T, up_weight[0].T, down_weight[0]
    block, slots = 40, 48
    return pl.pallas_call(
        functools.partial(layer_kernel, fs, vs, zs),
        out_shape=jax.ShapeDtypeStruct((tokens, width // vs), BF16),
        in_specs=[vmem] * 4 + [smem] * 2 + [vmem] * 4 + [hbm] * 2 + [vmem] * 2 + [hbm] * 3,
        out_specs=vmem,
        scratch_shapes=[
            pltpu.VMEM((owners, per_owner, width), BF16),
            pltpu.VMEM((owners, per_owner, padded), F32),
            pltpu.VMEM(pool_keys.shape, BF16),
            pltpu.VMEM(pool_values.shape, BF16),
            pltpu.VMEM((pool_pages // 2, page_rows, 512), F32),
            pltpu.VMEM((pool_pages // 2, 512), jnp.int32),
            pltpu.VMEM((fs, features), F32),
            pltpu.VMEM((256, 128), F32),
            pltpu.VMEM((fs, 2 * tree, features), BF16),
            pltpu.VMEM((fs, 2, 128), F32),
            pltpu.VMEM((fs, 2, 128), F32),
            pltpu.VMEM((fs, tree, features), BF16),
            pltpu.VMEM((fs, tree, features), BF16),
            pltpu.VMEM((fs, 4, 128), F32),
            pltpu.VMEM((fs, 4, 128), F32),
            pltpu.VMEM((owners, per_owner, width), F32),
            pltpu.VMEM((owners, per_owner, width), BF16),
            pltpu.VMEM((vs, per_owner, width), BF16),
            pltpu.VMEM((vs, per_owner, padded), F32),
            pltpu.VMEM((12, hidden, width), BF16),
            pltpu.VMEM((12, pitch, width), BF16),
            pltpu.VMEM((128, 128), F32),
            pltpu.VMEM((zs, 2 * block, width // 2), BF16),
            pltpu.VMEM((zs, 2 * block, width // 2), F32),
            pltpu.VMEM((2, zs // 2, 2 * block, width // 2), BF16),
            pltpu.VMEM((2, zs // 2, 2 * block, width // 2), BF16),
            pltpu.VMEM((vs, slots, padded), BF16),
            pltpu.VMEM((vs, slots, padded), BF16),
            dma((4,)), dma((2, 12)), dma((fs,)), dma((1,)), dma((2, zs // 2, 2)), dma((fs // 2,)),
            dma((2, fs)), dma((2, fs)), dma((2, fs)), dma((2, vs)), dma((2, vs)), dma((2, vs)),
            dma((2, 2, zs // 2, 2)), dma((2, 2, zs // 2, 2)), dma((2, vs)),
        ],
        compiler_params=pltpu.CompilerParams(
            collective_id=1, has_side_effects=True, vmem_limit_bytes=60 * 2**20),
        name="layer",
    )(
        queries, new_keys, new_values, page_table, cache_lengths, serve_pages.reshape(-1), parents,
        resid.reshape(owners, per_owner, width), out_weight, norm_gain, pool_keys, pool_values,
        routes.T, router.T, wg, wu, wd)


def solution(mesh):
    in_specs = (
        P("fsdp", None), P("fsdp", "vocab"), P("fsdp", "vocab"), P("fsdp", "vocab"),
        P("fsdp", None, "vocab"), P("fsdp", None, "vocab"), P("fsdp", None), P("fsdp", None, None),
        P("fsdp"), P("fsdp", None), P("vocab", None), P(), P(), P("fsdp", None),
        P("vocab", None, "fsdp"), P("vocab", None, "fsdp"), P("vocab", "fsdp", None),
    )
    return jax.shard_map(
        per_device, mesh=mesh, in_specs=in_specs, out_specs=P("fsdp", "vocab"), check_vma=False
    )
```
